32 devices in a mesh: tower: 2 (over y), dp: 16 (over z, x, core).
Axes of the slice: x: 2, y: 2, z: 4, core: 2. Of those that a mesh axis runs over, the one named last changes fastest.
Arguments:
- hidden_in: bfloat16 [2, 8192, 768], P('tower', 'dp'), may hold values from -6 to 6
- seg_ids: int32 [16, 512], P('dp'), may hold values from 0 to 3, never falling along the last dimension, each value on 1 to 320 neighbouring positions
- labels: int32 [256], P('dp'), may hold values from 0 to 63
- out_grad: bfloat16 [2, 8192, 768], P('tower', 'dp'), may hold values from -2 to 2
- w_qkv: bfloat16 [2, 768, 2304], P('tower'), may hold values from -0.3125 to 0.3125
- b_query: float32 [2, 768], P('tower'), may hold values from -3 to 3
- b_value: float32 [2, 768], P('tower'), may hold values from -3 to 3
- w_out: bfloat16 [2, 768, 768], P('tower'), may hold values from -0.625 to 0.625
- b_out: float32 [2, 768], P('tower'), may hold values from -3 to 3
- ln1_gain: float32 [2, 768], P('tower'), may hold values from 0.5 to 1.5
- ln1_bias: float32 [2, 768], P('tower'), may hold values from -2 to 2
- w_in: bfloat16 [2, 768, 3072], P('tower'), may hold values from -0.21875 to 0.21875
- b_in: float32 [2, 3072], P('tower'), may hold values from -3 to 3
- w_back: bfloat16 [2, 3072, 768], P('tower'), may hold values from -0.109375 to 0.109375
- b_back: float32 [2, 768], P('tower'), may hold values from -3 to 3
- ln2_gain: float32 [2, 768], P('tower'), may hold values from 0.5 to 1.5
- ln2_bias: float32 [2, 768], P('tower'), may hold values from -2 to 2
Outputs:
- out_hidden: bfloat16 [2, 8192, 768], P('tower', 'dp')
- grad_hidden: bfloat16 [2, 8192, 768], P('tower', 'dp')
- grad_w_qkv: float32 [2, 768, 2304], P('tower', 'dp')
- grad_b_query: float32 [2, 768], P('tower', 'dp')
- grad_b_value: float32 [2, 768], P('tower', 'dp')
- grad_w_out: float32 [2, 768, 768], P('tower', 'dp')
- grad_b_out: float32 [2, 768], P('tower', 'dp')
- grad_ln1_gain: float32 [2, 768], P('tower', 'dp')
- grad_ln1_bias: float32 [2, 768], P('tower', 'dp')
- grad_w_in: float32 [2, 768, 3072], P('tower', 'dp')
- grad_b_in: float32 [2, 3072], P('tower', 'dp')
- grad_w_back: float32 [2, 3072, 768], P('tower', 'dp')
- grad_b_back: float32 [2, 768], P('tower', 'dp')
- grad_ln2_gain: float32 [2, 768], P('tower', 'dp')
- grad_ln2_bias: float32 [2, 768], P('tower', 'dp')
The draws below stay inside these ranges and needn't reach their ends.
Inputs may be any that keep to these rules, and one draw needn't show every extreme that they name: `seg_ids`: each row holds 4 passages in order, each 1 to 320 tokens long, and one passage of each row has exactly 320.
All inputs are finite; a program needn't handle non-finite values.
Results may differ from the reference program's by a relative error of at most 0.014.
The reference program's roundings to bfloat16 on the way count: a program that leaves them out, or rounds other values in their place, can miss the bound.
Values may be sent and summed in bfloat16 or wider, within the bound.
No kernel may reach another device: no remote copies, remote signals or barrier semaphores. Data moves between devices by JAX's collectives and lax.ppermute only.
A program may use at most 192 MiB of HBM per device.

```python
import math
import jax
import jax.numpy as jnp
import numpy as np
from jax import lax

D = 768
HEAD_DIM = 64
FF = 3072
ROW_LEN = 512
QLEN = 32
SEGS = 4
SEG_MOST = 320
ROWS = 16
TOKENS = 8192
QUERIES = 256
PASSAGES = 64


def with_ends(drawn, rng, low, largest):
    index_at = [jax.random.randint(jax.random.fold_in(rng, axis), (), 0, length) for axis, length in enumerate(drawn.shape)]
    widest = drawn.shape.index(max(drawn.shape))
    beside = index_at[:widest] + [(index_at[widest] + 1) % drawn.shape[widest]] + index_at[widest + 1:]
    return drawn.at[tuple(index_at)].set(low).at[tuple(beside)].set(largest)


def shard_levels(key, shape, pieces, low, top_value):
    loudness = 1.0
    for axis_at, parts in pieces:
        draws = jax.random.uniform(jax.random.fold_in(jax.random.fold_in(key, 6), axis_at), (parts,), jnp.float32, low / len(pieces), top_value / len(pieces))
        loudness = loudness * jnp.repeat(jnp.exp(draws), shape[axis_at] // parts).reshape((-1,) + (1,) * (len(shape) - 1 - axis_at))
    return loudness


def length_profile(amount, total, bound, skew):
    portions = [(1 << 20) // math.isqrt(grade ** skew) + 1 for grade in range(2, amount + 1)]
    surplus, holding = total - bound - (amount - 1), [1] * (amount - 1)
    while surplus > 0:
        candidates = [i for i in range(amount - 1) if holding[i] < bound]
        mass, remaining = sum([portions[i] for i in candidates]), surplus
        for i in candidates:
            more = min(bound - holding[i], max(1, remaining * portions[i] // mass), surplus)
            holding[i] = holding[i] + more
            surplus = surplus - more
    return np.array([bound] + holding)


def uneven(own_key, count, total, most, lean):
    if count == 2:
        one = jax.random.randint(own_key, (), max(1, total - most), min(most, total - 1) + 1)
        return jnp.stack([one, total - one])
    tallies = jnp.asarray(length_profile(count, total, most, lean), jnp.int32)
    twos = (count - 1) // 2
    donor, receiver = tallies[1:1 + 2 * twos:2], tallies[2:2 + 2 * twos:2]
    slack = jnp.minimum(donor - 1, most - receiver)
    passed = jax.random.randint(jax.random.fold_in(own_key, 1), (twos,), 0, 1 << 20) % (slack + 1)
    tallies = tallies.at[1:1 + 2 * twos:2].set(donor - passed).at[2:2 + 2 * twos:2].set(receiver + passed)
    return tallies[jax.random.permutation(jax.random.fold_in(own_key, 2), count)]


def scatter_about(rng, shape, width, most, cuts=(), kind=jnp.bfloat16):
    entries = jax.random.normal(rng, shape, jnp.float32) * width
    if len(cuts) > 0:
        entries = shard_levels(rng, shape, cuts, -0.22, 0.18) * entries
    return jnp.clip(entries, min=-most, max=most).astype(kind)


def setup_inputs(seed: int = 0) -> dict:
    arg_keys = jax.random.split(jax.random.key(seed), 18)
    return {
        "hidden_in": scatter_about(arg_keys[0], (2, TOKENS, D), 1.0, 6.0, ((0, 2), (1, 16))),
        "seg_ids": jax.vmap(lambda own: jnp.searchsorted(jnp.cumsum(uneven(own, SEGS, ROW_LEN, SEG_MOST, 2)), jnp.arange(ROW_LEN), side="right"))(jax.random.split(arg_keys[1], ROWS)).reshape((ROWS, ROW_LEN)).astype(jnp.int32),
        "labels": with_ends(jax.random.randint(arg_keys[2], (QUERIES,), 0, PASSAGES), jax.random.fold_in(arg_keys[2], 1), 0, PASSAGES - 1).astype(jnp.int32),
        "out_grad": scatter_about(arg_keys[3], (2, TOKENS, D), 0.3, 2.0, ((0, 2), (1, 16))),
        "w_qkv": scatter_about(arg_keys[4], (2, D, 3 * D), (D // 2) ** -0.5, 0.3125, ((0, 2),)),
        "b_query": scatter_about(arg_keys[5], (2, D), 0.5, 3.0, ((0, 2),), jnp.float32),
        "b_value": scatter_about(arg_keys[6], (2, D), 0.5, 3.0, ((0, 2),), jnp.float32),
        "w_out": scatter_about(arg_keys[7], (2, D, D), (D // 8) ** -0.5, 0.625, ((0, 2),)),
        "b_out": scatter_about(arg_keys[8], (2, D), 0.5, 3.0, ((0, 2),), jnp.float32),
        "ln1_gain": jnp.clip(1.0 + 0.1 * jax.random.normal(arg_keys[9], (2, D), jnp.float32), 0.5, 1.5),
        "ln1_bias": scatter_about(arg_keys[10], (2, D), 0.3, 2.0, ((0, 2),), jnp.float32),
        "w_in": scatter_about(arg_keys[11], (2, D, FF), D ** -0.5, 0.21875, ((0, 2),)),
        "b_in": scatter_about(arg_keys[12], (2, FF), 0.5, 3.0, ((0, 2),), jnp.float32),
        "w_back": scatter_about(arg_keys[13], (2, FF, D), FF ** -0.5, 0.109375, ((0, 2),)),
        "b_back": scatter_about(arg_keys[14], (2, D), 0.5, 3.0, ((0, 2),), jnp.float32),
        "ln2_gain": jnp.clip(1.0 + 0.1 * jax.random.normal(arg_keys[15], (2, D), jnp.float32), 0.5, 1.5),
        "ln2_bias": scatter_about(arg_keys[16], (2, D), 0.3, 2.0, ((0, 2),), jnp.float32),
    }


@jax.custom_vjp
def low(v):
    return lax.optimization_barrier(v.astype(jnp.bfloat16)).astype(jnp.float32)

@jax.custom_vjp
def low_back(v):
    return v

def low_keep(v):
    return (low(v), None)

def low_pass(kept, grad):
    return (grad,)

def back_keep(v):
    return (v, None)

def back_low(kept, grad):
    return (low(grad),)
low.defvjp(low_keep, low_pass)
low_back.defvjp(back_keep, back_low)
eps_norm = 1e-05
highest = lax.Precision.HIGHEST

def layer_norm(hidden, norm_gain, norm_bias):
    average = lax.optimization_barrier(jnp.mean(hidden, -1, keepdims=True))
    centred = hidden - average
    variance = lax.optimization_barrier(jnp.mean(centred * centred, -1, keepdims=True))
    return centred * lax.rsqrt(variance + eps_norm) * norm_gain + norm_bias

def project(left, right):
    return jnp.einsum('gld,de->gle', left, right, precision=highest)

def encode(inputs, segment, params):
    w_qkv, b_query, b_value, w_out, b_out, ln1_gain, ln1_bias, w_in, b_in, w_back, b_back, ln2_gain, ln2_bias = params
    group, length, model_width = inputs.shape
    heads = model_width // HEAD_DIM
    bias_all = jnp.concatenate([b_query, jnp.zeros_like(b_query), b_value])
    proj = low_back(low(project(inputs, w_qkv) + bias_all))
    shaped = proj.reshape(group, length, 3, heads, HEAD_DIM)
    queries = shaped[:, :, 0]
    keys = shaped[:, :, 1]
    values = shaped[:, :, 2]
    scores = jnp.einsum('gqhe,gkhe->ghqk', queries, keys, precision=highest) * (1.0 / math.sqrt(HEAD_DIM))
    scores = low_back(scores)
    allowed = segment[:, None, :, None] == segment[:, None, None, :]
    scores = jnp.where(allowed, scores, -1000000000.0)
    row_top = lax.optimization_barrier(jnp.max(scores, -1, keepdims=True))
    shifted = jnp.exp(scores - row_top)
    probs = shifted / lax.optimization_barrier(jnp.sum(shifted, -1, keepdims=True))
    attended = jnp.einsum('ghqk,gkhe->gqhe', low(probs), values, precision=highest).reshape(group, length, model_width)
    attended = low_back(low(attended))
    branch = low_back(project(attended, w_out) + b_out)
    normed_first = layer_norm(inputs + branch, ln1_gain, ln1_bias)
    inner = low_back(project(low(normed_first), w_in) + b_in)
    act = low(jax.nn.gelu(inner, approximate=False))
    second = normed_first + low_back(project(act, w_back) + b_back)
    return layer_norm(second, ln2_gain, ln2_bias)

def reference(hidden_in, seg_ids, labels, out_grad, w_qkv, b_query, b_value, w_out, b_out, ln1_gain, ln1_bias, w_in, b_in, w_back, b_back, ln2_gain, ln2_bias):
    params = tuple((member.astype(jnp.float32) for member in (w_qkv, b_query, b_value, w_out, b_out, ln1_gain, ln1_bias, w_in, b_in, w_back, b_back, ln2_gain, ln2_bias)))
    inputs = hidden_in.astype(jnp.float32)
    cotangent = out_grad.astype(jnp.float32)
    position = jnp.arange(ROW_LEN, dtype=jnp.int32)
    query_segment = jnp.broadcast_to(position // QLEN, (ROWS, ROW_LEN)).astype(jnp.int32)
    starts = lax.optimization_barrier(jnp.sum((seg_ids[:, None, :] < jnp.arange(SEGS, dtype=jnp.int32)[None, :, None]).astype(jnp.int32), -1))
    chosen = (position[None, None, :] == starts[:, :, None]).astype(jnp.float32)
    target = (labels[:, None] == jnp.arange(PASSAGES, dtype=jnp.int32)[None, :]).astype(jnp.float32)
    group = math.gcd(ROWS, max(1, 4096 // ROW_LEN))

    def tower_out(tokens, segment, tower_params):
        blocks = tokens.reshape(ROWS // group, group, ROW_LEN, D)
        seg_blocks = segment.reshape(ROWS // group, group, ROW_LEN)
        block_fn = jax.checkpoint(lambda row_pair: encode(row_pair[0], row_pair[1], tower_params))
        return lax.map(block_fn, (blocks, seg_blocks)).reshape(TOKENS, D)

    def objective(tokens, weights):
        query_final = tower_out(tokens[0], query_segment, tuple((member[0] for member in weights)))
        passage_final = tower_out(tokens[1], seg_ids, tuple((member[1] for member in weights)))
        query_cls = low(query_final.reshape(QUERIES, QLEN, D)[:, 0])
        passage_cls = low(jnp.einsum('rsl,rld->rsd', chosen, passage_final.reshape(ROWS, ROW_LEN, D), precision=highest).reshape(PASSAGES, D))
        logits = jnp.einsum('qd,pd->qp', query_cls, passage_cls, precision=highest) * (2.0 / math.sqrt(D))
        row_top = lax.optimization_barrier(jnp.max(logits, -1, keepdims=True))
        log_sum = row_top[:, 0] + jnp.log(lax.optimization_barrier(jnp.sum(jnp.exp(logits - row_top), -1)))
        picked = lax.optimization_barrier(jnp.sum(logits * target, -1))
        objective_value = jnp.sum(log_sum - picked) + jnp.sum(cotangent[0] * query_final) + jnp.sum(cotangent[1] * passage_final)
        return (objective_value, (query_final, passage_final))
    objective_value, back_fn, finals = jax.vjp(objective, inputs, params, has_aux=True)
    grad_tokens, grad_params = back_fn(jnp.ones_like(objective_value))
    out_hidden = jnp.stack([finals[0], finals[1]]).astype(jnp.bfloat16)
    grad_hidden = grad_tokens.astype(jnp.bfloat16)
    return (out_hidden, grad_hidden, grad_params[0], grad_params[1], grad_params[2], grad_params[3], grad_params[4], grad_params[5], grad_params[6], grad_params[7], grad_params[8], grad_params[9], grad_params[10], grad_params[11], grad_params[12])
```

```python
import functools
import math

import jax
import jax.numpy as jnp
from jax import lax
from jax.experimental import pallas as pl
from jax.experimental.pallas import tpu as pltpu
from jax.sharding import PartitionSpec as P

HEAD_DIM = 64
QLEN = 32
SEGS = 4
PACKET = 24
EPS = 1e-05
BF = jnp.bfloat16
F32 = jnp.float32
TILE = 32

VM = pl.BlockSpec(memory_space=pltpu.VMEM)
SM = pl.BlockSpec(memory_space=pltpu.SMEM)


def nn(a, b):
    return lax.dot_general(a, b, (((1,), (0,)), ((), ())), preferred_element_type=F32)


def nt(a, b):
    return lax.dot_general(a, b, (((1,), (1,)), ((), ())), preferred_element_type=F32)


def tn(a, b):
    return lax.dot_general(a, b, (((0,), (0,)), ((), ())), preferred_element_type=F32)


def kernel_call(body, outs, args, scratch=(), smem=0, mib=32, flops=0, name=None):
    single = not isinstance(outs, (list, tuple))
    shapes = [outs] if single else list(outs)
    moved = sum(math.prod(a.shape) * a.dtype.itemsize for a in list(args) + shapes)
    result = pl.pallas_call(
        body,
        out_shape=shapes,
        in_specs=[SM] * smem + [VM] * (len(args) - smem),
        out_specs=[VM] * len(shapes),
        scratch_shapes=list(scratch),
        compiler_params=pltpu.CompilerParams(vmem_limit_bytes=mib << 20),
        cost_estimate=pl.CostEstimate(flops=flops, bytes_accessed=moved, transcendentals=0),
        name=name,
    )(*args)
    return result[0] if single else result


def sds(shape, dtype):
    return jax.ShapeDtypeStruct(shape, dtype)


def fold(value):
    rows, cols = value.shape
    return jnp.sum(value.reshape(rows // 8, 8, cols), 0)


def head_mask(half):
    lane = lax.broadcasted_iota(jnp.int32, (1, 2 * HEAD_DIM), 1)
    return (lane // HEAD_DIM == half).astype(F32).astype(BF)


def normalise(value):
    centred = value - jnp.mean(value, -1, keepdims=True)
    inverse = lax.rsqrt(jnp.mean(centred * centred, -1, keepdims=True) + EPS)
    return centred * inverse, inverse


def norm_back(grad, normed, inverse, gain):
    scaled = grad * gain
    return inverse * (
        scaled
        - jnp.mean(scaled, -1, keepdims=True)
        - normed * jnp.mean(scaled * normed, -1, keepdims=True)
    )


def gelu_pair(value):
    cdf = 0.5 * lax.erf(value * (1.0 / math.sqrt(2.0))) + 0.5
    density = jnp.exp(value * value * -0.5) * (1.0 / math.sqrt(2.0 * math.pi))
    return value * cdf, cdf + value * density


def proj_kernel(x, w, bq, bv, out):
    width = x.shape[1]
    for part in range(3):
        cols = slice(part * width, (part + 1) * width)
        value = nn(x[...], w[:, cols])
        if part == 0:
            value = value + bq[...]
        if part == 2:
            value = value + bv[...]
        out[:, cols] = value.astype(BF)


def chosen_rows(tower, seg, count, length):
    row = lax.broadcasted_iota(jnp.int32, (count, 1), 0)
    place = lax.broadcasted_iota(jnp.int32, (count, length), 1)
    start = jnp.sum((seg < row).astype(F32), 1, keepdims=True).astype(jnp.int32)
    wanted = jnp.where(tower == 0, row * QLEN, jnp.where(row < SEGS, start, -1))
    return (place == wanted).astype(F32)


def cls_kernel(place, seg, x, proj, w_out, b_out, g1, b1, w_in, b_in, w_back, b_back, g2, b2, cls):
    length, width = x.shape
    count = cls.shape[0]
    heads = width // HEAD_DIM
    tower = place[0]
    pick = chosen_rows(tower, seg[...], count, length)
    pick_low = pick.astype(BF)
    x_cls = nn(pick_low, x[...])
    q_cls = (nn(pick_low, proj[:, :width]) * (1.0 / math.sqrt(HEAD_DIM))).astype(BF)
    place_row = lax.broadcasted_iota(jnp.int32, (1, length), 1)
    own_seg = jnp.where(tower == 0, place_row // QLEN, seg[...])
    row = lax.broadcasted_iota(jnp.int32, (count, 1), 0)
    bias = jnp.where(own_seg == row, 0.0, -1e9)
    lane_head = lax.broadcasted_iota(jnp.int32, (1, width), 1) // HEAD_DIM
    spread = jnp.concatenate(
        [q_cls * (lane_head == h).astype(F32).astype(BF) for h in range(heads)], 0
    )
    scores = nt(spread, proj[:, width : 2 * width]) + jnp.concatenate([bias] * heads, 0)
    shifted = jnp.exp(scores - jnp.max(scores, -1, keepdims=True))
    probs = (shifted / jnp.sum(shifted, -1, keepdims=True)).astype(BF)
    mixed = nn(probs, proj[:, 2 * width :])
    attended = jnp.zeros((count, width), F32)
    for h in range(heads):
        attended = attended + jnp.where(lane_head == h, mixed[h * count : (h + 1) * count], 0.0)
    first = x_cls + (nn(attended.astype(BF), w_out[...]) + b_out[...])
    normed = normalise(first)[0] * g1[...] + b1[...]
    inner = nn(normed.astype(BF), w_in[...]) + b_in[...]
    act = gelu_pair(inner)[0].astype(BF)
    second = normed + (nn(act, w_back[...]) + b_back[...])
    final = normalise(second)[0] * g2[...] + b2[...]
    cls[...] = final.astype(BF)


def attention_kernel(place, seg_row, seg_col, proj, attended, probs, bias_scratch):
    length = proj.shape[0]
    width = proj.shape[1] // 3
    tower = place[0]
    lane = lax.broadcasted_iota(jnp.int32, (1, length), 1)
    sub = lax.broadcasted_iota(jnp.int32, (length, 1), 0)
    row_seg = jnp.where(tower == 0, lane // QLEN, seg_row[...])
    col_seg = jnp.where(tower == 0, sub // QLEN, seg_col[...])
    bias_scratch[...] = jnp.where(col_seg == row_seg, 0.0, -1e9)
    masks = [head_mask(0), head_mask(1)]
    scale = 1.0 / math.sqrt(HEAD_DIM)
    pair_width = 2 * HEAD_DIM

    def pair_step(pair, carry):
        at = pl.multiple_of(pair * pair_width, pair_width)
        queries = proj[:, pl.ds(at, pair_width)] * jnp.asarray(scale, BF)
        keys = proj[:, pl.ds(pl.multiple_of(width + at, pair_width), pair_width)]
        values = proj[:, pl.ds(pl.multiple_of(2 * width + at, pair_width), pair_width)]
        mixed = None
        for half in range(2):
            scores = nt(queries * masks[half], keys) + bias_scratch[...]
            shifted = jnp.exp(scores - jnp.max(scores, -1, keepdims=True))
            total = jnp.sum(shifted, -1, keepdims=True)
            low = (shifted * (1.0 / total)).astype(BF)
            probs[2 * pair + half] = low
            term = nn(low, values * masks[half])
            mixed = term if mixed is None else mixed + term
        attended[:, pl.ds(at, pair_width)] = mixed.astype(BF)
        return carry

    lax.fori_loop(0, width // pair_width, pair_step, 0)


def first_kernel(x, attended, w_out, b_out, g1, b1, n1, r1, low, work):
    work[...] = nn(attended[...], w_out[...])

    def step(i, carry):
        rows = pl.ds(pl.multiple_of(i * TILE, TILE), TILE)
        first = x[rows, :].astype(F32) + (work[rows, :] + b_out[...])
        normed, inverse = normalise(first)
        n1[rows, :] = normed
        r1[rows, :] = inverse
        low[rows, :] = (normed * g1[...] + b1[...]).astype(BF)
        return carry

    lax.fori_loop(0, x.shape[0] // TILE, step, 0)


def inner_kernel(low, w_in, b_in, act, slope, work):
    length = low.shape[0]
    block = work.shape[2]
    blocks = w_in.shape[1] // block
    work[0] = nn(low[...], w_in[:, :block])

    def gelu_block(i, slot):
        cols = pl.ds(pl.multiple_of(i * block, block), block)
        bias = b_in[:, cols]
        for r in range(0, length, TILE):
            value, grad = gelu_pair(work[slot, r : r + TILE, :] + bias)
            act[r : r + TILE, cols] = value.astype(BF)
            slope[r : r + TILE, cols] = grad.astype(BF)

    def step(i, carry):
        slot = lax.rem(i, 2)
        later = pl.ds(pl.multiple_of((i + 1) * block, block), block)
        work[1 - slot] = nn(low[...], w_in[:, later])
        gelu_block(i, slot)
        return carry

    lax.fori_loop(0, blocks - 1, step, 0)
    gelu_block(blocks - 1, (blocks - 1) % 2)


def second_kernel(act, w_back, b_back, n1, g1, b1, g2, b2, n2, r2, out, work):
    work[...] = nn(act[...], w_back[...])

    def step(i, carry):
        rows = pl.ds(pl.multiple_of(i * TILE, TILE), TILE)
        second = (n1[rows, :] * g1[...] + b1[...]) + (work[rows, :] + b_back[...])
        normed, inverse = normalise(second)
        n2[rows, :] = normed
        r2[rows, :] = inverse
        out[rows, :] = (normed * g2[...] + b2[...]).astype(BF)
        return carry

    lax.fori_loop(0, act.shape[0] // TILE, step, 0)


def loss_kernel(place, queries, passages, labels_row, labels_col, grad):
    tower, index = place[0], place[1]
    total_q, width = queries.shape
    total_p = passages.shape[0]
    count = grad.shape[0]
    scale = 2.0 / math.sqrt(width)
    own = (
        lax.broadcasted_iota(jnp.int32, (count, total_q), 1)
        == lax.broadcasted_iota(jnp.int32, (count, total_q), 0) + index * count
    )
    own_q = nn(own.astype(F32).astype(BF), queries[...]).astype(BF)
    logits = nt(own_q, passages[...]) * scale
    peak = jnp.max(logits, -1, keepdims=True)
    soft = jnp.exp(logits - peak)
    soft = soft / jnp.sum(soft, -1, keepdims=True)
    own_label = jnp.sum(
        jnp.where(own, labels_row[...].astype(F32), 0.0), 1, keepdims=True
    ).astype(jnp.int32)
    hit = lax.broadcasted_iota(jnp.int32, (count, total_p), 1) == own_label
    grad_logits = soft - hit.astype(F32)
    wide_p = passages[...].astype(F32)
    grad_q = (
        jnp.dot(grad_logits, wide_p, precision=lax.Precision.HIGHEST, preferred_element_type=F32)
        * scale
    )
    every = nt(queries[...], passages[...]) * scale
    peak = jnp.max(every, -1, keepdims=True)
    soft = jnp.exp(every - peak)
    soft = soft / jnp.sum(soft, -1, keepdims=True)
    hit = lax.broadcasted_iota(jnp.int32, (total_q, total_p), 1) == labels_col[...]
    every_grad = soft - hit.astype(F32)
    mine = jnp.logical_and(
        lax.broadcasted_iota(jnp.int32, (count, total_p), 1)
        == lax.broadcasted_iota(jnp.int32, (count, total_p), 0) + index * SEGS,
        lax.broadcasted_iota(jnp.int32, (count, total_p), 0) < SEGS,
    ).astype(F32)
    picked = lax.dot_general(
        mine, every_grad, (((1,), (1,)), ((), ())),
        precision=lax.Precision.HIGHEST, preferred_element_type=F32,
    )
    grad_p = (
        jnp.dot(
            picked, queries[...].astype(F32),
            precision=lax.Precision.HIGHEST, preferred_element_type=F32,
        )
        * scale
    )
    grad[...] = jnp.where(tower == 0, grad_q, grad_p)


def second_back_kernel(place, seg, out_grad, cls_grad, n2, r2, g2, grad, low, sums, work):
    length, width = out_grad.shape
    count = cls_grad.shape[0]
    pick = chosen_rows(place[0], seg[...], count, length)
    work[...] = lax.dot_general(
        pick, cls_grad[...], (((0,), (0,)), ((), ())),
        precision=lax.Precision.HIGHEST, preferred_element_type=F32,
    )

    def step(i, carry):
        gain_sum, bias_sum, low_sum = carry
        rows = pl.ds(pl.multiple_of(i * TILE, TILE), TILE)
        final = out_grad[rows, :].astype(F32) + work[rows, :]
        normed = n2[rows, :]
        back = norm_back(final, normed, r2[rows, :], g2[...])
        grad[rows, :] = back
        back_low = back.astype(BF)
        low[rows, :] = back_low
        return (
            gain_sum + fold(final * normed),
            bias_sum + fold(final),
            low_sum + fold(back_low.astype(F32)),
        )

    zero = jnp.zeros((8, width), F32)
    parts = lax.fori_loop(0, length // TILE, step, (zero, zero, zero))
    for k, part in enumerate(parts):
        sums[k : k + 1, :] = jnp.sum(part, 0, keepdims=True)


def inner_back_kernel(low, w_back, slope, out, sums):
    block = 256
    for i in range(w_back.shape[0] // block):
        cols = slice(i * block, (i + 1) * block)
        value = (nt(low[...], w_back[cols, :]) * slope[:, cols].astype(F32)).astype(BF)
        out[:, cols] = value
        sums[:, cols] = jnp.sum(value.astype(F32), 0, keepdims=True)


def first_back_kernel(inner, w_in, grad_second, n1, r1, g1, w_out, grad, low, att, sums, work):
    length, width = grad_second.shape
    block = 256
    for i in range(width // block):
        cols = slice(i * block, (i + 1) * block)
        work[:, cols] = nt(inner[...], w_in[cols, :])

    def step(i, carry):
        gain_sum, bias_sum, low_sum = carry
        rows = pl.ds(pl.multiple_of(i * TILE, TILE), TILE)
        value = grad_second[rows, :] + work[rows, :]
        normed = n1[rows, :]
        back = norm_back(value, normed, r1[rows, :], g1[...])
        grad[rows, :] = back
        back_low = back.astype(BF)
        low[rows, :] = back_low
        return (
            gain_sum + fold(value * normed),
            bias_sum + fold(value),
            low_sum + fold(back_low.astype(F32)),
        )

    zero = jnp.zeros((8, width), F32)
    parts = lax.fori_loop(0, length // TILE, step, (zero, zero, zero))
    for k, part in enumerate(parts):
        sums[k : k + 1, :] = jnp.sum(part, 0, keepdims=True)
    att[...] = nt(low[...], w_out[...]).astype(BF)


def attention_back_kernel(proj, probs, att_grad, out, sums):
    length = proj.shape[0]
    width = proj.shape[1] // 3
    masks = [head_mask(0), head_mask(1)]
    scale = 1.0 / math.sqrt(HEAD_DIM)
    pair_width = 2 * HEAD_DIM

    def pair_step(pair, carry):
        at = pl.multiple_of(pair * pair_width, pair_width)
        k_at = pl.multiple_of(width + at, pair_width)
        v_at = pl.multiple_of(2 * width + at, pair_width)
        queries = proj[:, pl.ds(at, pair_width)]
        keys = proj[:, pl.ds(k_at, pair_width)]
        values = proj[:, pl.ds(v_at, pair_width)]
        grads = att_grad[:, pl.ds(at, pair_width)]
        grads_t = grads.T
        queries_t = queries.T
        grad_q, grad_k_t, grad_v_t = None, [], []
        for half in range(2):
            low = probs[2 * pair + half]
            wide = low.astype(F32)
            grad_p = nt(grads * masks[half], values)
            delta = jnp.sum(grad_p * wide, -1, keepdims=True)
            grad_s = (wide * (grad_p - delta)).astype(BF)
            lanes = slice(half * HEAD_DIM, (half + 1) * HEAD_DIM)
            grad_v_t.append(nn(grads_t[lanes], low))
            grad_k_t.append(nn(queries_t[lanes], grad_s))
            term = nn(grad_s, keys * masks[half])
            grad_q = term if grad_q is None else grad_q + term
        parts = (
            grad_q * scale,
            jnp.concatenate(grad_k_t, 0).T * scale,
            jnp.concatenate(grad_v_t, 0).T,
        )
        for start, part in zip((at, k_at, v_at), parts):
            part_low = part.astype(BF)
            out[:, pl.ds(start, pair_width)] = part_low
            sums[:, pl.ds(start, pair_width)] = jnp.sum(part_low.astype(F32), 0, keepdims=True)
        return carry

    lax.fori_loop(0, width // pair_width, pair_step, 0)


def input_back_kernel(grad_proj, w_qkv, grad_first, out):
    block = 256
    for i in range(w_qkv.shape[0] // block):
        cols = slice(i * block, (i + 1) * block)
        value = grad_first[:, cols] + nt(grad_proj[...], w_qkv[cols, :])
        out[:, cols] = value.astype(BF)


def slot_device(me, bits, slot):
    mixed = 0
    for b in range(bits):
        mixed = mixed | (((slot >> (bits - 1 - b)) & 1) << b)
    return me ^ mixed


def weight_grad_kernel(place, left, right, keep, send, work, *, bits):
    share = keep.shape[1]
    total = left.shape[1]
    block = min(total, 768)
    for r in range(0, total, block):
        work[r : r + block, :] = tn(left[:, r : r + block], right[...]).astype(BF)
    half = keep.shape[0]
    for slot in range(half):
        for ref, index in ((keep, slot), (send, half + slot)):
            device = slot_device(place[1], bits, index)
            ref[slot] = work[pl.ds(pl.multiple_of(device * share, 16), share), :]


def last_grad_kernel(
    place, x, grad_proj, attended, low, sums_two, sums_one, sums_qkv, sums_in, keep, send, work, *, bits
):
    length, width = x.shape
    share = keep.shape[1]
    wide = grad_proj.shape[1]
    half = keep.shape[0]
    devices = 2 * half
    for part in range(3):
        cols = slice(part * width, (part + 1) * width)
        work[:, cols] = tn(x[...], grad_proj[:, cols]).astype(BF)
    work[:, wide : wide + width] = tn(attended[...], low[...]).astype(BF)
    extra = slice(wide + width, wide + width + 128)
    stacked = jnp.concatenate(
        [sums_qkv[:, :width], sums_qkv[:, 2 * width :], sums_two[0:3], sums_one[0:3]], 0
    )
    work[:, extra] = jnp.zeros((width, 128), BF)
    in_share = sums_in.shape[1] // devices
    for d in range(devices):
        rows = [stacked[:, d * share : (d + 1) * share]]
        for k in range(in_share // share):
            at = d * in_share + k * share
            rows.append(sums_in[:, at : at + share])
        rows.append(jnp.zeros((16 - 8 - in_share // share, share), F32))
        block = jnp.concatenate(rows, 0)
        block = jnp.concatenate([block, jnp.zeros((16, 128 - share), F32)], 1)
        high = block.astype(BF)
        work[d * share : d * share + 16, extra] = high
        work[d * share + 16 : d * share + 32, extra] = (block - high.astype(F32)).astype(BF)
    for slot in range(half):
        for ref, index in ((keep, slot), (send, half + slot)):
            device = slot_device(place[1], bits, index)
            ref[slot] = work[pl.ds(pl.multiple_of(device * share, 16), share), :]


def add_extra(left, right):
    total = (
        left[0:16].astype(F32) + left[16:32].astype(F32) + right[0:16].astype(F32) + right[16:32].astype(F32)
    )
    return total


def halve_kernel(kept, came, keep, send, *, extra):
    half = keep.shape[0]
    cols = keep.shape[2] - extra
    for slot in range(2 * half):
        ref, at = (keep, slot) if slot < half else (send, slot - half)
        ref[at, :, :cols] = (
            kept[slot, :, :cols].astype(F32) + came[slot, :, :cols].astype(F32)
        ).astype(BF)
        if extra:
            total = add_extra(kept[slot, :, cols:], came[slot, :, cols:])
            high = total.astype(BF)
            ref[at, 0:16, cols:] = high
            ref[at, 16:32, cols:] = (total - high.astype(F32)).astype(BF)
            ref[at, 32:, cols:] = jnp.zeros((keep.shape[1] - 32, extra), BF)


def finish_kernel(kept, came, out):
    out[...] = kept[0].astype(F32) + came[0].astype(F32)


def finish_last_kernel(
    kept, came, w_qkv, w_out, bq, bv, gain2, bias2, b_back, gain1, bias1, b_out, b_in
):
    wide, width = w_qkv.shape[1], w_out.shape[1]
    share = bq.shape[1]
    total = kept[0, :, : wide + width].astype(F32) + came[0, :, : wide + width].astype(F32)
    w_qkv[...] = total[:, :wide]
    w_out[...] = total[:, wide:]
    vectors = add_extra(kept[0, :, wide + width :], came[0, :, wide + width :])
    for k, ref in enumerate((bq, bv, gain2, bias2, b_back, gain1, bias1, b_out)):
        ref[...] = vectors[k : k + 1, :share]
    pieces = b_in.shape[1] // share
    b_in[...] = jnp.concatenate([vectors[8 + k : 9 + k, :share] for k in range(pieces)], 1)


def plain_grad_kernel(left, right, out):
    out[...] = tn(left[...], right[...])


def swapped(value, axis, mask):
    count = lax.axis_size(axis)
    return lax.ppermute(value, axis, [(i, i ^ mask) for i in range(count)])


def reduce_shares(keep, send, bits, finish, extra=0):
    for b in range(bits):
        came = swapped(send, "dp", 1 << b)
        if b == bits - 1:
            return finish(keep, came)
        half = keep.shape[0] // 2
        shape = (half,) + keep.shape[1:]
        keep, send = kernel_call(
            functools.partial(halve_kernel, extra=extra),
            [sds(shape, BF), sds(shape, BF)],
            [keep, came],
            mib=8,
            name=f"halve{b}",
        )


def gather_packets(packet, bits):
    count = 1 << bits
    order = [3, 2, 1, 0] if bits == 4 else list(range(bits))
    held = packet[None]
    for b in order:
        held = jnp.concatenate([held, swapped(held, "dp", 1 << b)], 0)
    me = lax.axis_index("dp")
    slots = []
    for s in range(count):
        mixed = 0
        for j, b in enumerate(order):
            mixed |= ((s >> j) & 1) << b
        slots.append(mixed)
    inverse = [0] * count
    for s, mixed in enumerate(slots):
        inverse[mixed] = s
    table = jnp.asarray(inverse, jnp.int32)
    return held[table[jnp.arange(count, dtype=jnp.int32) ^ me]]


def shards(
    hidden_in,
    seg_ids,
    labels,
    out_grad,
    w_qkv,
    b_query,
    b_value,
    w_out,
    b_out,
    ln1_gain,
    ln1_bias,
    w_in,
    b_in,
    w_back,
    b_back,
    ln2_gain,
    ln2_bias,
):
    x, cotangent = hidden_in[0], out_grad[0]
    w_qkv, w_out, w_in, w_back = w_qkv[0], w_out[0], w_in[0], w_back[0]
    length, width = x.shape
    hidden = w_in.shape[1]
    heads = width // HEAD_DIM
    count = length // QLEN
    devices = lax.axis_size("dp")
    bits = devices.bit_length() - 1
    tower, me = lax.axis_index("tower"), lax.axis_index("dp")
    place = jnp.stack([tower, me]).astype(jnp.int32)
    seg_col = seg_ids.reshape(length, 1)
    fast = devices == 16

    proj = kernel_call(
        proj_kernel, sds((length, 3 * width), BF), [x, w_qkv, b_query, b_value],
        mib=16, flops=2 * length * 3 * width * width, name="proj",
    )
    cls = kernel_call(
        cls_kernel, sds((count, width), BF),
        [place, seg_ids, x, proj, w_out, b_out, ln1_gain, ln1_bias, w_in, b_in, w_back, b_back,
         ln2_gain, ln2_bias],
        smem=1, mib=16, flops=2 * 256 * width * hidden * 2, name="cls",
    )
    other = swapped(cls, "tower", 1)
    label_rows = jnp.stack([labels // 256, labels % 256]).astype(F32).astype(BF)
    label_rows = jnp.pad(label_rows, ((0, PACKET - count - SEGS - 2), (0, width - count)))
    q_rows = jnp.where(tower == 0, cls, other)
    p_rows = jnp.where(tower == 0, other, cls)[:SEGS]
    packet = jnp.concatenate([q_rows, p_rows, label_rows], 0)
    if fast:
        packets = gather_packets(packet, bits)
    else:
        packets = lax.all_gather(packet, "dp", axis=0)

    attended, probs = kernel_call(
        attention_kernel, [sds((length, width), BF), sds((heads, length, length), BF)],
        [place, seg_ids, seg_col, proj], smem=1,
        scratch=[pltpu.VMEM((length, length), F32)],
        mib=16, flops=4 * heads * length * length * 256, name="attention",
    )
    work = pltpu.VMEM((length, width), F32)
    n1, r1, first_low = kernel_call(
        first_kernel,
        [sds((length, width), F32), sds((length, 1), F32), sds((length, width), BF)],
        [x, attended, w_out, b_out, ln1_gain, ln1_bias], scratch=[work],
        mib=16, flops=2 * length * width * width, name="first",
    )
    act, slope = kernel_call(
        inner_kernel, [sds((length, hidden), BF), sds((length, hidden), BF)],
        [first_low, w_in, b_in], scratch=[pltpu.VMEM((2, length, 256), F32)],
        mib=16, flops=8 * length * width * hidden, name="inner",
    )
    n2, r2, out_hidden = kernel_call(
        second_kernel,
        [sds((length, width), F32), sds((length, 1), F32), sds((length, width), BF)],
        [act, w_back, b_back, n1, ln1_gain, ln1_bias, ln2_gain, ln2_bias], scratch=[work],
        mib=16, flops=2 * length * width * hidden, name="second",
    )

    queries = packets[:, :count].reshape(devices * count, width)
    passages = packets[:, count : count + SEGS].reshape(devices * SEGS, width)
    label_parts = packets[:, count + SEGS : count + SEGS + 2, :count].astype(jnp.int32)
    all_labels = (label_parts[:, 0] * 256 + label_parts[:, 1]).reshape(devices * count)
    cls_grad = kernel_call(
        loss_kernel, sds((count, width), F32),
        [place, queries, passages, all_labels[None], all_labels[:, None]], smem=1,
        mib=24, flops=8 * devices * count * devices * SEGS * width, name="loss",
    )

    grad_second, second_low, sums_two = kernel_call(
        second_back_kernel,
        [sds((length, width), F32), sds((length, width), BF), sds((8, width), F32)],
        [place, seg_ids, cotangent, cls_grad, n2, r2, ln2_gain], smem=1, scratch=[work],
        mib=16, flops=2 * length * width * 256, name="second_back",
    )

    def weight_grad(left, right, name):
        rows, cols = left.shape[1], right.shape[1]
        flops = 2 * length * rows * cols
        if not fast:
            whole = kernel_call(
                plain_grad_kernel, sds((rows, cols), F32), [left, right], mib=24, flops=flops, name=name
            )
            return lax.psum_scatter(whole, "dp", scatter_dimension=0, tiled=True)
        share = rows // devices
        shape = sds((devices // 2, share, cols), BF)
        keep, send = kernel_call(
            functools.partial(weight_grad_kernel, bits=bits), [shape, shape], [place, left, right],
            smem=1, scratch=[pltpu.VMEM((rows, cols), BF)], mib=24, flops=flops, name=name,
        )
        return reduce_shares(
            keep, send, bits,
            lambda kept, came: kernel_call(
                finish_kernel, sds((share, cols), F32), [kept, came], mib=8, name="finish"
            ),
        )

    share_w_back = weight_grad(act, second_low, "grad_w_back")
    inner_low, sums_in = kernel_call(
        inner_back_kernel, [sds((length, hidden), BF), sds((1, hidden), F32)],
        [second_low, w_back, slope], mib=16, flops=2 * length * width * hidden, name="inner_back",
    )
    share_w_in = weight_grad(first_low, inner_low, "grad_w_in")
    grad_first, branch_low, att_grad, sums_one = kernel_call(
        first_back_kernel,
        [sds((length, width), F32), sds((length, width), BF), sds((length, width), BF), sds((8, width), F32)],
        [inner_low, w_in, grad_second, n1, r1, ln1_gain, w_out], scratch=[work],
        mib=16, flops=2 * length * width * (hidden + width), name="first_back",
    )
    grad_proj, sums_qkv = kernel_call(
        attention_back_kernel, [sds((length, 3 * width), BF), sds((1, 3 * width), F32)],
        [proj, probs, att_grad], mib=16, flops=8 * heads * length * length * 256, name="attention_back",
    )
    if fast:
        share = width // devices
        cols = 4 * width + 128
        shape = sds((devices // 2, share, cols), BF)
        keep, send = kernel_call(
            functools.partial(last_grad_kernel, bits=bits), [shape, shape],
            [place, x, grad_proj, attended, branch_low, sums_two, sums_one, sums_qkv, sums_in],
            smem=1, scratch=[pltpu.VMEM((width, cols), BF)], mib=24,
            flops=8 * length * width * width, name="grad_w_qkv_out",
        )
        small = sds((1, share), F32)
        (
            share_w_qkv, share_w_out, share_bq, share_bv, share_gain2, share_bias2, share_b_back,
            share_gain1, share_bias1, share_b_out, share_b_in,
        ) = reduce_shares(
            keep, send, bits,
            lambda kept, came: kernel_call(
                finish_last_kernel,
                [sds((share, 3 * width), F32), sds((share, width), F32)] + [small] * 8
                + [sds((1, hidden // devices), F32)],
                [kept, came], mib=8, name="finish_last",
            ),
            extra=128,
        )
    else:
        share_w_qkv = weight_grad(x, grad_proj, "grad_w_qkv")
        share_w_out = weight_grad(attended, branch_low, "grad_w_out")

        def scattered(vector):
            return lax.psum_scatter(vector, "dp", scatter_dimension=1, tiled=True)

        share_bq, share_bv = scattered(sums_qkv[:, :width]), scattered(sums_qkv[:, 2 * width :])
        share_gain2, share_bias2, share_b_back = (scattered(sums_two[k : k + 1]) for k in range(3))
        share_gain1, share_bias1, share_b_out = (scattered(sums_one[k : k + 1]) for k in range(3))
        share_b_in = scattered(sums_in)
    grad_hidden = kernel_call(
        input_back_kernel, sds((length, width), BF), [grad_proj, w_qkv, grad_first],
        mib=16, flops=6 * length * width * width, name="input_back",
    )
    return (
        out_hidden[None],
        grad_hidden[None],
        share_w_qkv[None],
        share_bq,
        share_bv,
        share_w_out[None],
        share_b_out,
        share_gain1,
        share_bias1,
        share_w_in[None],
        share_b_in,
        share_w_back[None],
        share_b_back,
        share_gain2,
        share_bias2,
    )


def solution(mesh):
    matrix, vector = P("tower", None, None), P("tower", None)
    rows, spread = P("tower", "dp", None), P("tower", "dp")
    return jax.shard_map(
        shards,
        mesh=mesh,
        in_specs=(
            rows, P("dp", None), P("dp"), rows, matrix, vector, vector, matrix, vector, vector, vector,
            matrix, vector, matrix, vector, vector, vector,
        ),
        out_specs=(
            rows, rows, rows, spread, spread, rows, spread, spread, spread, rows, spread, rows, spread,
            spread, spread,
        ),
        check_vma=False,
    )
```

```python
import functools
import math

import jax
import jax.numpy as jnp
from jax import lax
from jax.experimental import pallas as pl
from jax.experimental.pallas import tpu as pltpu
from jax.sharding import PartitionSpec as P

HEAD_DIM = 64
QLEN = 32
SEGS = 4
PACKET = 24
EPS = 1e-05
BF = jnp.bfloat16
F32 = jnp.float32
TILE = 32

VM = pl.BlockSpec(memory_space=pltpu.VMEM)
SM = pl.BlockSpec(memory_space=pltpu.SMEM)
HB = pl.BlockSpec(memory_space=pltpu.HBM)


def nn(a, b):
    return lax.dot_general(a, b, (((1,), (0,)), ((), ())), preferred_element_type=F32)


def nt(a, b):
    return lax.dot_general(a, b, (((1,), (1,)), ((), ())), preferred_element_type=F32)


def tn(a, b):
    return lax.dot_general(a, b, (((0,), (0,)), ((), ())), preferred_element_type=F32)


def kernel_call(body, outs, args, scratch=(), smem=0, hbm=0, mib=32, flops=0, name=None):
    single = not isinstance(outs, (list, tuple))
    shapes = [outs] if single else list(outs)
    moved = sum(math.prod(a.shape) * a.dtype.itemsize for a in list(args) + shapes)
    result = pl.pallas_call(
        body,
        out_shape=shapes,
        in_specs=[SM] * smem + [VM] * (len(args) - smem - hbm) + [HB] * hbm,
        out_specs=[VM] * len(shapes),
        scratch_shapes=list(scratch),
        compiler_params=pltpu.CompilerParams(vmem_limit_bytes=mib << 20),
        cost_estimate=pl.CostEstimate(flops=flops // 1000, bytes_accessed=moved // 1000, transcendentals=0),
        name=name,
    )(*args)
    return result[0] if single else result


def sds(shape, dtype):
    return jax.ShapeDtypeStruct(shape, dtype)


def fold(value):
    rows, cols = value.shape
    return jnp.sum(value.reshape(rows // 8, 8, cols), 0)


def head_mask(half):
    lane = lax.broadcasted_iota(jnp.int32, (1, 2 * HEAD_DIM), 1)
    return (lane // HEAD_DIM == half).astype(F32).astype(BF)


def normalise(value):
    centred = value - jnp.mean(value, -1, keepdims=True)
    inverse = lax.rsqrt(jnp.mean(centred * centred, -1, keepdims=True) + EPS)
    return centred * inverse, inverse


def norm_back(grad, normed, inverse, gain):
    scaled = grad * gain
    return inverse * (
        scaled
        - jnp.mean(scaled, -1, keepdims=True)
        - normed * jnp.mean(scaled * normed, -1, keepdims=True)
    )


def gelu_pair(value):
    cdf = 0.5 * lax.erf(value * (1.0 / math.sqrt(2.0))) + 0.5
    density = jnp.exp(value * value * -0.5) * (1.0 / math.sqrt(2.0 * math.pi))
    return value * cdf, cdf + value * density


def proj_kernel(x_hbm, w_hbm, bq_hbm, bv_hbm, out, x, w0, w1, w2, bq, bv, sems):
    width = x.shape[1]
    parts = (w0, w1, w2)
    copies = [
        pltpu.make_async_copy(w_hbm.at[:, pl.ds(k * width, width)], parts[k], sems.at[k]) for k in range(3)
    ]
    x_copy = pltpu.make_async_copy(x_hbm, x, sems.at[3])
    bq_copy = pltpu.make_async_copy(bq_hbm, bq, sems.at[4])
    bv_copy = pltpu.make_async_copy(bv_hbm, bv, sems.at[5])
    for copy in (x_copy, copies[1], copies[0], bq_copy, copies[2], bv_copy):
        copy.start()
    x_copy.wait()
    for k in (1, 0, 2):
        copies[k].wait()
        value = nn(x[...], parts[k][...])
        if k == 0:
            bq_copy.wait()
            value = value + bq[...]
        if k == 2:
            bv_copy.wait()
            value = value + bv[...]
        out[:, k * width : (k + 1) * width] = value.astype(BF)


def chosen_rows(tower, seg, count, length):
    row = lax.broadcasted_iota(jnp.int32, (count, 1), 0)
    place = lax.broadcasted_iota(jnp.int32, (count, length), 1)
    start = jnp.sum((seg < row).astype(F32), 1, keepdims=True).astype(jnp.int32)
    wanted = jnp.where(tower == 0, row * QLEN, jnp.where(row < SEGS, start, -1))
    return (place == wanted).astype(F32)


def cls_kernel(place, seg, x, proj, w_out, b_out, g1, b1, w_in, b_in, w_back, b_back, g2, b2, cls):
    length, width = x.shape
    count = cls.shape[0]
    heads = width // HEAD_DIM
    tower = place[0]
    pick = chosen_rows(tower, seg[...], count, length)
    pick_low = pick.astype(BF)
    x_cls = nn(pick_low, x[...])
    q_cls = (nn(pick_low, proj[:, :width]) * (1.0 / math.sqrt(HEAD_DIM))).astype(BF)
    place_row = lax.broadcasted_iota(jnp.int32, (1, length), 1)
    own_seg = jnp.where(tower == 0, place_row // QLEN, seg[...])
    row = lax.broadcasted_iota(jnp.int32, (count, 1), 0)
    bias = jnp.where(own_seg == row, 0.0, -1e9)
    lane_head = lax.broadcasted_iota(jnp.int32, (1, width), 1) // HEAD_DIM
    spread = jnp.concatenate(
        [q_cls * (lane_head == h).astype(F32).astype(BF) for h in range(heads)], 0
    )
    scores = nt(spread, proj[:, width : 2 * width]) + jnp.concatenate([bias] * heads, 0)
    shifted = jnp.exp(scores - jnp.max(scores, -1, keepdims=True))
    probs = (shifted / jnp.sum(shifted, -1, keepdims=True)).astype(BF)
    mixed = nn(probs, proj[:, 2 * width :])
    attended = jnp.zeros((count, width), F32)
    for h in range(heads):
        attended = attended + jnp.where(lane_head == h, mixed[h * count : (h + 1) * count], 0.0)
    first = x_cls + (nn(attended.astype(BF), w_out[...]) + b_out[...])
    normed = normalise(first)[0] * g1[...] + b1[...]
    inner = nn(normed.astype(BF), w_in[...]) + b_in[...]
    act = gelu_pair(inner)[0].astype(BF)
    second = normed + (nn(act, w_back[...]) + b_back[...])
    final = normalise(second)[0] * g2[...] + b2[...]
    cls[...] = final.astype(BF)


def attention_kernel(place, seg_row, seg_col, proj, attended, probs, bias, *work):
    length = proj.shape[0]
    width = proj.shape[1] // 3
    tower = place[0]
    lane = lax.broadcasted_iota(jnp.int32, (1, length), 1)
    sub = lax.broadcasted_iota(jnp.int32, (length, 1), 0)
    row_seg = jnp.where(tower == 0, lane // QLEN, seg_row[...])
    col_seg = jnp.where(tower == 0, sub // QLEN, seg_col[...])
    bias[...] = jnp.where(col_seg == row_seg, 0.0, -1e9)
    masks = [head_mask(0), head_mask(1)]
    scale = jnp.asarray(1.0 / math.sqrt(HEAD_DIM), BF)
    step = 2 * HEAD_DIM
    pairs = width // step

    def columns(part, pair):
        return proj[:, part * width + pair * step : part * width + (pair + 1) * step]

    def scores(pair):
        queries, keys = columns(0, pair) * scale, columns(1, pair)
        for half in range(2):
            work[pair % 2][half] = nt(queries * masks[half], keys)

    def soften(pair):
        for half in range(2):
            for r in range(0, length, TILE):
                value = work[pair % 2][half, r : r + TILE, :] + bias[r : r + TILE, :]
                shifted = jnp.exp(value - jnp.max(value, -1, keepdims=True))
                total = jnp.sum(shifted, -1, keepdims=True)
                probs[2 * pair + half, r : r + TILE, :] = (shifted * (1.0 / total)).astype(BF)

    def mix(pair):
        values = columns(2, pair)
        mixed = nn(probs[2 * pair], values * masks[0]) + nn(probs[2 * pair + 1], values * masks[1])
        attended[:, pair * step : (pair + 1) * step] = mixed.astype(BF)

    scores(0)
    for pair in range(pairs):
        if pair + 1 < pairs:
            scores(pair + 1)
        if pair > 0:
            mix(pair - 1)
        soften(pair)
    mix(pairs - 1)


def first_kernel(x, attended, w_out, b_out, g1, b1, n1, r1, low, work):
    work[...] = nn(attended[...], w_out[...])
    for r in range(0, x.shape[0], TILE):
        rows = slice(r, r + TILE)
        first = x[rows, :].astype(F32) + (work[rows, :] + b_out[...])
        normed, inverse = normalise(first)
        n1[rows, :] = normed
        r1[rows, :] = inverse
        low[rows, :] = (normed * g1[...] + b1[...]).astype(BF)


def inner_kernel(low, w_in, b_in, act, slope, work_a, work_b):
    length = low.shape[0]
    block = work_a.shape[1]
    blocks = w_in.shape[1] // block

    def columns(i):
        return pl.ds(pl.multiple_of(i * block, block), block)

    def gelu_block(i, work):
        bias = b_in[:, columns(i)]
        for r in range(0, length, TILE):
            value, grad = gelu_pair(work[r : r + TILE, :] + bias)
            act[r : r + TILE, columns(i)] = value.astype(BF)
            slope[r : r + TILE, columns(i)] = grad.astype(BF)

    work_a[...] = nn(low[...], w_in[:, :block])

    def step(k, carry):
        i = 2 * k
        work_b[...] = nn(low[...], w_in[:, columns(i + 1)])
        gelu_block(i, work_a)
        work_a[...] = nn(low[...], w_in[:, columns(jnp.minimum(i + 2, blocks - 1))])
        gelu_block(i + 1, work_b)
        return carry

    lax.fori_loop(0, blocks // 2, step, 0)


def second_kernel(act, w_back, b_back, n1, g1, b1, g2, b2, n2, r2, out, work_a, work_b):
    length = act.shape[0]
    part = length // 2
    works = (work_a, work_b)

    def normalise_part(k):
        for r in range(0, part, TILE):
            rows = slice(k * part + r, k * part + r + TILE)
            branch = works[k][r : r + TILE, :] + b_back[...]
            second = (n1[rows, :] * g1[...] + b1[...]) + branch
            normed, inverse = normalise(second)
            n2[rows, :] = normed
            r2[rows, :] = inverse
            out[rows, :] = (normed * g2[...] + b2[...]).astype(BF)

    work_a[...] = nn(act[:part, :], w_back[...])
    work_b[...] = nn(act[part:, :], w_back[...])
    normalise_part(0)
    normalise_part(1)


def packet_kernel(place, cls, other, labels, out):
    query = place[0] == 0
    count, width = cls.shape
    mine, came = cls[...].astype(F32), other[...].astype(F32)
    q_rows = jnp.where(query, mine, came)
    p_rows = jnp.where(query, came, mine)[:SEGS]
    value = labels[...]
    gap = jnp.zeros((1, 128 - count), F32)
    row = jnp.concatenate(
        [(value >> 8).astype(F32), gap, (value & 255).astype(F32), gap, jnp.zeros((1, width - 256), F32)], 1
    )
    rest = jnp.zeros((PACKET - count - SEGS - 1, width), F32)
    out[...] = jnp.concatenate([q_rows, p_rows, row, rest], 0).astype(BF)


def loss_kernel(place, near, far, grad, *, order, count):
    tower, me = place[0], place[1]
    packets = jnp.concatenate([near[...], far[...]], 0)
    total, width = packets.shape
    scale = 2.0 / math.sqrt(width)
    row = lax.broadcasted_iota(jnp.int32, (total, 1), 0)
    col = lax.broadcasted_iota(jnp.int32, (1, total), 1)
    col_slot, col_part = col // PACKET, col % PACKET
    mixed = jnp.zeros_like(col)
    for j, b in enumerate(order):
        mixed = mixed | (((col_slot >> j) & 1) << b)
    is_passage = jnp.logical_and(col_part >= count, col_part < count + SEGS)
    number = jnp.where(is_passage, (mixed ^ me) * SEGS + (col_part - count), -1)
    label_of = ((row // PACKET) * PACKET + (count + SEGS) == col).astype(F32).astype(BF)
    label_rows = nn(label_of, packets[:, :256])
    lane = lax.broadcasted_iota(jnp.int32, (1, 256), 1)
    part = row % PACKET
    weight = jnp.where(lane == part, 256.0, 0.0) + jnp.where(lane == part + 128, 1.0, 0.0)
    label = jnp.sum(label_rows * weight, 1, keepdims=True).astype(jnp.int32)
    logits = jnp.where(is_passage, nt(packets, packets) * scale, -1e30)
    soft = jnp.exp(logits - jnp.max(logits, -1, keepdims=True))
    soft = soft / jnp.sum(soft, -1, keepdims=True)
    grad_logits = soft - (number == label).astype(F32)
    grad_logits = grad_logits * (part < count).astype(F32)
    wide = packets.astype(F32)
    grad_q = jnp.dot(
        grad_logits[:count], wide, precision=lax.Precision.HIGHEST, preferred_element_type=F32
    )
    pick = lax.broadcasted_iota(jnp.int32, (count, 1), 0)
    pick = jnp.logical_and(pick + count == col, pick < SEGS).astype(F32)
    turned = lax.dot_general(
        pick, grad_logits, (((1,), (1,)), ((), ())),
        precision=lax.Precision.HIGHEST, preferred_element_type=F32,
    )
    grad_p = jnp.dot(turned, wide, precision=lax.Precision.HIGHEST, preferred_element_type=F32)
    grad[...] = jnp.where(tower == 0, grad_q, grad_p) * scale


def plain_loss(packets, tower, me, count):
    devices, _, width = packets.shape
    scale = 2.0 / math.sqrt(width)
    queries = packets[:, :count].reshape(devices * count, width)
    passages = packets[:, count : count + SEGS].reshape(devices * SEGS, width)
    row = packets[:, count + SEGS].astype(jnp.int32)
    label = (row[:, :count] * 256 + row[:, 128 : 128 + count]).reshape(devices * count, 1)
    soft = jax.nn.softmax(nt(queries, passages) * scale, -1)
    grad = soft - (label == jnp.arange(devices * SEGS, dtype=jnp.int32)).astype(F32)
    grad_q = lax.dynamic_slice_in_dim(grad, me * count, count, 0)
    grad_q = jnp.dot(grad_q, passages.astype(F32), precision=lax.Precision.HIGHEST)
    grad_p = lax.dynamic_slice_in_dim(grad, me * SEGS, SEGS, 1)
    grad_p = jnp.dot(grad_p.T, queries.astype(F32), precision=lax.Precision.HIGHEST)
    grad_p = jnp.pad(grad_p, ((0, count - SEGS), (0, 0)))
    return jnp.where(tower == 0, grad_q, grad_p) * scale


def split_three(value):
    high = value.astype(BF)
    rest = value - high.astype(F32)
    middle = rest.astype(BF)
    return jnp.concatenate([high, middle, (rest - middle.astype(F32)).astype(BF)], 0)


def norm_back_rows(rows, grad, normed, inverse, gain, out, low, totals):
    back = norm_back(grad, normed[rows, :], inverse[rows, :], gain[...])
    out[rows, :] = back
    back_low = back.astype(BF)
    low[rows, :] = back_low
    parts = (fold(grad * normed[rows, :]), fold(grad), fold(back_low.astype(F32)))
    return parts if totals is None else tuple(a + b for a, b in zip(totals, parts))


def second_back_kernel(place, seg, out_grad, cls_grad, n2, r2, g2, grad, low, sums, work):
    length, width = out_grad.shape
    count = cls_grad.shape[0]
    pick = chosen_rows(place[0], seg[...], count, length).astype(BF)
    work[...] = tn(jnp.concatenate([pick] * 3, 0), split_three(cls_grad[...]))
    totals = None
    for r in range(0, length, TILE):
        rows = slice(r, r + TILE)
        final = out_grad[rows, :].astype(F32) + work[rows, :]
        totals = norm_back_rows(rows, final, n2, r2, g2, grad, low, totals)
    for k, part in enumerate(totals):
        sums[k : k + 1, :] = jnp.sum(part, 0, keepdims=True)


def inner_back_kernel(low, w_back, slope, out, sums):
    block = 256
    for i in range(w_back.shape[0] // block):
        cols = slice(i * block, (i + 1) * block)
        value = (nt(low[...], w_back[cols, :]) * slope[:, cols].astype(F32)).astype(BF)
        out[:, cols] = value
        sums[:, cols] = jnp.sum(value.astype(F32), 0, keepdims=True)


def first_back_kernel(inner, w_in, grad_second, n1, r1, g1, w_out, grad, low, att, sums, work_a, work_b):
    length, width = grad_second.shape
    part = length // 2
    works = (work_a, work_b)
    for k in range(2):
        works[k][...] = nt(inner[k * part : (k + 1) * part, :], w_in[...])
    totals = None
    for k in range(2):
        for r in range(0, part, TILE):
            rows = slice(k * part + r, k * part + r + TILE)
            value = grad_second[rows, :] + works[k][r : r + TILE, :]
            totals = norm_back_rows(rows, value, n1, r1, g1, grad, low, totals)
        rows = slice(k * part, (k + 1) * part)
        att[rows, :] = nt(low[rows, :], w_out[...]).astype(BF)
    for k, total in enumerate(totals):
        sums[k : k + 1, :] = jnp.sum(total, 0, keepdims=True)


def attention_back_kernel(proj, probs, att_grad, out, sums, dp_a, dp_b, ds_a, ds_b, *, first):
    length = proj.shape[0]
    width = proj.shape[1] // 3
    own = out.shape[1] // 3
    masks = [head_mask(0), head_mask(1)]
    scale = 1.0 / math.sqrt(HEAD_DIM)
    step = 2 * HEAD_DIM
    pairs = own // step
    dp, ds = (dp_a, dp_b), (ds_a, ds_b)

    def columns(part, pair):
        at = part * width + (first + pair) * step
        return proj[:, at : at + step]

    def grad_columns(pair):
        at = (first + pair) * step
        return att_grad[:, at : at + step]

    def grad_probs(pair):
        grads, values = grad_columns(pair), columns(2, pair)
        for half in range(2):
            dp[pair % 2][half] = nt(grads * masks[half], values)

    def grad_scores(pair):
        for half in range(2):
            for r in range(0, length, TILE):
                wide = probs[2 * (first + pair) + half, r : r + TILE, :].astype(F32)
                grad = dp[pair % 2][half, r : r + TILE, :]
                delta = jnp.sum(grad * wide, -1, keepdims=True)
                ds[pair % 2][half, r : r + TILE, :] = (wide * (grad - delta)).astype(BF)

    def results(pair):
        queries_t, grads_t = columns(0, pair).T, grad_columns(pair).T
        keys = columns(1, pair)
        grad_q, grad_k_t, grad_v_t = None, [], []
        for half in range(2):
            scores = ds[pair % 2][half]
            lanes = slice(half * HEAD_DIM, (half + 1) * HEAD_DIM)
            grad_v_t.append(nn(grads_t[lanes], probs[2 * (first + pair) + half]))
            grad_k_t.append(nn(queries_t[lanes], scores))
            term = nn(scores, keys * masks[half])
            grad_q = term if grad_q is None else grad_q + term
        parts = (
            grad_q * scale,
            jnp.concatenate(grad_k_t, 0).T * scale,
            jnp.concatenate(grad_v_t, 0).T,
        )
        for k, part in enumerate(parts):
            cols = slice(k * own + pair * step, k * own + (pair + 1) * step)
            part_low = part.astype(BF)
            out[:, cols] = part_low
            sums[:, cols] = jnp.sum(part_low.astype(F32), 0, keepdims=True)

    grad_probs(0)
    for pair in range(pairs):
        if pair + 1 < pairs:
            grad_probs(pair + 1)
        if pair > 0:
            results(pair - 1)
        grad_scores(pair)
    results(pairs - 1)


def input_back_kernel(left, right, w_qkv, grad_first, out, work):
    width = out.shape[1]
    for k in range(3):
        at = k * width
        for part in (left, right):
            own = part.shape[1] // 3
            work[:, at : at + own] = part[:, k * own : (k + 1) * own]
            at += own
    block = 256
    for i in range(width // block):
        cols = slice(i * block, (i + 1) * block)
        value = grad_first[:, cols] + nt(work[...], w_qkv[cols, :])
        out[:, cols] = value.astype(BF)


def slot_device(me, order, slot):
    mixed = 0
    for j, b in enumerate(order):
        mixed = mixed | (((slot >> (len(order) - 1 - j)) & 1) << b)
    return me ^ mixed


def spread_shares(place, work, outs, order):
    me = place[1]
    if len(outs) == 1:
        outs = (outs[0].at[0], outs[0].at[1])
        me = me & ~(1 << order[0])
    keep, *sends = outs
    half, share, _ = keep.shape
    for slot in range(2 * half):
        ref, at = (keep, slot) if slot < half else piece_of(sends, slot - half)
        device = slot_device(me, order, slot)
        ref[at] = work[pl.ds(pl.multiple_of(device * share, 16), share), :]


def piece_of(refs, slot):
    size = refs[0].shape[0]
    return refs[slot // size], slot % size


def weight_grad_kernel(place, *refs, order, pairs):
    *outs, work = refs[2 * pairs :]
    at = 0
    for left, right in zip(refs[: 2 * pairs : 2], refs[1 : 2 * pairs : 2]):
        cols = slice(at, at + right.shape[1])
        block = min(left.shape[1], 768)
        for r in range(0, left.shape[1], block):
            work[r : r + block, cols] = tn(left[:, r : r + block], right[...]).astype(BF)
        at += right.shape[1]
    spread_shares(place, work, outs, order)


def last_grad_kernel(
    place, x, grad_proj, sums_two, sums_one, sums_left, sums_right, sums_in, out, work, *, order
):
    width = x.shape[1]
    share = out.shape[2]
    devices = 2 * out.shape[1]
    wide = grad_proj.shape[1]
    work[:, :wide] = tn(x[...], grad_proj[...]).astype(BF)
    extra = slice(wide, wide + 128)
    thirds = [sums.shape[1] // 3 for sums in (sums_left, sums_right)]
    query, value = (
        jnp.concatenate(
            [sums[:, k * own : (k + 1) * own] for sums, own in zip((sums_left, sums_right), thirds)], 1
        )
        for k in (0, 2)
    )
    stacked = jnp.concatenate([query, value, sums_two[0:3], sums_one[0:3]], 0)
    work[:, extra] = jnp.zeros((width, 128), BF)
    in_share = sums_in.shape[1] // devices
    for d in range(devices):
        rows = [stacked[:, d * share : (d + 1) * share]]
        for k in range(in_share // share):
            at = d * in_share + k * share
            rows.append(sums_in[:, at : at + share])
        rows.append(jnp.zeros((16 - 8 - in_share // share, share), F32))
        block = jnp.concatenate(rows, 0)
        block = jnp.concatenate([block, jnp.zeros((16, 128 - share), F32)], 1)
        high = block.astype(BF)
        work[d * share : d * share + 16, extra] = high
        work[d * share + 16 : d * share + 32, extra] = (block - high.astype(F32)).astype(BF)
    spread_shares(place, work, [out], order)


def add_extra(left, right):
    total = (
        left[0:16].astype(F32) + left[16:32].astype(F32) + right[0:16].astype(F32) + right[16:32].astype(F32)
    )
    return total


def halve_kernel(*refs, cames, extra):
    kept, came, (keep, *sends) = refs[0], refs[1 : 1 + cames], refs[1 + cames :]
    half = keep.shape[0]
    cols = keep.shape[2] - extra
    for slot in range(2 * half):
        ref, at = (keep, slot) if slot < half else piece_of(sends, slot - half)
        other, there = piece_of(came, slot)
        ref[at, :, :cols] = (kept[slot, :, :cols].astype(F32) + other[there, :, :cols].astype(F32)).astype(BF)
        if extra:
            total = add_extra(kept[slot, :, cols:], other[there, :, cols:])
            high = total.astype(BF)
            ref[at, 0:16, cols:] = high
            ref[at, 16:32, cols:] = (total - high.astype(F32)).astype(BF)
            ref[at, 32:, cols:] = jnp.zeros((keep.shape[1] - 32, extra), BF)


def halve_cores_kernel(both, *outs, extra):
    halve_kernel(both.at[0], both.at[1], *outs, cames=1, extra=extra)


def finish_kernel(kept, came, out):
    out[...] = kept[0].astype(F32) + came[0].astype(F32)


def finish_last_kernel(
    kept, came, kept_last, came_last, w_qkv, w_out, bq, bv, gain2, bias2, b_back, gain1, bias1, b_out, b_in
):
    width = w_out.shape[1]
    share = bq.shape[1]
    left, right = (kept.shape[2] - width) // 3, (kept_last.shape[2] - 128) // 3
    for k in range(3):
        at = k * width
        cols = slice(k * left, (k + 1) * left)
        w_qkv[:, at : at + left] = kept[0, :, cols].astype(F32) + came[0, :, cols].astype(F32)
        cols = slice(k * right, (k + 1) * right)
        w_qkv[:, at + left : at + width] = kept_last[0, :, cols].astype(F32) + came_last[0, :, cols].astype(F32)
    w_out[...] = kept[0, :, 3 * left :].astype(F32) + came[0, :, 3 * left :].astype(F32)
    vectors = add_extra(kept_last[0, :, 3 * right :], came_last[0, :, 3 * right :])
    for k, ref in enumerate((bq, bv, gain2, bias2, b_back, gain1, bias1, b_out)):
        ref[...] = vectors[k : k + 1, :share]
    pieces = b_in.shape[1] // share
    b_in[...] = jnp.concatenate([vectors[8 + k : 9 + k, :share] for k in range(pieces)], 1)


def plain_grad_kernel(left, right, out):
    out[...] = tn(left[...], right[...])


def swapped(value, axis, mask):
    count = lax.axis_size(axis)
    return lax.ppermute(value, axis, [(i, i ^ mask) for i in range(count)])


class Sequence:
    def __init__(self):
        self.last = None

    def now(self, value):
        return value if self.last is None else after(value, self.last)

    def ran(self, results):
        self.last = results[0]
        return results

    def chunk(self, outs, extra=0, pieces=1):
        chunk = {"extra": extra}
        if len(outs) > 1:
            chunk["keep"], *chunk["sends"] = self.ran(outs)
        else:
            pairs = [[i, i + 1] for i in range(0, lax.axis_size("dp"), 2)]
            both = lax.all_to_all(outs[0], "dp", 0, 0, tiled=True, axis_index_groups=pairs)
            self.last = both
            self.parted(chunk, functools.partial(halve_cores_kernel, extra=extra), [both], both.shape[1:], pieces)
        return chunk

    def parted(self, chunk, body, args, shape, pieces):
        half = sds((shape[0] // 2,) + shape[1:], BF)
        piece = sds((shape[0] // 2 // pieces,) + shape[1:], BF)
        chunk["keep"], *chunk["sends"] = self.ran(
            kernel_call(body, [half] + [piece] * pieces, args, mib=4, name="halve")
        )

    def go(self, chunk, bit, behind=None):
        sends = [self.now(send) for send in chunk["sends"]]
        if behind is not None:
            sends = [after(send, *behind["came"]) for send in sends]
        chunk["came"] = [swapped(send, "dp", 1 << bit) for send in sends]

    def take(self, chunk, pieces=1):
        keep, came = chunk["keep"], [self.now(value) for value in chunk["came"]]
        body = functools.partial(halve_kernel, cames=len(came), extra=chunk["extra"])
        self.parted(chunk, body, [keep] + came, keep.shape, pieces)

    def finish(self, chunk):
        args = [chunk["keep"], self.now(chunk["came"][0])]
        return self.ran([kernel_call(finish_kernel, sds(args[0].shape[1:], F32), args, mib=4, name="finish")])[0]


def after(value, *earlier):
    return lax.optimization_barrier((value,) + earlier)[0]


def shards(
    hidden_in,
    seg_ids,
    labels,
    out_grad,
    w_qkv,
    b_query,
    b_value,
    w_out,
    b_out,
    ln1_gain,
    ln1_bias,
    w_in,
    b_in,
    w_back,
    b_back,
    ln2_gain,
    ln2_bias,
):
    x, cotangent = hidden_in[0], out_grad[0]
    w_qkv, w_out, w_in, w_back = w_qkv[0], w_out[0], w_in[0], w_back[0]
    length, width = x.shape
    hidden = w_in.shape[1]
    heads = width // HEAD_DIM
    count = length // QLEN
    devices = lax.axis_size("dp")
    bits = devices.bit_length() - 1
    tower, me = lax.axis_index("tower"), lax.axis_index("dp")
    place = jnp.stack([tower, me]).astype(jnp.int32)
    seg_col = seg_ids.reshape(length, 1)
    fast = devices == 16

    proj = kernel_call(
        proj_kernel, sds((length, 3 * width), BF), [x, w_qkv, b_query, b_value], hbm=4,
        scratch=[pltpu.VMEM((length, width), BF)] + [pltpu.VMEM((width, width), BF)] * 3
        + [pltpu.VMEM((1, width), F32)] * 2 + [pltpu.SemaphoreType.DMA((6,))],
        mib=8, flops=2 * length * 3 * width * width, name="proj",
    )
    cls = kernel_call(
        cls_kernel, sds((count, width), BF),
        [place, seg_ids, x, proj, w_out, b_out, ln1_gain, ln1_bias, w_in, b_in, w_back, b_back,
         ln2_gain, ln2_bias],
        smem=1, mib=3, flops=2 * 256 * width * hidden * 2, name="cls",
    )
    other = swapped(cls, "tower", 1)
    attended, probs = kernel_call(
        attention_kernel, [sds((length, width), BF), sds((heads, length, length), BF)],
        [place, seg_ids, seg_col, after(proj, cls)], smem=1,
        scratch=[pltpu.VMEM((length, length), F32)] + [pltpu.VMEM((2, length, length), F32)] * 2,
        mib=9, flops=4 * heads * length * length * 256, name="attention",
    )
    held = kernel_call(
        packet_kernel, sds((PACKET, width), BF), [place, cls, after(other, attended), labels[None]],
        smem=1, mib=1, name="packet",
    )
    order = [3, 2, 1, 0] if fast else list(range(bits))
    if fast:
        came = swapped(held, "dp", 1 << order[0])
    work, half_work = pltpu.VMEM((length, width), F32), pltpu.VMEM((length // 2, width), F32)
    n1, r1, first_low = kernel_call(
        first_kernel,
        [sds((length, width), F32), sds((length, 1), F32), sds((length, width), BF)],
        [x, after(attended, held), w_out, b_out, ln1_gain, ln1_bias], scratch=[work],
        mib=4, flops=2 * length * width * width, name="first",
    )
    if fast:
        held = jnp.concatenate([held, after(came, first_low)], 0)
        came = swapped(held, "dp", 1 << order[1])
    act, slope = kernel_call(
        inner_kernel, [sds((length, hidden), BF), sds((length, hidden), BF)],
        [after(first_low, held), w_in, b_in], scratch=[pltpu.VMEM((length, 256), F32)] * 2,
        mib=4, flops=8 * length * width * hidden, name="inner",
    )
    if fast:
        held = jnp.concatenate([held, after(came, act)], 0)
        came = swapped(held, "dp", 1 << order[2])
    n2, r2, out_hidden = kernel_call(
        second_kernel,
        [sds((length, width), F32), sds((length, 1), F32), sds((length, width), BF)],
        [after(act, held), w_back, b_back, n1, ln1_gain, ln1_bias, ln2_gain, ln2_bias], scratch=[half_work] * 2,
        mib=5, flops=2 * length * width * hidden, name="second",
    )
    if fast:
        near = jnp.concatenate([held, after(came, out_hidden)], 0)
        far = swapped(near, "dp", 1 << order[3])
        cls_grad = kernel_call(
            functools.partial(loss_kernel, order=order, count=count), sds((count, width), F32),
            [place, near, far], smem=1,
            mib=5, flops=8 * devices * count * devices * SEGS * width, name="loss",
        )
    else:
        packets = lax.all_gather(held, "dp", axis=0)
        cls_grad = plain_loss(packets, tower, me, count)

    grad_second, second_low, sums_two = kernel_call(
        second_back_kernel,
        [sds((length, width), F32), sds((length, width), BF), sds((8, width), F32)],
        [place, seg_ids, cotangent, cls_grad, n2, r2, ln2_gain], smem=1, scratch=[work],
        mib=4, flops=2 * length * width * 256, name="second_back",
    )

    def plain_grad(left, right, name):
        rows, cols = left.shape[1], right.shape[1]
        whole = kernel_call(
            plain_grad_kernel, sds((rows, cols), F32), [left, right], mib=24,
            flops=2 * length * rows * cols, name=name,
        )
        return lax.psum_scatter(whole, "dp", scatter_dimension=0, tiled=True)

    inner_call = dict(mib=3, flops=2 * length * width * hidden, name="inner_back")
    inner_shape = [sds((length, hidden), BF), sds((1, hidden), F32)]
    first_call = dict(
        scratch=[half_work] * 2, mib=5, flops=2 * length * width * (hidden + width), name="first_back"
    )
    first_shape = [
        sds((length, width), F32), sds((length, width), BF), sds((length, width), BF), sds((8, width), F32)
    ]
    def attention_back(gradient, first, pairs):
        step = (length, length)
        return kernel_call(
            functools.partial(attention_back_kernel, first=first),
            [sds((length, 6 * HEAD_DIM * pairs), BF), sds((1, 6 * HEAD_DIM * pairs), F32)],
            [proj, probs, gradient],
            scratch=[pltpu.VMEM((2,) + step, F32)] * 2 + [pltpu.VMEM((2,) + step, BF)] * 2,
            mib=9, flops=16 * pairs * length * length * 256, name=f"attention_back_{first}",
        )

    head_pairs = heads // 2
    split = 2 * head_pairs // 3

    def input_back(left, right):
        return kernel_call(
            input_back_kernel, sds((length, width), BF), [left, right, w_qkv, grad_first],
            scratch=[pltpu.VMEM((length, 3 * width), BF)],
            mib=5, flops=6 * length * width * width, name="input_back",
        )

    if fast:
        share = width // devices
        line = Sequence()

        CORE, X, Z1, Z2 = range(4)

        def grads(*pairs, name, order=(CORE, X, Z1, Z2), pieces=1, at_once=False):
            rows = pairs[0][0].shape[1]
            shape = (devices // 2, rows // devices, sum(right.shape[1] for _, right in pairs))
            args = [member for left, right in pairs for member in (left, line.now(right))]
            outs = kernel_call(
                functools.partial(weight_grad_kernel, order=order, pairs=len(pairs)),
                [sds((2,) + shape, BF)] if at_once
                else [sds(shape, BF)] + [sds((shape[0] // pieces,) + shape[1:], BF)] * pieces,
                [place] + args, smem=1, scratch=[pltpu.VMEM((rows, shape[2]), BF)],
                mib=8, flops=2 * length * rows * shape[2], name=name,
            )
            return line.chunk(outs, pieces=pieces)

        a = grads((act, second_low), name="grad_w_back", order=(CORE, Z1, Z2, X))
        line.go(a, CORE)
        inner_low, sums_in = line.ran(
            kernel_call(inner_back_kernel, inner_shape, [line.now(second_low), w_back, slope], **inner_call)
        )
        line.take(a)
        line.go(a, Z1)
        b = grads((first_low, inner_low), name="grad_w_in", pieces=4)
        line.go(b, CORE)
        grad_first, branch_low, att_grad, sums_one = line.ran(
            kernel_call(
                first_back_kernel, first_shape,
                [line.now(inner_low), w_in, grad_second, n1, r1, ln1_gain, w_out], **first_call
            )
        )
        line.take(b)
        line.go(b, X)
        grad_left, sums_left = line.ran(attention_back(line.now(att_grad), 0, split))
        c = grads((x, grad_left), (attended, branch_low), name="grad_w_qkv_1", pieces=2, at_once=True)
        grad_right, sums_right = line.ran(attention_back(line.now(att_grad), split, head_pairs - split))
        line.take(a)
        line.go(a, Z2)
        cols = 6 * HEAD_DIM * (head_pairs - split) + 128
        d = line.chunk(
            kernel_call(
                functools.partial(last_grad_kernel, order=(CORE, X, Z1, Z2)),
                [sds((2, devices // 2, share, cols), BF)],
                [place, x, line.now(grad_right), sums_two, sums_one, sums_left, sums_right, sums_in],
                smem=1, scratch=[pltpu.VMEM((width, cols), BF)], mib=5,
                flops=2 * length * width * cols, name="grad_w_qkv_2",
            ),
            extra=128,
        )
        grad_hidden = line.ran([input_back(grad_left, line.now(grad_right))])[0]
        line.go(c, X, behind=b)
        line.take(b, pieces=2)
        line.go(b, Z1)
        line.take(a)
        line.go(d, X, behind=c)
        line.take(c, pieces=2)
        line.go(c, Z1)
        line.take(b)
        line.go(b, Z2)
        line.go(a, X, behind=d)
        line.take(d)
        line.go(d, Z1)
        line.take(c)
        line.go(c, Z2)
        share_w_in = line.finish(b)
        line.take(d)
        line.go(d, Z2)
        share_w_back = line.finish(a)
        (
            share_w_qkv, share_w_out, share_bq, share_bv, share_gain2, share_bias2, share_b_back,
            share_gain1, share_bias1, share_b_out, share_b_in,
        ) = kernel_call(
            finish_last_kernel,
            [sds((share, 3 * width), F32), sds((share, width), F32)] + [sds((1, share), F32)] * 8
            + [sds((1, hidden // devices), F32)],
            [c["keep"], line.now(c["came"][0]), d["keep"], d["came"][0]], mib=4, name="finish_last",
        )
    else:
        share_w_back = plain_grad(act, second_low, "grad_w_back")
        inner_low, sums_in = kernel_call(
            inner_back_kernel, inner_shape, [second_low, w_back, slope], **inner_call
        )
        share_w_in = plain_grad(first_low, inner_low, "grad_w_in")
        grad_first, branch_low, att_grad, sums_one = kernel_call(
            first_back_kernel, first_shape, [inner_low, w_in, grad_second, n1, r1, ln1_gain, w_out],
            **first_call
        )
        grad_left, sums_left = attention_back(att_grad, 0, split)
        grad_right, sums_right = attention_back(att_grad, split, head_pairs - split)
        grad_hidden = input_back(grad_left, grad_right)

        def joined(left, right):
            pieces = [jnp.split(half, 3, 1) for half in (left, right)]
            return jnp.concatenate([piece for both in zip(*pieces) for piece in both], 1)

        grad_proj, sums_qkv = joined(grad_left, grad_right), joined(sums_left, sums_right)
        share_w_qkv = plain_grad(x, grad_proj, "grad_w_qkv")
        share_w_out = plain_grad(attended, branch_low, "grad_w_out")

        def scattered(vector):
            return lax.psum_scatter(vector, "dp", scatter_dimension=1, tiled=True)

        share_bq, share_bv = scattered(sums_qkv[:, :width]), scattered(sums_qkv[:, 2 * width :])
        share_gain2, share_bias2, share_b_back = (scattered(sums_two[k : k + 1]) for k in range(3))
        share_gain1, share_bias1, share_b_out = (scattered(sums_one[k : k + 1]) for k in range(3))
        share_b_in = scattered(sums_in)
    return (
        out_hidden[None],
        grad_hidden[None],
        share_w_qkv[None],
        share_bq,
        share_bv,
        share_w_out[None],
        share_b_out,
        share_gain1,
        share_bias1,
        share_w_in[None],
        share_b_in,
        share_w_back[None],
        share_b_back,
        share_gain2,
        share_bias2,
    )


def solution(mesh):
    matrix, vector = P("tower", None, None), P("tower", None)
    rows, spread = P("tower", "dp", None), P("tower", "dp")
    return jax.shard_map(
        shards,
        mesh=mesh,
        in_specs=(
            rows, P("dp", None), P("dp"), rows, matrix, vector, vector, matrix, vector, vector, vector,
            matrix, vector, matrix, vector, vector, vector,
        ),
        out_specs=(
            rows, rows, rows, spread, spread, rows, spread, spread, spread, rows, spread, rows, spread,
            spread, spread,
        ),
        check_vma=False,
    )
```

```python
import functools
import math

import jax
import jax.numpy as jnp
from jax import lax
from jax.experimental import pallas as pl
from jax.experimental.pallas import tpu as pltpu
from jax.sharding import PartitionSpec as P

HEAD_DIM = 64
QLEN = 32
SEGS = 4
PACKET = 24
EPS = 1e-05
BF = jnp.bfloat16
F32 = jnp.float32
TILE = 32

COSTS = {"first_back": 3 * 10**10, "attention_back_4": 3 * 10**10, "input_back": 3 * 10**10}

VM = pl.BlockSpec(memory_space=pltpu.VMEM)
SM = pl.BlockSpec(memory_space=pltpu.SMEM)
HB = pl.BlockSpec(memory_space=pltpu.HBM)


def nn(a, b):
    return lax.dot_general(a, b, (((1,), (0,)), ((), ())), preferred_element_type=F32)


def nt(a, b):
    return lax.dot_general(a, b, (((1,), (1,)), ((), ())), preferred_element_type=F32)


def tn(a, b):
    return lax.dot_general(a, b, (((0,), (0,)), ((), ())), preferred_element_type=F32)


def kernel_call(body, outs, args, scratch=(), smem=0, hbm=0, mib=32, flops=0, name=None):
    single = not isinstance(outs, (list, tuple))
    shapes = [outs] if single else list(outs)
    result = pl.pallas_call(
        body,
        out_shape=shapes,
        in_specs=[SM] * smem + [VM] * (len(args) - smem - hbm) + [HB] * hbm,
        out_specs=[VM] * len(shapes),
        scratch_shapes=list(scratch),
        compiler_params=pltpu.CompilerParams(vmem_limit_bytes=mib << 20),
        cost_estimate=pl.CostEstimate(flops=COSTS.get(name, 0), bytes_accessed=0, transcendentals=0),
        name=name,
    )(*args)
    return result[0] if single else result


def sds(shape, dtype):
    return jax.ShapeDtypeStruct(shape, dtype)


def fold(value):
    rows, cols = value.shape
    return jnp.sum(value.reshape(rows // 8, 8, cols), 0)


def head_mask(half):
    lane = lax.broadcasted_iota(jnp.int32, (1, 2 * HEAD_DIM), 1)
    return (lane // HEAD_DIM == half).astype(F32).astype(BF)


def normalise(value):
    centred = value - jnp.mean(value, -1, keepdims=True)
    inverse = lax.rsqrt(jnp.mean(centred * centred, -1, keepdims=True) + EPS)
    return centred * inverse, inverse


def norm_back(grad, normed, inverse, gain):
    scaled = grad * gain
    return inverse * (
        scaled
        - jnp.mean(scaled, -1, keepdims=True)
        - normed * jnp.mean(scaled * normed, -1, keepdims=True)
    )


def gelu_pair(value):
    cdf = 0.5 * lax.erf(value * (1.0 / math.sqrt(2.0))) + 0.5
    density = jnp.exp(value * value * -0.5) * (1.0 / math.sqrt(2.0 * math.pi))
    return value * cdf, cdf + value * density


def proj_kernel(x_hbm, w_hbm, bq_hbm, bv_hbm, out, x, w0, w1, w2, bq, bv, sems):
    width = x.shape[1]
    parts = (w0, w1, w2)
    copies = [
        pltpu.make_async_copy(w_hbm.at[:, pl.ds(k * width, width)], parts[k], sems.at[k]) for k in range(3)
    ]
    x_copy = pltpu.make_async_copy(x_hbm, x, sems.at[3])
    bq_copy = pltpu.make_async_copy(bq_hbm, bq, sems.at[4])
    bv_copy = pltpu.make_async_copy(bv_hbm, bv, sems.at[5])
    for copy in (x_copy, copies[1], copies[0], bq_copy, copies[2], bv_copy):
        copy.start()
    x_copy.wait()
    for k in (1, 0, 2):
        copies[k].wait()
        value = nn(x[...], parts[k][...])
        if k == 0:
            bq_copy.wait()
            value = value + bq[...]
        if k == 2:
            bv_copy.wait()
            value = value + bv[...]
        out[:, k * width : (k + 1) * width] = value.astype(BF)


def chosen_rows(tower, seg, count, length):
    row = lax.broadcasted_iota(jnp.int32, (count, 1), 0)
    place = lax.broadcasted_iota(jnp.int32, (count, length), 1)
    start = jnp.sum((seg < row).astype(F32), 1, keepdims=True).astype(jnp.int32)
    wanted = jnp.where(tower == 0, row * QLEN, jnp.where(row < SEGS, start, -1))
    return (place == wanted).astype(F32)


def cls_kernel(place, seg, x, proj, w_out, b_out, g1, b1, w_in, b_in, w_back, b_back, g2, b2, cls):
    length, width = x.shape
    count = cls.shape[0]
    heads = width // HEAD_DIM
    tower = place[0]
    pick = chosen_rows(tower, seg[...], count, length)
    pick_low = pick.astype(BF)
    x_cls = nn(pick_low, x[...])
    q_cls = (nn(pick_low, proj[:, :width]) * (1.0 / math.sqrt(HEAD_DIM))).astype(BF)
    place_row = lax.broadcasted_iota(jnp.int32, (1, length), 1)
    own_seg = jnp.where(tower == 0, place_row // QLEN, seg[...])
    row = lax.broadcasted_iota(jnp.int32, (count, 1), 0)
    bias = jnp.where(own_seg == row, 0.0, -1e9)
    lane_head = lax.broadcasted_iota(jnp.int32, (1, width), 1) // HEAD_DIM
    spread = jnp.concatenate(
        [q_cls * (lane_head == h).astype(F32).astype(BF) for h in range(heads)], 0
    )
    scores = nt(spread, proj[:, width : 2 * width]) + jnp.concatenate([bias] * heads, 0)
    shifted = jnp.exp(scores - jnp.max(scores, -1, keepdims=True))
    probs = (shifted / jnp.sum(shifted, -1, keepdims=True)).astype(BF)
    mixed = nn(probs, proj[:, 2 * width :])
    attended = jnp.zeros((count, width), F32)
    for h in range(heads):
        attended = attended + jnp.where(lane_head == h, mixed[h * count : (h + 1) * count], 0.0)
    first = x_cls + (nn(attended.astype(BF), w_out[...]) + b_out[...])
    normed = normalise(first)[0] * g1[...] + b1[...]
    inner = nn(normed.astype(BF), w_in[...]) + b_in[...]
    act = gelu_pair(inner)[0].astype(BF)
    second = normed + (nn(act, w_back[...]) + b_back[...])
    final = normalise(second)[0] * g2[...] + b2[...]
    cls[...] = final.astype(BF)


def attention_kernel(place, seg_row, seg_col, proj, attended, probs, bias, *work):
    length = proj.shape[0]
    width = proj.shape[1] // 3
    tower = place[0]
    lane = lax.broadcasted_iota(jnp.int32, (1, length), 1)
    sub = lax.broadcasted_iota(jnp.int32, (length, 1), 0)
    row_seg = jnp.where(tower == 0, lane // QLEN, seg_row[...])
    col_seg = jnp.where(tower == 0, sub // QLEN, seg_col[...])
    bias[...] = jnp.where(col_seg == row_seg, 0.0, -1e9)
    masks = [head_mask(0), head_mask(1)]
    scale = jnp.asarray(1.0 / math.sqrt(HEAD_DIM), BF)
    step = 2 * HEAD_DIM
    pairs = width // step

    def columns(part, pair):
        return proj[:, part * width + pair * step : part * width + (pair + 1) * step]

    def scores(pair):
        queries, keys = columns(0, pair) * scale, columns(1, pair)
        for half in range(2):
            work[pair % 2][half] = nt(queries * masks[half], keys)

    def soften(pair):
        for half in range(2):
            for r in range(0, length, TILE):
                value = work[pair % 2][half, r : r + TILE, :] + bias[r : r + TILE, :]
                shifted = jnp.exp(value - jnp.max(value, -1, keepdims=True))
                total = jnp.sum(shifted, -1, keepdims=True)
                probs[2 * pair + half, r : r + TILE, :] = (shifted * (1.0 / total)).astype(BF)

    def mix(pair):
        values = columns(2, pair)
        mixed = nn(probs[2 * pair], values * masks[0]) + nn(probs[2 * pair + 1], values * masks[1])
        attended[:, pair * step : (pair + 1) * step] = mixed.astype(BF)

    scores(0)
    for pair in range(pairs):
        if pair + 1 < pairs:
            scores(pair + 1)
        if pair > 0:
            mix(pair - 1)
        soften(pair)
    mix(pairs - 1)


def first_kernel(x, attended, w_out, b_out, g1, b1, n1, r1, low, work):
    work[...] = nn(attended[...], w_out[...])
    for r in range(0, x.shape[0], TILE):
        rows = slice(r, r + TILE)
        first = x[rows, :].astype(F32) + (work[rows, :] + b_out[...])
        normed, inverse = normalise(first)
        n1[rows, :] = normed
        r1[rows, :] = inverse
        low[rows, :] = (normed * g1[...] + b1[...]).astype(BF)


def inner_kernel(low, w_in, b_in, act, slope, work_a, work_b):
    length = low.shape[0]
    block = work_a.shape[1]
    blocks = w_in.shape[1] // block

    def columns(i):
        return pl.ds(pl.multiple_of(i * block, block), block)

    def gelu_block(i, work):
        bias = b_in[:, columns(i)]
        for r in range(0, length, TILE):
            value, grad = gelu_pair(work[r : r + TILE, :] + bias)
            act[r : r + TILE, columns(i)] = value.astype(BF)
            slope[r : r + TILE, columns(i)] = grad.astype(BF)

    work_a[...] = nn(low[...], w_in[:, :block])

    def step(k, carry):
        i = 2 * k
        work_b[...] = nn(low[...], w_in[:, columns(i + 1)])
        gelu_block(i, work_a)
        work_a[...] = nn(low[...], w_in[:, columns(jnp.minimum(i + 2, blocks - 1))])
        gelu_block(i + 1, work_b)
        return carry

    lax.fori_loop(0, blocks // 2, step, 0)


def second_kernel(act, w_back, b_back, n1, g1, b1, g2, b2, n2, r2, out, work_a, work_b):
    length = act.shape[0]
    part = length // 2
    works = (work_a, work_b)

    def normalise_part(k):
        for r in range(0, part, TILE):
            rows = slice(k * part + r, k * part + r + TILE)
            branch = works[k][r : r + TILE, :] + b_back[...]
            second = (n1[rows, :] * g1[...] + b1[...]) + branch
            normed, inverse = normalise(second)
            n2[rows, :] = normed
            r2[rows, :] = inverse
            out[rows, :] = (normed * g2[...] + b2[...]).astype(BF)

    work_a[...] = nn(act[:part, :], w_back[...])
    work_b[...] = nn(act[part:, :], w_back[...])
    normalise_part(0)
    normalise_part(1)


def packet_kernel(place, cls, other, labels, out):
    query = place[0] == 0
    count, width = cls.shape
    mine, came = cls[...].astype(F32), other[...].astype(F32)
    q_rows = jnp.where(query, mine, came)
    p_rows = jnp.where(query, came, mine)[:SEGS]
    value = labels[...]
    gap = jnp.zeros((1, 128 - count), F32)
    row = jnp.concatenate(
        [(value >> 8).astype(F32), gap, (value & 255).astype(F32), gap, jnp.zeros((1, width - 256), F32)], 1
    )
    rest = jnp.zeros((PACKET - count - SEGS - 1, width), F32)
    out[...] = jnp.concatenate([q_rows, p_rows, row, rest], 0).astype(BF)


def loss_kernel(place, near, far, grad, *, order, count):
    tower, me = place[0], place[1]
    packets = jnp.concatenate([near[...], far[...]], 0)
    total, width = packets.shape
    scale = 2.0 / math.sqrt(width)
    row = lax.broadcasted_iota(jnp.int32, (total, 1), 0)
    col = lax.broadcasted_iota(jnp.int32, (1, total), 1)
    col_slot, col_part = col // PACKET, col % PACKET
    mixed = jnp.zeros_like(col)
    for j, b in enumerate(order):
        mixed = mixed | (((col_slot >> j) & 1) << b)
    is_passage = jnp.logical_and(col_part >= count, col_part < count + SEGS)
    number = jnp.where(is_passage, (mixed ^ me) * SEGS + (col_part - count), -1)
    label_of = ((row // PACKET) * PACKET + (count + SEGS) == col).astype(F32).astype(BF)
    label_rows = nn(label_of, packets[:, :256])
    lane = lax.broadcasted_iota(jnp.int32, (1, 256), 1)
    part = row % PACKET
    weight = jnp.where(lane == part, 256.0, 0.0) + jnp.where(lane == part + 128, 1.0, 0.0)
    label = jnp.sum(label_rows * weight, 1, keepdims=True).astype(jnp.int32)
    logits = jnp.where(is_passage, nt(packets, packets) * scale, -1e30)
    soft = jnp.exp(logits - jnp.max(logits, -1, keepdims=True))
    soft = soft / jnp.sum(soft, -1, keepdims=True)
    grad_logits = soft - (number == label).astype(F32)
    grad_logits = grad_logits * (part < count).astype(F32)
    wide = packets.astype(F32)
    grad_q = jnp.dot(
        grad_logits[:count], wide, precision=lax.Precision.HIGHEST, preferred_element_type=F32
    )
    pick = lax.broadcasted_iota(jnp.int32, (count, 1), 0)
    pick = jnp.logical_and(pick + count == col, pick < SEGS).astype(F32)
    turned = lax.dot_general(
        pick, grad_logits, (((1,), (1,)), ((), ())),
        precision=lax.Precision.HIGHEST, preferred_element_type=F32,
    )
    grad_p = jnp.dot(turned, wide, precision=lax.Precision.HIGHEST, preferred_element_type=F32)
    grad[...] = jnp.where(tower == 0, grad_q, grad_p) * scale


def plain_loss(packets, tower, me, count):
    devices, _, width = packets.shape
    scale = 2.0 / math.sqrt(width)
    queries = packets[:, :count].reshape(devices * count, width)
    passages = packets[:, count : count + SEGS].reshape(devices * SEGS, width)
    row = packets[:, count + SEGS].astype(jnp.int32)
    label = (row[:, :count] * 256 + row[:, 128 : 128 + count]).reshape(devices * count, 1)
    soft = jax.nn.softmax(nt(queries, passages) * scale, -1)
    grad = soft - (label == jnp.arange(devices * SEGS, dtype=jnp.int32)).astype(F32)
    grad_q = lax.dynamic_slice_in_dim(grad, me * count, count, 0)
    grad_q = jnp.dot(grad_q, passages.astype(F32), precision=lax.Precision.HIGHEST)
    grad_p = lax.dynamic_slice_in_dim(grad, me * SEGS, SEGS, 1)
    grad_p = jnp.dot(grad_p.T, queries.astype(F32), precision=lax.Precision.HIGHEST)
    grad_p = jnp.pad(grad_p, ((0, count - SEGS), (0, 0)))
    return jnp.where(tower == 0, grad_q, grad_p) * scale


def split_three(value):
    high = value.astype(BF)
    rest = value - high.astype(F32)
    middle = rest.astype(BF)
    return jnp.concatenate([high, middle, (rest - middle.astype(F32)).astype(BF)], 0)


def norm_back_rows(rows, grad, normed, inverse, gain, out, low, totals):
    back = norm_back(grad, normed[rows, :], inverse[rows, :], gain[...])
    out[rows, :] = back
    back_low = back.astype(BF)
    low[rows, :] = back_low
    parts = (fold(grad * normed[rows, :]), fold(grad), fold(back_low.astype(F32)))
    return parts if totals is None else tuple(a + b for a, b in zip(totals, parts))


def second_back_kernel(place, seg, out_grad, cls_grad, n2, r2, g2, grad, low, sums, work):
    length, width = out_grad.shape
    count = cls_grad.shape[0]
    pick = chosen_rows(place[0], seg[...], count, length).astype(BF)
    work[...] = tn(jnp.concatenate([pick] * 3, 0), split_three(cls_grad[...]))
    totals = None
    for r in range(0, length, TILE):
        rows = slice(r, r + TILE)
        final = out_grad[rows, :].astype(F32) + work[rows, :]
        totals = norm_back_rows(rows, final, n2, r2, g2, grad, low, totals)
    for k, part in enumerate(totals):
        sums[k : k + 1, :] = jnp.sum(part, 0, keepdims=True)


def inner_back_kernel(low, w_back, slope, out, sums):
    block = 256
    for i in range(w_back.shape[0] // block):
        cols = slice(i * block, (i + 1) * block)
        value = (nt(low[...], w_back[cols, :]) * slope[:, cols].astype(F32)).astype(BF)
        out[:, cols] = value
        sums[:, cols] = jnp.sum(value.astype(F32), 0, keepdims=True)


def first_back_kernel(inner, w_in, grad_second, n1, r1, g1, w_out, grad, low, att, sums, work_a, work_b):
    length, width = grad_second.shape
    part = length // 2
    works = (work_a, work_b)
    for k in range(2):
        works[k][...] = nt(inner[k * part : (k + 1) * part, :], w_in[...])
    totals = None
    for k in range(2):
        for r in range(0, part, TILE):
            rows = slice(k * part + r, k * part + r + TILE)
            value = grad_second[rows, :] + works[k][r : r + TILE, :]
            totals = norm_back_rows(rows, value, n1, r1, g1, grad, low, totals)
        rows = slice(k * part, (k + 1) * part)
        att[rows, :] = nt(low[rows, :], w_out[...]).astype(BF)
    for k, total in enumerate(totals):
        sums[k : k + 1, :] = jnp.sum(total, 0, keepdims=True)


def attention_back_kernel(proj, probs, att_grad, out, sums, dp_a, dp_b, ds_a, ds_b, *, first):
    length = proj.shape[0]
    width = proj.shape[1] // 3
    own = out.shape[1] // 3
    masks = [head_mask(0), head_mask(1)]
    scale = 1.0 / math.sqrt(HEAD_DIM)
    step = 2 * HEAD_DIM
    pairs = own // step
    dp, ds = (dp_a, dp_b), (ds_a, ds_b)

    def columns(part, pair):
        at = part * width + (first + pair) * step
        return proj[:, at : at + step]

    def grad_columns(pair):
        at = (first + pair) * step
        return att_grad[:, at : at + step]

    def grad_probs(pair):
        grads, values = grad_columns(pair), columns(2, pair)
        for half in range(2):
            dp[pair % 2][half] = nt(grads * masks[half], values)

    def grad_scores(pair):
        for half in range(2):
            for r in range(0, length, TILE):
                wide = probs[2 * (first + pair) + half, r : r + TILE, :].astype(F32)
                grad = dp[pair % 2][half, r : r + TILE, :]
                delta = jnp.sum(grad * wide, -1, keepdims=True)
                ds[pair % 2][half, r : r + TILE, :] = (wide * (grad - delta)).astype(BF)

    def results(pair):
        queries_t, grads_t = columns(0, pair).T, grad_columns(pair).T
        keys = columns(1, pair)
        grad_q, grad_k_t, grad_v_t = None, [], []
        for half in range(2):
            scores = ds[pair % 2][half]
            lanes = slice(half * HEAD_DIM, (half + 1) * HEAD_DIM)
            grad_v_t.append(nn(grads_t[lanes], probs[2 * (first + pair) + half]))
            grad_k_t.append(nn(queries_t[lanes], scores))
            term = nn(scores, keys * masks[half])
            grad_q = term if grad_q is None else grad_q + term
        parts = (
            grad_q * scale,
            jnp.concatenate(grad_k_t, 0).T * scale,
            jnp.concatenate(grad_v_t, 0).T,
        )
        for k, part in enumerate(parts):
            cols = slice(k * own + pair * step, k * own + (pair + 1) * step)
            part_low = part.astype(BF)
            out[:, cols] = part_low
            sums[:, cols] = jnp.sum(part_low.astype(F32), 0, keepdims=True)

    grad_probs(0)
    for pair in range(pairs):
        if pair + 1 < pairs:
            grad_probs(pair + 1)
        if pair > 0:
            results(pair - 1)
        grad_scores(pair)
    results(pairs - 1)


def input_back_kernel(left, right, w_qkv, grad_first, out, work):
    width = out.shape[1]
    for k in range(3):
        at = k * width
        for part in (left, right):
            own = part.shape[1] // 3
            work[:, at : at + own] = part[:, k * own : (k + 1) * own]
            at += own
    block = 256
    for i in range(width // block):
        cols = slice(i * block, (i + 1) * block)
        value = grad_first[:, cols] + nt(work[...], w_qkv[cols, :])
        out[:, cols] = value.astype(BF)


def slot_device(me, order, slot):
    mixed = 0
    for j, b in enumerate(order):
        mixed = mixed | (((slot >> (len(order) - 1 - j)) & 1) << b)
    return me ^ mixed


def spread_shares(place, work, outs, order):
    me = place[1]
    if len(outs) == 1:
        outs = (outs[0].at[0], outs[0].at[1])
        me = me & ~(1 << order[0])
    keep, *sends = outs
    half, share, _ = keep.shape
    for slot in range(2 * half):
        ref, at = (keep, slot) if slot < half else piece_of(sends, slot - half)
        device = slot_device(me, order, slot)
        ref[at] = work[pl.ds(pl.multiple_of(device * share, 16), share), :]


def piece_of(refs, slot):
    size = refs[0].shape[0]
    return refs[slot // size], slot % size


def weight_grad_kernel(place, *refs, order, pairs):
    *outs, work = refs[2 * pairs :]
    at = 0
    for left, right in zip(refs[: 2 * pairs : 2], refs[1 : 2 * pairs : 2]):
        cols = slice(at, at + right.shape[1])
        block = min(left.shape[1], 768)
        for r in range(0, left.shape[1], block):
            work[r : r + block, cols] = tn(left[:, r : r + block], right[...]).astype(BF)
        at += right.shape[1]
    spread_shares(place, work, outs, order)


def last_grad_kernel(
    place, x, grad_proj, sums_two, sums_one, sums_left, sums_right, sums_in, *refs, order
):
    *outs, work = refs
    width = x.shape[1]
    share = outs[0].shape[1]
    devices = 2 * outs[0].shape[0]
    wide = grad_proj.shape[1]
    work[:, :wide] = tn(x[...], grad_proj[...]).astype(BF)
    extra = slice(wide, wide + 128)
    thirds = [sums.shape[1] // 3 for sums in (sums_left, sums_right)]
    query, value = (
        jnp.concatenate(
            [sums[:, k * own : (k + 1) * own] for sums, own in zip((sums_left, sums_right), thirds)], 1
        )
        for k in (0, 2)
    )
    stacked = jnp.concatenate([query, value, sums_two[0:3], sums_one[0:3]], 0)
    work[:, extra] = jnp.zeros((width, 128), BF)
    in_share = sums_in.shape[1] // devices
    for d in range(devices):
        rows = [stacked[:, d * share : (d + 1) * share]]
        for k in range(in_share // share):
            at = d * in_share + k * share
            rows.append(sums_in[:, at : at + share])
        rows.append(jnp.zeros((16 - 8 - in_share // share, share), F32))
        block = jnp.concatenate(rows, 0)
        block = jnp.concatenate([block, jnp.zeros((16, 128 - share), F32)], 1)
        high = block.astype(BF)
        work[d * share : d * share + 16, extra] = high
        work[d * share + 16 : d * share + 32, extra] = (block - high.astype(F32)).astype(BF)
    spread_shares(place, work, outs, order)


def add_extra(left, right):
    total = (
        left[0:16].astype(F32) + left[16:32].astype(F32) + right[0:16].astype(F32) + right[16:32].astype(F32)
    )
    return total


def halve_kernel(*refs, cames, extra):
    kept, came, (keep, *sends) = refs[0], refs[1 : 1 + cames], refs[1 + cames :]
    half = keep.shape[0]
    cols = keep.shape[2] - extra
    for slot in range(2 * half):
        ref, at = (keep, slot) if slot < half else piece_of(sends, slot - half)
        other, there = piece_of(came, slot)
        ref[at, :, :cols] = (kept[slot, :, :cols].astype(F32) + other[there, :, :cols].astype(F32)).astype(BF)
        if extra:
            total = add_extra(kept[slot, :, cols:], other[there, :, cols:])
            high = total.astype(BF)
            ref[at, 0:16, cols:] = high
            ref[at, 16:32, cols:] = (total - high.astype(F32)).astype(BF)
            ref[at, 32:, cols:] = jnp.zeros((keep.shape[1] - 32, extra), BF)


def halve_cores_kernel(both, *outs, extra):
    halve_kernel(both.at[0], both.at[1], *outs, cames=1, extra=extra)


def finish_kernel(kept, came, out):
    out[...] = kept[0].astype(F32) + came[0].astype(F32)


def finish_last_kernel(
    kept, came, kept_last, came_last, w_qkv, w_out, bq, bv, gain2, bias2, b_back, gain1, bias1, b_out, b_in
):
    width = w_out.shape[1]
    share = bq.shape[1]
    left, right = (kept.shape[2] - width) // 3, (kept_last.shape[2] - 128) // 3
    for k in range(3):
        at = k * width
        cols = slice(k * left, (k + 1) * left)
        w_qkv[:, at : at + left] = kept[0, :, cols].astype(F32) + came[0, :, cols].astype(F32)
        cols = slice(k * right, (k + 1) * right)
        w_qkv[:, at + left : at + width] = kept_last[0, :, cols].astype(F32) + came_last[0, :, cols].astype(F32)
    w_out[...] = kept[0, :, 3 * left :].astype(F32) + came[0, :, 3 * left :].astype(F32)
    vectors = add_extra(kept_last[0, :, 3 * right :], came_last[0, :, 3 * right :])
    for k, ref in enumerate((bq, bv, gain2, bias2, b_back, gain1, bias1, b_out)):
        ref[...] = vectors[k : k + 1, :share]
    pieces = b_in.shape[1] // share
    b_in[...] = jnp.concatenate([vectors[8 + k : 9 + k, :share] for k in range(pieces)], 1)


def plain_grad_kernel(left, right, out):
    out[...] = tn(left[...], right[...])


def swapped(value, axis, mask):
    count = lax.axis_size(axis)
    return lax.ppermute(value, axis, [(i, i ^ mask) for i in range(count)])


class Sequence:
    def __init__(self):
        self.last = None

    def now(self, value):
        return value if self.last is None else after(value, self.last)

    def ran(self, results):
        self.last = results[0]
        return results

    def chunk(self, outs, extra=0, pieces=1):
        chunk = {"extra": extra}
        if len(outs) > 1:
            chunk["keep"], *chunk["sends"] = self.ran(outs)
        else:
            pairs = [[i, i + 1] for i in range(0, lax.axis_size("dp"), 2)]
            both = lax.all_to_all(outs[0], "dp", 0, 0, tiled=True, axis_index_groups=pairs)
            self.last = both
            self.parted(chunk, functools.partial(halve_cores_kernel, extra=extra), [both], both.shape[1:], pieces)
        return chunk

    def parted(self, chunk, body, args, shape, pieces):
        half = sds((shape[0] // 2,) + shape[1:], BF)
        piece = sds((shape[0] // 2 // pieces,) + shape[1:], BF)
        chunk["keep"], *chunk["sends"] = self.ran(
            kernel_call(body, [half] + [piece] * pieces, args, mib=4, name="halve")
        )

    def go(self, chunk, bit, behind=None):
        sends = [self.now(send) for send in chunk["sends"]]
        if behind is not None:
            sends = [after(send, *behind["came"]) for send in sends]
        chunk["came"] = [swapped(send, "dp", 1 << bit) for send in sends]

    def take(self, chunk, pieces=1):
        keep, came = chunk["keep"], [self.now(value) for value in chunk["came"]]
        body = functools.partial(halve_kernel, cames=len(came), extra=chunk["extra"])
        self.parted(chunk, body, [keep] + came, keep.shape, pieces)

    def finish(self, chunk):
        args = [chunk["keep"], self.now(chunk["came"][0])]
        return self.ran([kernel_call(finish_kernel, sds(args[0].shape[1:], F32), args, mib=4, name="finish")])[0]


def after(value, *earlier):
    return lax.optimization_barrier((value,) + earlier)[0]


def shards(
    hidden_in,
    seg_ids,
    labels,
    out_grad,
    w_qkv,
    b_query,
    b_value,
    w_out,
    b_out,
    ln1_gain,
    ln1_bias,
    w_in,
    b_in,
    w_back,
    b_back,
    ln2_gain,
    ln2_bias,
):
    x, cotangent = hidden_in[0], out_grad[0]
    w_qkv, w_out, w_in, w_back = w_qkv[0], w_out[0], w_in[0], w_back[0]
    length, width = x.shape
    hidden = w_in.shape[1]
    heads = width // HEAD_DIM
    count = length // QLEN
    devices = lax.axis_size("dp")
    bits = devices.bit_length() - 1
    tower, me = lax.axis_index("tower"), lax.axis_index("dp")
    place = jnp.stack([tower, me]).astype(jnp.int32)
    seg_col = seg_ids.reshape(length, 1)
    fast = devices == 16

    proj = kernel_call(
        proj_kernel, sds((length, 3 * width), BF),
        [pltpu.with_memory_space_constraint(member, pltpu.HBM) for member in (x, w_qkv, b_query, b_value)], hbm=4,
        scratch=[pltpu.VMEM((length, width), BF)] + [pltpu.VMEM((width, width), BF)] * 3
        + [pltpu.VMEM((1, width), F32)] * 2 + [pltpu.SemaphoreType.DMA((6,))],
        mib=8, flops=2 * length * 3 * width * width, name="proj",
    )
    cls = kernel_call(
        cls_kernel, sds((count, width), BF),
        [place, seg_ids, x, proj, w_out, b_out, ln1_gain, ln1_bias, w_in, b_in, w_back, b_back,
         ln2_gain, ln2_bias],
        smem=1, mib=3, flops=2 * 256 * width * hidden * 2, name="cls",
    )
    other = swapped(cls, "tower", 1)
    attended, probs = kernel_call(
        attention_kernel, [sds((length, width), BF), sds((heads, length, length), BF)],
        [place, seg_ids, seg_col, after(proj, cls)], smem=1,
        scratch=[pltpu.VMEM((length, length), F32)] + [pltpu.VMEM((2, length, length), F32)] * 2,
        mib=9, flops=4 * heads * length * length * 256, name="attention",
    )
    held = kernel_call(
        packet_kernel, sds((PACKET, width), BF), [place, cls, after(other, attended), labels[None]],
        smem=1, mib=1, name="packet",
    )
    order = [3, 2, 1, 0] if fast else list(range(bits))
    if fast:
        came = swapped(held, "dp", 1 << order[0])
    work, half_work = pltpu.VMEM((length, width), F32), pltpu.VMEM((length // 2, width), F32)
    n1, r1, first_low = kernel_call(
        first_kernel,
        [sds((length, width), F32), sds((length, 1), F32), sds((length, width), BF)],
        [x, after(attended, held), w_out, b_out, ln1_gain, ln1_bias], scratch=[work],
        mib=4, flops=2 * length * width * width, name="first",
    )
    if fast:
        held = jnp.concatenate([held, after(came, first_low)], 0)
        came = swapped(held, "dp", 1 << order[1])
    act, slope = kernel_call(
        inner_kernel, [sds((length, hidden), BF), sds((length, hidden), BF)],
        [after(first_low, held), w_in, b_in], scratch=[pltpu.VMEM((length, 256), F32)] * 2,
        mib=4, flops=8 * length * width * hidden, name="inner",
    )
    if fast:
        held = jnp.concatenate([held, after(came, act)], 0)
        came = swapped(held, "dp", 1 << order[2])
    n2, r2, out_hidden = kernel_call(
        second_kernel,
        [sds((length, width), F32), sds((length, 1), F32), sds((length, width), BF)],
        [after(act, held), w_back, b_back, n1, ln1_gain, ln1_bias, ln2_gain, ln2_bias], scratch=[half_work] * 2,
        mib=5, flops=2 * length * width * hidden, name="second",
    )
    if fast:
        near = jnp.concatenate([held, after(came, out_hidden)], 0)
        far = swapped(near, "dp", 1 << order[3])
        cls_grad = kernel_call(
            functools.partial(loss_kernel, order=order, count=count), sds((count, width), F32),
            [place, near, far], smem=1,
            mib=5, flops=8 * devices * count * devices * SEGS * width, name="loss",
        )
    else:
        packets = lax.all_gather(held, "dp", axis=0)
        cls_grad = plain_loss(packets, tower, me, count)

    grad_second, second_low, sums_two = kernel_call(
        second_back_kernel,
        [sds((length, width), F32), sds((length, width), BF), sds((8, width), F32)],
        [place, seg_ids, cotangent, cls_grad, n2, r2, ln2_gain], smem=1, scratch=[work],
        mib=4, flops=2 * length * width * 256, name="second_back",
    )

    def plain_grad(left, right, name):
        rows, cols = left.shape[1], right.shape[1]
        whole = kernel_call(
            plain_grad_kernel, sds((rows, cols), F32), [left, right], mib=24,
            flops=2 * length * rows * cols, name=name,
        )
        return lax.psum_scatter(whole, "dp", scatter_dimension=0, tiled=True)

    inner_call = dict(mib=3, flops=2 * length * width * hidden, name="inner_back")
    inner_shape = [sds((length, hidden), BF), sds((1, hidden), F32)]
    first_call = dict(
        scratch=[half_work] * 2, mib=5, flops=2 * length * width * (hidden + width), name="first_back"
    )
    first_shape = [
        sds((length, width), F32), sds((length, width), BF), sds((length, width), BF), sds((8, width), F32)
    ]
    def attention_back(gradient, first, pairs):
        step = (length, length)
        return kernel_call(
            functools.partial(attention_back_kernel, first=first),
            [sds((length, 6 * HEAD_DIM * pairs), BF), sds((1, 6 * HEAD_DIM * pairs), F32)],
            [proj, probs, gradient],
            scratch=[pltpu.VMEM((2,) + step, F32)] * 2 + [pltpu.VMEM((2,) + step, BF)] * 2,
            mib=9, flops=16 * pairs * length * length * 256, name=f"attention_back_{first}",
        )

    head_pairs = heads // 2
    split = 2 * head_pairs // 3

    def input_back(left, right):
        return kernel_call(
            input_back_kernel, sds((length, width), BF), [left, right, w_qkv, grad_first],
            scratch=[pltpu.VMEM((length, 3 * width), BF)],
            mib=5, flops=6 * length * width * width, name="input_back",
        )

    if fast:
        share = width // devices
        line = Sequence()

        CORE, X, Z1, Z2 = range(4)

        def grads(*pairs, name, order=(CORE, X, Z1, Z2), pieces=1, at_once=False):
            rows = pairs[0][0].shape[1]
            shape = (devices // 2, rows // devices, sum(right.shape[1] for _, right in pairs))
            args = [member for left, right in pairs for member in (left, line.now(right))]
            outs = kernel_call(
                functools.partial(weight_grad_kernel, order=order, pairs=len(pairs)),
                [sds((2,) + shape, BF)] if at_once
                else [sds(shape, BF)] + [sds((shape[0] // pieces,) + shape[1:], BF)] * pieces,
                [place] + args, smem=1, scratch=[pltpu.VMEM((rows, shape[2]), BF)],
                mib=8, flops=2 * length * rows * shape[2], name=name,
            )
            return line.chunk(outs, pieces=pieces)

        a = grads((act, second_low), name="grad_w_back", order=(CORE, Z1, Z2, X))
        line.go(a, CORE)
        inner_low, sums_in = line.ran(
            kernel_call(inner_back_kernel, inner_shape, [line.now(second_low), w_back, slope], **inner_call)
        )
        line.take(a)
        line.go(a, Z1)
        b = grads((first_low, inner_low), name="grad_w_in", pieces=1)
        line.go(b, CORE)
        grad_first, branch_low, att_grad, sums_one = line.ran(
            kernel_call(
                first_back_kernel, first_shape,
                [line.now(inner_low), w_in, grad_second, n1, r1, ln1_gain, w_out], **first_call
            )
        )
        line.take(b)
        line.go(b, X)
        grad_left, sums_left = line.ran(attention_back(line.now(att_grad), 0, split))
        c = grads((x, grad_left), (attended, branch_low), name="grad_w_qkv_1", pieces=1)
        line.go(c, CORE)
        grad_right, sums_right = line.ran(attention_back(line.now(att_grad), split, head_pairs - split))
        line.take(c, pieces=2)
        line.take(a)
        line.go(a, Z2)
        cols = 6 * HEAD_DIM * (head_pairs - split) + 128
        d = line.chunk(
            kernel_call(
                functools.partial(last_grad_kernel, order=(CORE, X, Z1, Z2)),
                [sds((devices // 2, share, cols), BF)] + [sds((devices // 2 // 1, share, cols), BF)] * 1,
                [place, x, line.now(grad_right), sums_two, sums_one, sums_left, sums_right, sums_in],
                smem=1, scratch=[pltpu.VMEM((width, cols), BF)], mib=5,
                flops=2 * length * width * cols, name="grad_w_qkv_2",
            ),
            extra=128,
        )
        line.go(d, CORE)
        grad_hidden = line.ran([input_back(grad_left, line.now(grad_right))])[0]
        line.take(d)
        line.go(c, X, behind=b)
        line.take(b, pieces=2)
        line.go(b, Z1)
        line.take(a)
        line.go(d, X, behind=c)
        line.take(c, pieces=2)
        line.go(c, Z1)
        line.take(b)
        line.go(b, Z2)
        line.go(a, X, behind=d)
        line.take(d)
        line.go(d, Z1)
        line.take(c)
        line.go(c, Z2)
        share_w_in = line.finish(b)
        line.take(d)
        line.go(d, Z2)
        share_w_back = line.finish(a)
        (
            share_w_qkv, share_w_out, share_bq, share_bv, share_gain2, share_bias2, share_b_back,
            share_gain1, share_bias1, share_b_out, share_b_in,
        ) = kernel_call(
            finish_last_kernel,
            [sds((share, 3 * width), F32), sds((share, width), F32)] + [sds((1, share), F32)] * 8
            + [sds((1, hidden // devices), F32)],
            [c["keep"], line.now(c["came"][0]), d["keep"], d["came"][0]], mib=4, name="finish_last",
        )
    else:
        share_w_back = plain_grad(act, second_low, "grad_w_back")
        inner_low, sums_in = kernel_call(
            inner_back_kernel, inner_shape, [second_low, w_back, slope], **inner_call
        )
        share_w_in = plain_grad(first_low, inner_low, "grad_w_in")
        grad_first, branch_low, att_grad, sums_one = kernel_call(
            first_back_kernel, first_shape, [inner_low, w_in, grad_second, n1, r1, ln1_gain, w_out],
            **first_call
        )
        grad_left, sums_left = attention_back(att_grad, 0, split)
        grad_right, sums_right = attention_back(att_grad, split, head_pairs - split)
        grad_hidden = input_back(grad_left, grad_right)

        def joined(left, right):
            pieces = [jnp.split(half, 3, 1) for half in (left, right)]
            return jnp.concatenate([piece for both in zip(*pieces) for piece in both], 1)

        grad_proj, sums_qkv = joined(grad_left, grad_right), joined(sums_left, sums_right)
        share_w_qkv = plain_grad(x, grad_proj, "grad_w_qkv")
        share_w_out = plain_grad(attended, branch_low, "grad_w_out")

        def scattered(vector):
            return lax.psum_scatter(vector, "dp", scatter_dimension=1, tiled=True)

        share_bq, share_bv = scattered(sums_qkv[:, :width]), scattered(sums_qkv[:, 2 * width :])
        share_gain2, share_bias2, share_b_back = (scattered(sums_two[k : k + 1]) for k in range(3))
        share_gain1, share_bias1, share_b_out = (scattered(sums_one[k : k + 1]) for k in range(3))
        share_b_in = scattered(sums_in)
    return (
        out_hidden[None],
        grad_hidden[None],
        share_w_qkv[None],
        share_bq,
        share_bv,
        share_w_out[None],
        share_b_out,
        share_gain1,
        share_bias1,
        share_w_in[None],
        share_b_in,
        share_w_back[None],
        share_b_back,
        share_gain2,
        share_bias2,
    )


def solution(mesh):
    matrix, vector = P("tower", None, None), P("tower", None)
    rows, spread = P("tower", "dp", None), P("tower", "dp")
    return jax.shard_map(
        shards,
        mesh=mesh,
        in_specs=(
            rows, P("dp", None), P("dp"), rows, matrix, vector, vector, matrix, vector, vector, vector,
            matrix, vector, matrix, vector, vector, vector,
        ),
        out_specs=(
            rows, rows, rows, spread, spread, rows, spread, spread, spread, rows, spread, rows, spread,
            spread, spread,
        ),
        check_vma=False,
    )
```

```python
import functools
import math

import jax
import jax.numpy as jnp
from jax import lax
from jax.experimental import pallas as pl
from jax.experimental.pallas import tpu as pltpu
from jax.sharding import PartitionSpec as P

HEAD_DIM = 64
QLEN = 32
SEGS = 4
PACKET = 24
EPS = 1e-05
BF = jnp.bfloat16
F32 = jnp.float32
TILE = 32

COSTS = {"first_back": 3 * 10**10, "attention_back_4": 3 * 10**10, "input_back": 3 * 10**10}

VM = pl.BlockSpec(memory_space=pltpu.VMEM)
SM = pl.BlockSpec(memory_space=pltpu.SMEM)
HB = pl.BlockSpec(memory_space=pltpu.HBM)


def nn(a, b):
    return lax.dot_general(a, b, (((1,), (0,)), ((), ())), preferred_element_type=F32)


def nt(a, b):
    return lax.dot_general(a, b, (((1,), (1,)), ((), ())), preferred_element_type=F32)


def tn(a, b):
    return lax.dot_general(a, b, (((0,), (0,)), ((), ())), preferred_element_type=F32)


def kernel_call(body, outs, args, scratch=(), smem=0, hbm=0, mib=32, flops=0, name=None):
    single = not isinstance(outs, (list, tuple))
    shapes = [outs] if single else list(outs)
    result = pl.pallas_call(
        body,
        out_shape=shapes,
        in_specs=[SM] * smem + [VM] * (len(args) - smem - hbm) + [HB] * hbm,
        out_specs=[VM] * len(shapes),
        scratch_shapes=list(scratch),
        compiler_params=pltpu.CompilerParams(vmem_limit_bytes=mib << 20),
        cost_estimate=pl.CostEstimate(flops=COSTS.get(name, 0), bytes_accessed=0, transcendentals=0),
        name=name,
    )(*args)
    return result[0] if single else result


def sds(shape, dtype):
    return jax.ShapeDtypeStruct(shape, dtype)


def fold(value):
    rows, cols = value.shape
    return jnp.sum(value.reshape(rows // 8, 8, cols), 0)


def head_mask(half):
    lane = lax.broadcasted_iota(jnp.int32, (1, 2 * HEAD_DIM), 1)
    return (lane // HEAD_DIM == half).astype(F32).astype(BF)


def normalise(value):
    centred = value - jnp.mean(value, -1, keepdims=True)
    inverse = lax.rsqrt(jnp.mean(centred * centred, -1, keepdims=True) + EPS)
    return centred * inverse, inverse


def norm_back(grad, normed, inverse, gain):
    scaled = grad * gain
    return inverse * (
        scaled
        - jnp.mean(scaled, -1, keepdims=True)
        - normed * jnp.mean(scaled * normed, -1, keepdims=True)
    )


def gelu_pair(value):
    cdf = 0.5 * lax.erf(value * (1.0 / math.sqrt(2.0))) + 0.5
    density = jnp.exp(value * value * -0.5) * (1.0 / math.sqrt(2.0 * math.pi))
    return value * cdf, cdf + value * density


def proj_kernel(x_hbm, w_hbm, bq_hbm, bv_hbm, out, x, w0, w1, w2, bq, bv, sems):
    width = x.shape[1]
    parts = (w0, w1, w2)
    copies = [
        pltpu.make_async_copy(w_hbm.at[:, pl.ds(k * width, width)], parts[k], sems.at[k]) for k in range(3)
    ]
    x_copy = pltpu.make_async_copy(x_hbm, x, sems.at[3])
    bq_copy = pltpu.make_async_copy(bq_hbm, bq, sems.at[4])
    bv_copy = pltpu.make_async_copy(bv_hbm, bv, sems.at[5])
    for copy in (x_copy, copies[1], copies[0], bq_copy, copies[2], bv_copy):
        copy.start()
    x_copy.wait()
    for k in (1, 0, 2):
        copies[k].wait()
        value = nn(x[...], parts[k][...])
        if k == 0:
            bq_copy.wait()
            value = value + bq[...]
        if k == 2:
            bv_copy.wait()
            value = value + bv[...]
        out[:, k * width : (k + 1) * width] = value.astype(BF)


def chosen_rows(tower, seg, count, length):
    row = lax.broadcasted_iota(jnp.int32, (count, 1), 0)
    place = lax.broadcasted_iota(jnp.int32, (count, length), 1)
    start = jnp.sum((seg < row).astype(F32), 1, keepdims=True).astype(jnp.int32)
    wanted = jnp.where(tower == 0, row * QLEN, jnp.where(row < SEGS, start, -1))
    return (place == wanted).astype(F32)


def cls_kernel(place, seg, x, proj, w_out, b_out, g1, b1, w_in, b_in, w_back, b_back, g2, b2, cls):
    length, width = x.shape
    count = cls.shape[0]
    heads = width // HEAD_DIM
    tower = place[0]
    pick = chosen_rows(tower, seg[...], count, length)
    pick_low = pick.astype(BF)
    x_cls = nn(pick_low, x[...])
    q_cls = (nn(pick_low, proj[:, :width]) * (1.0 / math.sqrt(HEAD_DIM))).astype(BF)
    place_row = lax.broadcasted_iota(jnp.int32, (1, length), 1)
    own_seg = jnp.where(tower == 0, place_row // QLEN, seg[...])
    row = lax.broadcasted_iota(jnp.int32, (count, 1), 0)
    bias = jnp.where(own_seg == row, 0.0, -1e9)
    lane_head = lax.broadcasted_iota(jnp.int32, (1, width), 1) // HEAD_DIM
    spread = jnp.concatenate(
        [q_cls * (lane_head == h).astype(F32).astype(BF) for h in range(heads)], 0
    )
    scores = nt(spread, proj[:, width : 2 * width]) + jnp.concatenate([bias] * heads, 0)
    shifted = jnp.exp(scores - jnp.max(scores, -1, keepdims=True))
    probs = (shifted / jnp.sum(shifted, -1, keepdims=True)).astype(BF)
    mixed = nn(probs, proj[:, 2 * width :])
    attended = jnp.zeros((count, width), F32)
    for h in range(heads):
        attended = attended + jnp.where(lane_head == h, mixed[h * count : (h + 1) * count], 0.0)
    first = x_cls + (nn(attended.astype(BF), w_out[...]) + b_out[...])
    normed = normalise(first)[0] * g1[...] + b1[...]
    inner = nn(normed.astype(BF), w_in[...]) + b_in[...]
    act = gelu_pair(inner)[0].astype(BF)
    second = normed + (nn(act, w_back[...]) + b_back[...])
    final = normalise(second)[0] * g2[...] + b2[...]
    cls[...] = final.astype(BF)


def attention_kernel(place, seg_row, seg_col, proj, attended, probs, bias, *work):
    length = proj.shape[0]
    width = proj.shape[1] // 3
    tower = place[0]
    lane = lax.broadcasted_iota(jnp.int32, (1, length), 1)
    sub = lax.broadcasted_iota(jnp.int32, (length, 1), 0)
    row_seg = jnp.where(tower == 0, lane // QLEN, seg_row[...])
    col_seg = jnp.where(tower == 0, sub // QLEN, seg_col[...])
    bias[...] = jnp.where(col_seg == row_seg, 0.0, -1e9)
    masks = [head_mask(0), head_mask(1)]
    scale = jnp.asarray(1.0 / math.sqrt(HEAD_DIM), BF)
    step = 2 * HEAD_DIM
    pairs = width // step
    work_a, work_b = work

    def columns(part, pair):
        return proj[:, pl.ds(pl.multiple_of(part * width + pair * step, step), step)]

    def scores(pair, ref):
        queries, keys = columns(0, pair) * scale, columns(1, pair)
        for half in range(2):
            ref[half] = nt(queries * masks[half], keys)

    def soften(pair, ref):
        for half in range(2):
            for r in range(0, length, TILE):
                value = ref[half, r : r + TILE, :] + bias[r : r + TILE, :]
                shifted = jnp.exp(value - jnp.max(value, -1, keepdims=True))
                total = jnp.sum(shifted, -1, keepdims=True)
                probs[2 * pair + half, r : r + TILE, :] = (shifted * (1.0 / total)).astype(BF)

    def mix(pair):
        values = columns(2, pair)
        mixed = nn(probs[2 * pair], values * masks[0]) + nn(probs[2 * pair + 1], values * masks[1])
        attended[:, pl.ds(pl.multiple_of(pair * step, step), step)] = mixed.astype(BF)

    def two_pairs(k, carry):
        pair = 2 * k
        scores(pair + 1, work_b)
        soften(pair, work_a)
        scores(jnp.minimum(pair + 2, pairs - 1), work_a)
        mix(pair)
        soften(pair + 1, work_b)
        mix(pair + 1)
        return carry

    scores(0, work_a)
    lax.fori_loop(0, pairs // 2, two_pairs, 0)


def first_kernel(x, attended, w_out, b_out, g1, b1, n1, r1, low, work):
    work[...] = nn(attended[...], w_out[...])
    def step(i, carry):
        rows = pl.ds(pl.multiple_of(i * TILE, TILE), TILE)
        first = x[rows, :].astype(F32) + (work[rows, :] + b_out[...])
        normed, inverse = normalise(first)
        n1[rows, :] = normed
        r1[rows, :] = inverse
        low[rows, :] = (normed * g1[...] + b1[...]).astype(BF)
        return carry

    lax.fori_loop(0, x.shape[0] // TILE, step, 0, unroll=4)


def inner_kernel(low, w_in, b_in, act, slope, work_a, work_b):
    length = low.shape[0]
    block = work_a.shape[1]
    blocks = w_in.shape[1] // block

    def columns(i):
        return pl.ds(pl.multiple_of(i * block, block), block)

    def gelu_block(i, work):
        bias = b_in[:, columns(i)]
        for r in range(0, length, TILE):
            value, grad = gelu_pair(work[r : r + TILE, :] + bias)
            act[r : r + TILE, columns(i)] = value.astype(BF)
            slope[r : r + TILE, columns(i)] = grad.astype(BF)

    work_a[...] = nn(low[...], w_in[:, :block])

    def step(k, carry):
        i = 2 * k
        work_b[...] = nn(low[...], w_in[:, columns(i + 1)])
        gelu_block(i, work_a)
        work_a[...] = nn(low[...], w_in[:, columns(jnp.minimum(i + 2, blocks - 1))])
        gelu_block(i + 1, work_b)
        return carry

    lax.fori_loop(0, blocks // 2, step, 0)


def second_kernel(act, w_back, b_back, n1, g1, b1, g2, b2, n2, r2, out, work):
    part = work.shape[0]

    def normalise_part(k, carry):
        at = pl.multiple_of(k * part, part)
        work[...] = nn(act[pl.ds(at, part), :], w_back[...])
        for r in range(0, part, TILE):
            rows = pl.ds(pl.multiple_of(at + r, TILE), TILE)
            branch = work[r : r + TILE, :] + b_back[...]
            second = (n1[rows, :] * g1[...] + b1[...]) + branch
            normed, inverse = normalise(second)
            n2[rows, :] = normed
            r2[rows, :] = inverse
            out[rows, :] = (normed * g2[...] + b2[...]).astype(BF)
        return carry

    lax.fori_loop(0, act.shape[0] // part, normalise_part, 0)


def packet_kernel(place, cls, other, labels, out):
    query = place[0] == 0
    count, width = cls.shape
    mine, came = cls[...].astype(F32), other[...].astype(F32)
    q_rows = jnp.where(query, mine, came)
    p_rows = jnp.where(query, came, mine)[:SEGS]
    value = labels[...]
    gap = jnp.zeros((1, 128 - count), F32)
    row = jnp.concatenate(
        [(value >> 8).astype(F32), gap, (value & 255).astype(F32), gap, jnp.zeros((1, width - 256), F32)], 1
    )
    rest = jnp.zeros((PACKET - count - SEGS - 1, width), F32)
    out[...] = jnp.concatenate([q_rows, p_rows, row, rest], 0).astype(BF)


def loss_kernel(place, near, far, grad, *, order, count):
    tower, me = place[0], place[1]
    packets = jnp.concatenate([near[...], far[...]], 0)
    total, width = packets.shape
    scale = 2.0 / math.sqrt(width)
    row = lax.broadcasted_iota(jnp.int32, (total, 1), 0)
    col = lax.broadcasted_iota(jnp.int32, (1, total), 1)
    col_slot, col_part = col // PACKET, col % PACKET
    mixed = jnp.zeros_like(col)
    for j, b in enumerate(order):
        mixed = mixed | (((col_slot >> j) & 1) << b)
    is_passage = jnp.logical_and(col_part >= count, col_part < count + SEGS)
    number = jnp.where(is_passage, (mixed ^ me) * SEGS + (col_part - count), -1)
    label_of = ((row // PACKET) * PACKET + (count + SEGS) == col).astype(F32).astype(BF)
    label_rows = nn(label_of, packets[:, :256])
    lane = lax.broadcasted_iota(jnp.int32, (1, 256), 1)
    part = row % PACKET
    weight = jnp.where(lane == part, 256.0, 0.0) + jnp.where(lane == part + 128, 1.0, 0.0)
    label = jnp.sum(label_rows * weight, 1, keepdims=True).astype(jnp.int32)
    logits = jnp.where(is_passage, nt(packets, packets) * scale, -1e30)
    soft = jnp.exp(logits - jnp.max(logits, -1, keepdims=True))
    soft = soft / jnp.sum(soft, -1, keepdims=True)
    grad_logits = soft - (number == label).astype(F32)
    grad_logits = grad_logits * (part < count).astype(F32)
    wide = packets.astype(F32)
    grad_q = jnp.dot(
        grad_logits[:count], wide, precision=lax.Precision.HIGHEST, preferred_element_type=F32
    )
    pick = lax.broadcasted_iota(jnp.int32, (count, 1), 0)
    pick = jnp.logical_and(pick + count == col, pick < SEGS).astype(F32)
    turned = lax.dot_general(
        pick, grad_logits, (((1,), (1,)), ((), ())),
        precision=lax.Precision.HIGHEST, preferred_element_type=F32,
    )
    grad_p = jnp.dot(turned, wide, precision=lax.Precision.HIGHEST, preferred_element_type=F32)
    grad[...] = jnp.where(tower == 0, grad_q, grad_p) * scale


def plain_loss(packets, tower, me, count):
    devices, _, width = packets.shape
    scale = 2.0 / math.sqrt(width)
    queries = packets[:, :count].reshape(devices * count, width)
    passages = packets[:, count : count + SEGS].reshape(devices * SEGS, width)
    row = packets[:, count + SEGS].astype(jnp.int32)
    label = (row[:, :count] * 256 + row[:, 128 : 128 + count]).reshape(devices * count, 1)
    soft = jax.nn.softmax(nt(queries, passages) * scale, -1)
    grad = soft - (label == jnp.arange(devices * SEGS, dtype=jnp.int32)).astype(F32)
    grad_q = lax.dynamic_slice_in_dim(grad, me * count, count, 0)
    grad_q = jnp.dot(grad_q, passages.astype(F32), precision=lax.Precision.HIGHEST)
    grad_p = lax.dynamic_slice_in_dim(grad, me * SEGS, SEGS, 1)
    grad_p = jnp.dot(grad_p.T, queries.astype(F32), precision=lax.Precision.HIGHEST)
    grad_p = jnp.pad(grad_p, ((0, count - SEGS), (0, 0)))
    return jnp.where(tower == 0, grad_q, grad_p) * scale


def split_three(value):
    high = value.astype(BF)
    rest = value - high.astype(F32)
    middle = rest.astype(BF)
    return jnp.concatenate([high, middle, (rest - middle.astype(F32)).astype(BF)], 0)


def norm_back_rows(rows, grad, normed, inverse, gain, out, low, totals):
    back = norm_back(grad, normed[rows, :], inverse[rows, :], gain[...])
    out[rows, :] = back
    back_low = back.astype(BF)
    low[rows, :] = back_low
    parts = (fold(grad * normed[rows, :]), fold(grad), fold(back_low.astype(F32)))
    return parts if totals is None else tuple(a + b for a, b in zip(totals, parts))


def second_back_kernel(place, seg, out_grad, cls_grad, n2, r2, g2, grad, low, sums, work):
    length, width = out_grad.shape
    count = cls_grad.shape[0]
    pick = chosen_rows(place[0], seg[...], count, length).astype(BF)
    work[...] = tn(jnp.concatenate([pick] * 3, 0), split_three(cls_grad[...]))
    totals = None
    for r in range(0, length, TILE):
        rows = slice(r, r + TILE)
        final = out_grad[rows, :].astype(F32) + work[rows, :]
        totals = norm_back_rows(rows, final, n2, r2, g2, grad, low, totals)
    for k, part in enumerate(totals):
        sums[k : k + 1, :] = jnp.sum(part, 0, keepdims=True)


def inner_back_kernel(low, w_back, slope, out, sums):
    block = 256

    def step(i, carry):
        cols = pl.ds(pl.multiple_of(i * block, block), block)
        value = (nt(low[...], w_back[cols, :]) * slope[:, cols].astype(F32)).astype(BF)
        out[:, cols] = value
        sums[:, cols] = jnp.sum(value.astype(F32), 0, keepdims=True)
        return carry

    lax.fori_loop(0, w_back.shape[0] // block, step, 0, unroll=2)


def first_back_kernel(inner, w_in, grad_second, n1, r1, g1, w_out, grad, low, att, sums, work):
    length, width = grad_second.shape
    part = work.shape[0]

    def back_part(k, totals):
        at = pl.multiple_of(k * part, part)
        work[...] = nt(inner[pl.ds(at, part), :], w_in[...])
        for r in range(0, part, TILE):
            rows = pl.ds(pl.multiple_of(at + r, TILE), TILE)
            value = grad_second[rows, :] + work[r : r + TILE, :]
            totals = norm_back_rows(rows, value, n1, r1, g1, grad, low, totals)
        rows = pl.ds(at, part)
        att[rows, :] = nt(low[rows, :], w_out[...]).astype(BF)
        return totals

    zero = jnp.zeros((8, width), F32)
    totals = lax.fori_loop(0, length // part, back_part, (zero, zero, zero))
    for k, total in enumerate(totals):
        sums[k : k + 1, :] = jnp.sum(total, 0, keepdims=True)


def attention_back_kernel(proj, probs, att_grad, out, sums, dp_a, dp_b, ds_a, ds_b, *, first):
    length = proj.shape[0]
    width = proj.shape[1] // 3
    own = out.shape[1] // 3
    masks = [head_mask(0), head_mask(1)]
    scale = 1.0 / math.sqrt(HEAD_DIM)
    step = 2 * HEAD_DIM
    pairs = own // step

    def columns(part, pair):
        return proj[:, pl.ds(pl.multiple_of(part * width + (first + pair) * step, step), step)]

    def grad_columns(pair):
        return att_grad[:, pl.ds(pl.multiple_of((first + pair) * step, step), step)]

    def grad_probs(pair, dp):
        grads, values = grad_columns(pair), columns(2, pair)
        for half in range(2):
            dp[half] = nt(grads * masks[half], values)

    def grad_scores(pair, dp, ds):
        for half in range(2):
            for r in range(0, length, TILE):
                wide = probs[2 * (first + pair) + half, r : r + TILE, :].astype(F32)
                grad = dp[half, r : r + TILE, :]
                delta = jnp.sum(grad * wide, -1, keepdims=True)
                ds[half, r : r + TILE, :] = (wide * (grad - delta)).astype(BF)

    def results(pair, ds):
        queries_t, grads_t = columns(0, pair).T, grad_columns(pair).T
        keys = columns(1, pair)
        grad_q, grad_k_t, grad_v_t = None, [], []
        for half in range(2):
            scores = ds[half]
            lanes = slice(half * HEAD_DIM, (half + 1) * HEAD_DIM)
            grad_v_t.append(nn(grads_t[lanes], probs[2 * (first + pair) + half]))
            grad_k_t.append(nn(queries_t[lanes], scores))
            term = nn(scores, keys * masks[half])
            grad_q = term if grad_q is None else grad_q + term
        parts = (
            grad_q * scale,
            jnp.concatenate(grad_k_t, 0).T * scale,
            jnp.concatenate(grad_v_t, 0).T,
        )
        for k, part in enumerate(parts):
            cols = pl.ds(pl.multiple_of(k * own + pair * step, step), step)
            part_low = part.astype(BF)
            out[:, cols] = part_low
            sums[:, cols] = jnp.sum(part_low.astype(F32), 0, keepdims=True)

    def two_pairs(k, carry):
        pair = 2 * k
        grad_probs(pair + 1, dp_b)
        grad_scores(pair, dp_a, ds_a)
        grad_probs(jnp.minimum(pair + 2, pairs - 1), dp_a)
        results(pair, ds_a)
        grad_scores(pair + 1, dp_b, ds_b)
        results(pair + 1, ds_b)
        return carry

    grad_probs(0, dp_a)
    lax.fori_loop(0, pairs // 2, two_pairs, 0)


def input_back_kernel(left, right, w_qkv, grad_first, out, work):
    width = out.shape[1]
    for k in range(3):
        at = k * width
        for part in (left, right):
            own = part.shape[1] // 3
            work[:, at : at + own] = part[:, k * own : (k + 1) * own]
            at += own
    block = 256
    for i in range(width // block):
        cols = slice(i * block, (i + 1) * block)
        value = grad_first[:, cols] + nt(work[...], w_qkv[cols, :])
        out[:, cols] = value.astype(BF)


def slot_device(me, order, slot):
    mixed = 0
    for j, b in enumerate(order):
        mixed = mixed | (((slot >> (len(order) - 1 - j)) & 1) << b)
    return me ^ mixed


def spread_shares(place, work, outs, order):
    me = place[1]
    if len(outs) == 1:
        outs = (outs[0].at[0], outs[0].at[1])
        me = me & ~(1 << order[0])
    keep, *sends = outs
    half, share, _ = keep.shape
    for slot in range(2 * half):
        ref, at = (keep, slot) if slot < half else piece_of(sends, slot - half)
        device = slot_device(me, order, slot)
        ref[at] = work[pl.ds(pl.multiple_of(device * share, 16), share), :]


def piece_of(refs, slot):
    size = refs[0].shape[0]
    return refs[slot // size], slot % size


def weight_grad_kernel(place, *refs, order, pairs):
    *outs, work = refs[2 * pairs :]
    block = 768

    def run(i):
        return pl.ds(pl.multiple_of(i * block, block), block)

    at = 0
    for left, right in zip(refs[: 2 * pairs : 2], refs[1 : 2 * pairs : 2]):
        rows, cols = left.shape[1], right.shape[1]

        def by_rows(i, carry, left=left, right=right, at=at, cols=cols):
            work[run(i), at : at + cols] = tn(left[:, run(i)], right[...]).astype(BF)
            return carry

        def by_columns(i, carry, left=left, right=right, at=at):
            there = pl.ds(pl.multiple_of(at + i * block, 128), block)
            work[:, there] = tn(left[...], right[:, run(i)]).astype(BF)
            return carry

        if rows > block:
            lax.fori_loop(0, rows // block, by_rows, 0)
        else:
            lax.fori_loop(0, cols // block, by_columns, 0)
        at += cols
    spread_shares(place, work, outs, order)


def last_grad_kernel(
    place, x, grad_proj, sums_two, sums_one, sums_left, sums_right, sums_in, *refs, order
):
    *outs, work = refs
    width = x.shape[1]
    share = outs[0].shape[1]
    devices = 2 * outs[0].shape[0]
    wide = grad_proj.shape[1]
    work[:, :wide] = tn(x[...], grad_proj[...]).astype(BF)
    extra = slice(wide, wide + 128)
    thirds = [sums.shape[1] // 3 for sums in (sums_left, sums_right)]
    query, value = (
        jnp.concatenate(
            [sums[:, k * own : (k + 1) * own] for sums, own in zip((sums_left, sums_right), thirds)], 1
        )
        for k in (0, 2)
    )
    stacked = jnp.concatenate([query, value, sums_two[0:3], sums_one[0:3]], 0)
    work[:, extra] = jnp.zeros((width, 128), BF)
    in_share = sums_in.shape[1] // devices
    for d in range(devices):
        rows = [stacked[:, d * share : (d + 1) * share]]
        for k in range(in_share // share):
            at = d * in_share + k * share
            rows.append(sums_in[:, at : at + share])
        rows.append(jnp.zeros((16 - 8 - in_share // share, share), F32))
        block = jnp.concatenate(rows, 0)
        block = jnp.concatenate([block, jnp.zeros((16, 128 - share), F32)], 1)
        high = block.astype(BF)
        work[d * share : d * share + 16, extra] = high
        work[d * share + 16 : d * share + 32, extra] = (block - high.astype(F32)).astype(BF)
    spread_shares(place, work, outs, order)


def add_extra(left, right):
    total = (
        left[0:16].astype(F32) + left[16:32].astype(F32) + right[0:16].astype(F32) + right[16:32].astype(F32)
    )
    return total


def halve_kernel(*refs, cames, extra):
    kept, came, (keep, *sends) = refs[0], refs[1 : 1 + cames], refs[1 + cames :]
    half = keep.shape[0]
    cols = keep.shape[2] - extra
    for slot in range(2 * half):
        ref, at = (keep, slot) if slot < half else piece_of(sends, slot - half)
        other, there = piece_of(came, slot)
        ref[at, :, :cols] = (kept[slot, :, :cols].astype(F32) + other[there, :, :cols].astype(F32)).astype(BF)
        if extra:
            total = add_extra(kept[slot, :, cols:], other[there, :, cols:])
            high = total.astype(BF)
            ref[at, 0:16, cols:] = high
            ref[at, 16:32, cols:] = (total - high.astype(F32)).astype(BF)
            ref[at, 32:, cols:] = jnp.zeros((keep.shape[1] - 32, extra), BF)


def halve_cores_kernel(both, *outs, extra):
    halve_kernel(both.at[0], both.at[1], *outs, cames=1, extra=extra)


def finish_kernel(kept, came, out):
    out[...] = kept[0].astype(F32) + came[0].astype(F32)


def finish_last_kernel(
    kept, came, kept_last, came_last, w_qkv, w_out, bq, bv, gain2, bias2, b_back, gain1, bias1, b_out, b_in
):
    width = w_out.shape[1]
    share = bq.shape[1]
    left, right = (kept.shape[2] - width) // 3, (kept_last.shape[2] - 128) // 3
    for k in range(3):
        at = k * width
        cols = slice(k * left, (k + 1) * left)
        w_qkv[:, at : at + left] = kept[0, :, cols].astype(F32) + came[0, :, cols].astype(F32)
        cols = slice(k * right, (k + 1) * right)
        w_qkv[:, at + left : at + width] = kept_last[0, :, cols].astype(F32) + came_last[0, :, cols].astype(F32)
    w_out[...] = kept[0, :, 3 * left :].astype(F32) + came[0, :, 3 * left :].astype(F32)
    vectors = add_extra(kept_last[0, :, 3 * right :], came_last[0, :, 3 * right :])
    for k, ref in enumerate((bq, bv, gain2, bias2, b_back, gain1, bias1, b_out)):
        ref[...] = vectors[k : k + 1, :share]
    pieces = b_in.shape[1] // share
    b_in[...] = jnp.concatenate([vectors[8 + k : 9 + k, :share] for k in range(pieces)], 1)


def plain_grad_kernel(left, right, out):
    out[...] = tn(left[...], right[...])


def swapped(value, axis, mask):
    count = lax.axis_size(axis)
    return lax.ppermute(value, axis, [(i, i ^ mask) for i in range(count)])


class Sequence:
    def __init__(self):
        self.last = None

    def now(self, value):
        return value if self.last is None else after(value, self.last)

    def ran(self, results):
        self.last = results[0]
        return results

    def chunk(self, outs, extra=0, pieces=1):
        chunk = {"extra": extra}
        if len(outs) > 1:
            chunk["keep"], *chunk["sends"] = self.ran(outs)
        else:
            pairs = [[i, i + 1] for i in range(0, lax.axis_size("dp"), 2)]
            both = lax.all_to_all(outs[0], "dp", 0, 0, tiled=True, axis_index_groups=pairs)
            self.last = both
            self.parted(chunk, functools.partial(halve_cores_kernel, extra=extra), [both], both.shape[1:], pieces)
        return chunk

    def parted(self, chunk, body, args, shape, pieces):
        half = sds((shape[0] // 2,) + shape[1:], BF)
        piece = sds((shape[0] // 2 // pieces,) + shape[1:], BF)
        chunk["keep"], *chunk["sends"] = self.ran(
            kernel_call(body, [half] + [piece] * pieces, args, mib=4, name="halve")
        )

    def go(self, chunk, bit, behind=None):
        sends = [self.now(send) for send in chunk["sends"]]
        if behind is not None:
            sends = [after(send, *behind["came"]) for send in sends]
        chunk["came"] = [swapped(send, "dp", 1 << bit) for send in sends]

    def take(self, chunk, pieces=1):
        keep, came = chunk["keep"], [self.now(value) for value in chunk["came"]]
        body = functools.partial(halve_kernel, cames=len(came), extra=chunk["extra"])
        self.parted(chunk, body, [keep] + came, keep.shape, pieces)

    def finish(self, chunk):
        args = [chunk["keep"], self.now(chunk["came"][0])]
        return self.ran([kernel_call(finish_kernel, sds(args[0].shape[1:], F32), args, mib=4, name="finish")])[0]


def after(value, *earlier):
    return lax.optimization_barrier((value,) + earlier)[0]


def shards(
    hidden_in,
    seg_ids,
    labels,
    out_grad,
    w_qkv,
    b_query,
    b_value,
    w_out,
    b_out,
    ln1_gain,
    ln1_bias,
    w_in,
    b_in,
    w_back,
    b_back,
    ln2_gain,
    ln2_bias,
):
    x, cotangent = hidden_in[0], out_grad[0]
    w_qkv, w_out, w_in, w_back = w_qkv[0], w_out[0], w_in[0], w_back[0]
    length, width = x.shape
    hidden = w_in.shape[1]
    heads = width // HEAD_DIM
    count = length // QLEN
    devices = lax.axis_size("dp")
    bits = devices.bit_length() - 1
    tower, me = lax.axis_index("tower"), lax.axis_index("dp")
    place = jnp.stack([tower, me]).astype(jnp.int32)
    seg_col = seg_ids.reshape(length, 1)
    fast = devices == 16

    proj = kernel_call(
        proj_kernel, sds((length, 3 * width), BF),
        [pltpu.with_memory_space_constraint(member, pltpu.HBM) for member in (x, w_qkv, b_query, b_value)], hbm=4,
        scratch=[pltpu.VMEM((length, width), BF)] + [pltpu.VMEM((width, width), BF)] * 3
        + [pltpu.VMEM((1, width), F32)] * 2 + [pltpu.SemaphoreType.DMA((6,))],
        mib=8, flops=2 * length * 3 * width * width, name="proj",
    )
    cls = kernel_call(
        cls_kernel, sds((count, width), BF),
        [place, seg_ids, x, proj, w_out, b_out, ln1_gain, ln1_bias, w_in, b_in, w_back, b_back,
         ln2_gain, ln2_bias],
        smem=1, mib=3, flops=2 * 256 * width * hidden * 2, name="cls",
    )
    other = swapped(cls, "tower", 1)
    attended, probs = kernel_call(
        attention_kernel, [sds((length, width), BF), sds((heads, length, length), BF)],
        [place, seg_ids, seg_col, after(proj, cls)], smem=1,
        scratch=[pltpu.VMEM((length, length), F32)] + [pltpu.VMEM((2, length, length), F32)] * 2,
        mib=9, flops=4 * heads * length * length * 256, name="attention",
    )
    held = kernel_call(
        packet_kernel, sds((PACKET, width), BF), [place, cls, after(other, attended), labels[None]],
        smem=1, mib=1, name="packet",
    )
    order = [3, 2, 1, 0] if fast else list(range(bits))
    if fast:
        came = swapped(held, "dp", 1 << order[0])
    work, half_work = pltpu.VMEM((length, width), F32), pltpu.VMEM((length // 2, width), F32)
    n1, r1, first_low = kernel_call(
        first_kernel,
        [sds((length, width), F32), sds((length, 1), F32), sds((length, width), BF)],
        [x, after(attended, held), w_out, b_out, ln1_gain, ln1_bias], scratch=[work],
        mib=4, flops=2 * length * width * width, name="first",
    )
    if fast:
        held = jnp.concatenate([held, after(came, first_low)], 0)
        came = swapped(held, "dp", 1 << order[1])
    act, slope = kernel_call(
        inner_kernel, [sds((length, hidden), BF), sds((length, hidden), BF)],
        [after(first_low, held), w_in, b_in], scratch=[pltpu.VMEM((length, 256), F32)] * 2,
        mib=4, flops=8 * length * width * hidden, name="inner",
    )
    if fast:
        held = jnp.concatenate([held, after(came, act)], 0)
        came = swapped(held, "dp", 1 << order[2])
    n2, r2, out_hidden = kernel_call(
        second_kernel,
        [sds((length, width), F32), sds((length, 1), F32), sds((length, width), BF)],
        [after(act, held), w_back, b_back, n1, ln1_gain, ln1_bias, ln2_gain, ln2_bias], scratch=[half_work],
        mib=5, flops=2 * length * width * hidden, name="second",
    )
    if fast:
        near = jnp.concatenate([held, after(came, out_hidden)], 0)
        far = swapped(near, "dp", 1 << order[3])
        cls_grad = kernel_call(
            functools.partial(loss_kernel, order=order, count=count), sds((count, width), F32),
            [place, near, far], smem=1,
            mib=5, flops=8 * devices * count * devices * SEGS * width, name="loss",
        )
    else:
        packets = lax.all_gather(held, "dp", axis=0)
        cls_grad = plain_loss(packets, tower, me, count)

    grad_second, second_low, sums_two = kernel_call(
        second_back_kernel,
        [sds((length, width), F32), sds((length, width), BF), sds((8, width), F32)],
        [place, seg_ids, cotangent, cls_grad, n2, r2, ln2_gain], smem=1, scratch=[work],
        mib=4, flops=2 * length * width * 256, name="second_back",
    )

    def plain_grad(left, right, name):
        rows, cols = left.shape[1], right.shape[1]
        whole = kernel_call(
            plain_grad_kernel, sds((rows, cols), F32), [left, right], mib=24,
            flops=2 * length * rows * cols, name=name,
        )
        return lax.psum_scatter(whole, "dp", scatter_dimension=0, tiled=True)

    inner_call = dict(mib=3, flops=2 * length * width * hidden, name="inner_back")
    inner_shape = [sds((length, hidden), BF), sds((1, hidden), F32)]
    first_call = dict(
        scratch=[half_work], mib=5, flops=2 * length * width * (hidden + width), name="first_back"
    )
    first_shape = [
        sds((length, width), F32), sds((length, width), BF), sds((length, width), BF), sds((8, width), F32)
    ]
    def attention_back(gradient, first, pairs):
        step = (length, length)
        return kernel_call(
            functools.partial(attention_back_kernel, first=first),
            [sds((length, 6 * HEAD_DIM * pairs), BF), sds((1, 6 * HEAD_DIM * pairs), F32)],
            [proj, probs, gradient],
            scratch=[pltpu.VMEM((2,) + step, F32)] * 2 + [pltpu.VMEM((2,) + step, BF)] * 2,
            mib=9, flops=16 * pairs * length * length * 256, name=f"attention_back_{first}",
        )

    head_pairs = heads // 2
    split = 2 * head_pairs // 3

    def input_back(left, right):
        return kernel_call(
            input_back_kernel, sds((length, width), BF), [left, right, w_qkv, grad_first],
            scratch=[pltpu.VMEM((length, 3 * width), BF)],
            mib=5, flops=6 * length * width * width, name="input_back",
        )

    if fast:
        share = width // devices
        line = Sequence()

        CORE, X, Z1, Z2 = range(4)

        def grads(*pairs, name, order=(CORE, X, Z1, Z2), pieces=1, at_once=False):
            rows = pairs[0][0].shape[1]
            shape = (devices // 2, rows // devices, sum(right.shape[1] for _, right in pairs))
            args = [member for left, right in pairs for member in (left, line.now(right))]
            outs = kernel_call(
                functools.partial(weight_grad_kernel, order=order, pairs=len(pairs)),
                [sds((2,) + shape, BF)] if at_once
                else [sds(shape, BF)] + [sds((shape[0] // pieces,) + shape[1:], BF)] * pieces,
                [place] + args, smem=1, scratch=[pltpu.VMEM((rows, shape[2]), BF)],
                mib=8, flops=2 * length * rows * shape[2], name=name,
            )
            return line.chunk(outs, pieces=pieces)

        a = grads((act, second_low), name="grad_w_back", order=(CORE, Z1, Z2, X))
        line.go(a, CORE)
        inner_low, sums_in = line.ran(
            kernel_call(inner_back_kernel, inner_shape, [line.now(second_low), w_back, slope], **inner_call)
        )
        line.take(a)
        line.go(a, Z1)
        b = grads((first_low, inner_low), name="grad_w_in", pieces=1)
        line.go(b, CORE)
        grad_first, branch_low, att_grad, sums_one = line.ran(
            kernel_call(
                first_back_kernel, first_shape,
                [line.now(inner_low), w_in, grad_second, n1, r1, ln1_gain, w_out], **first_call
            )
        )
        line.take(b)
        line.go(b, X)
        grad_left, sums_left = line.ran(attention_back(line.now(att_grad), 0, split))
        c = grads((x, grad_left), (attended, branch_low), name="grad_w_qkv_1", pieces=1)
        line.go(c, CORE)
        grad_right, sums_right = line.ran(attention_back(line.now(att_grad), split, head_pairs - split))
        line.take(c, pieces=2)
        line.take(a)
        line.go(a, Z2)
        cols = 6 * HEAD_DIM * (head_pairs - split) + 128
        d = line.chunk(
            kernel_call(
                functools.partial(last_grad_kernel, order=(CORE, X, Z1, Z2)),
                [sds((devices // 2, share, cols), BF)] + [sds((devices // 2 // 1, share, cols), BF)] * 1,
                [place, x, line.now(grad_right), sums_two, sums_one, sums_left, sums_right, sums_in],
                smem=1, scratch=[pltpu.VMEM((width, cols), BF)], mib=5,
                flops=2 * length * width * cols, name="grad_w_qkv_2",
            ),
            extra=128,
        )
        line.go(d, CORE)
        grad_hidden = line.ran([input_back(grad_left, line.now(grad_right))])[0]
        line.take(d)
        line.go(c, X, behind=b)
        line.take(b, pieces=2)
        line.go(b, Z1)
        line.take(a)
        line.go(d, X, behind=c)
        line.take(c, pieces=2)
        line.go(c, Z1)
        line.take(b)
        line.go(b, Z2)
        line.go(a, X, behind=d)
        line.take(d)
        line.go(d, Z1)
        line.take(c)
        line.go(c, Z2)
        share_w_in = line.finish(b)
        line.take(d)
        line.go(d, Z2)
        share_w_back = line.finish(a)
        (
            share_w_qkv, share_w_out, share_bq, share_bv, share_gain2, share_bias2, share_b_back,
            share_gain1, share_bias1, share_b_out, share_b_in,
        ) = kernel_call(
            finish_last_kernel,
            [sds((share, 3 * width), F32), sds((share, width), F32)] + [sds((1, share), F32)] * 8
            + [sds((1, hidden // devices), F32)],
            [c["keep"], line.now(c["came"][0]), d["keep"], d["came"][0]], mib=4, name="finish_last",
        )
    else:
        share_w_back = plain_grad(act, second_low, "grad_w_back")
        inner_low, sums_in = kernel_call(
            inner_back_kernel, inner_shape, [second_low, w_back, slope], **inner_call
        )
        share_w_in = plain_grad(first_low, inner_low, "grad_w_in")
        grad_first, branch_low, att_grad, sums_one = kernel_call(
            first_back_kernel, first_shape, [inner_low, w_in, grad_second, n1, r1, ln1_gain, w_out],
            **first_call
        )
        grad_left, sums_left = attention_back(att_grad, 0, split)
        grad_right, sums_right = attention_back(att_grad, split, head_pairs - split)
        grad_hidden = input_back(grad_left, grad_right)

        def joined(left, right):
            pieces = [jnp.split(half, 3, 1) for half in (left, right)]
            return jnp.concatenate([piece for both in zip(*pieces) for piece in both], 1)

        grad_proj, sums_qkv = joined(grad_left, grad_right), joined(sums_left, sums_right)
        share_w_qkv = plain_grad(x, grad_proj, "grad_w_qkv")
        share_w_out = plain_grad(attended, branch_low, "grad_w_out")

        def scattered(vector):
            return lax.psum_scatter(vector, "dp", scatter_dimension=1, tiled=True)

        share_bq, share_bv = scattered(sums_qkv[:, :width]), scattered(sums_qkv[:, 2 * width :])
        share_gain2, share_bias2, share_b_back = (scattered(sums_two[k : k + 1]) for k in range(3))
        share_gain1, share_bias1, share_b_out = (scattered(sums_one[k : k + 1]) for k in range(3))
        share_b_in = scattered(sums_in)
    return (
        out_hidden[None],
        grad_hidden[None],
        share_w_qkv[None],
        share_bq,
        share_bv,
        share_w_out[None],
        share_b_out,
        share_gain1,
        share_bias1,
        share_w_in[None],
        share_b_in,
        share_w_back[None],
        share_b_back,
        share_gain2,
        share_bias2,
    )


def solution(mesh):
    matrix, vector = P("tower", None, None), P("tower", None)
    rows, spread = P("tower", "dp", None), P("tower", "dp")
    return jax.shard_map(
        shards,
        mesh=mesh,
        in_specs=(
            rows, P("dp", None), P("dp"), rows, matrix, vector, vector, matrix, vector, vector, vector,
            matrix, vector, matrix, vector, vector, vector,
        ),
        out_specs=(
            rows, rows, rows, spread, spread, rows, spread, spread, spread, rows, spread, rows, spread,
            spread, spread,
        ),
        check_vma=False,
    )
```

```python
import functools
import math

import jax
import jax.numpy as jnp
from jax import lax
from jax.experimental import pallas as pl
from jax.experimental.pallas import tpu as pltpu
from jax.sharding import PartitionSpec as P

HEAD_DIM = 64
QLEN = 32
SEGS = 4
PACKET = 24
EPS = 1e-05
BF = jnp.bfloat16
F32 = jnp.float32
TILE = 32

COSTS = {"proj": 3 * 10**9, "cls": 3 * 10**9, "attention": 8 * 10**9, "first": 2 * 10**9, "inner": 6 * 10**9, "second": 4 * 10**9, "first_back": 3 * 10**10, "attention_back_4": 3 * 10**10, "input_back": 3 * 10**10}

VM = pl.BlockSpec(memory_space=pltpu.VMEM)
SM = pl.BlockSpec(memory_space=pltpu.SMEM)
HB = pl.BlockSpec(memory_space=pltpu.HBM)


def nn(a, b):
    return lax.dot_general(a, b, (((1,), (0,)), ((), ())), preferred_element_type=F32)


def nt(a, b):
    return lax.dot_general(a, b, (((1,), (1,)), ((), ())), preferred_element_type=F32)


def tn(a, b):
    return lax.dot_general(a, b, (((0,), (0,)), ((), ())), preferred_element_type=F32)


def kernel_call(body, outs, args, scratch=(), smem=0, hbm=0, mib=32, flops=0, name=None):
    single = not isinstance(outs, (list, tuple))
    shapes = [outs] if single else list(outs)
    result = pl.pallas_call(
        body,
        out_shape=shapes,
        in_specs=[SM] * smem + [VM] * (len(args) - smem - hbm) + [HB] * hbm,
        out_specs=[VM] * len(shapes),
        scratch_shapes=list(scratch),
        compiler_params=pltpu.CompilerParams(vmem_limit_bytes=mib << 20),
        cost_estimate=pl.CostEstimate(flops=COSTS.get(name, 0), bytes_accessed=0, transcendentals=0),
        name=name,
    )(*args)
    return result[0] if single else result


def sds(shape, dtype):
    return jax.ShapeDtypeStruct(shape, dtype)


def fold(value):
    rows, cols = value.shape
    return jnp.sum(value.reshape(rows // 8, 8, cols), 0)


def head_mask(half):
    lane = lax.broadcasted_iota(jnp.int32, (1, 2 * HEAD_DIM), 1)
    return (lane // HEAD_DIM == half).astype(F32).astype(BF)


def normalise(value):
    centred = value - jnp.mean(value, -1, keepdims=True)
    inverse = lax.rsqrt(jnp.mean(centred * centred, -1, keepdims=True) + EPS)
    return centred * inverse, inverse


def norm_back(grad, normed, inverse, gain):
    scaled = grad * gain
    return inverse * (
        scaled
        - jnp.mean(scaled, -1, keepdims=True)
        - normed * jnp.mean(scaled * normed, -1, keepdims=True)
    )


def gelu_pair(value):
    cdf = 0.5 * lax.erf(value * (1.0 / math.sqrt(2.0))) + 0.5
    density = jnp.exp(value * value * -0.5) * (1.0 / math.sqrt(2.0 * math.pi))
    return value * cdf, cdf + value * density


def proj_kernel(x_hbm, w_hbm, bq_hbm, bv_hbm, out, x, w0, w1, w2, bq, bv, sems):
    width = x.shape[1]
    parts = (w0, w1, w2)
    copies = [
        pltpu.make_async_copy(w_hbm.at[:, pl.ds(k * width, width)], parts[k], sems.at[k]) for k in range(3)
    ]
    x_copy = pltpu.make_async_copy(x_hbm, x, sems.at[3])
    bq_copy = pltpu.make_async_copy(bq_hbm, bq, sems.at[4])
    bv_copy = pltpu.make_async_copy(bv_hbm, bv, sems.at[5])
    for copy in (x_copy, copies[1], copies[0], bq_copy, copies[2], bv_copy):
        copy.start()
    x_copy.wait()
    for k in (1, 0, 2):
        copies[k].wait()
        value = nn(x[...], parts[k][...])
        if k == 0:
            bq_copy.wait()
            value = value + bq[...]
        if k == 2:
            bv_copy.wait()
            value = value + bv[...]
        out[:, k * width : (k + 1) * width] = value.astype(BF)


def chosen_rows(tower, seg, count, length):
    row = lax.broadcasted_iota(jnp.int32, (count, 1), 0)
    place = lax.broadcasted_iota(jnp.int32, (count, length), 1)
    start = jnp.sum((seg < row).astype(F32), 1, keepdims=True).astype(jnp.int32)
    wanted = jnp.where(tower == 0, row * QLEN, jnp.where(row < SEGS, start, -1))
    return (place == wanted).astype(F32)


def cls_kernel(place, seg, x, proj, w_out, w_in, w_back, *refs):
    vectors, (cls, *held, sems) = refs[:7], refs[7:]
    copies = [pltpu.make_async_copy(a, b, sems.at[k]) for k, (a, b) in enumerate(zip(vectors, held))]
    for copy in copies:
        copy.start()
    b_out, g1, b1, b_in, b_back, g2, b2 = held
    length, width = x.shape
    count = cls.shape[0]
    heads = width // HEAD_DIM
    tower = place[0]
    pick = chosen_rows(tower, seg[...], count, length)
    pick_low = pick.astype(BF)
    x_cls = nn(pick_low, x[...])
    q_cls = (nn(pick_low, proj[:, :width]) * (1.0 / math.sqrt(HEAD_DIM))).astype(BF)
    place_row = lax.broadcasted_iota(jnp.int32, (1, length), 1)
    own_seg = jnp.where(tower == 0, place_row // QLEN, seg[...])
    row = lax.broadcasted_iota(jnp.int32, (count, 1), 0)
    bias = jnp.where(own_seg == row, 0.0, -1e9)
    lane_head = lax.broadcasted_iota(jnp.int32, (1, width), 1) // HEAD_DIM
    spread = jnp.concatenate(
        [q_cls * (lane_head == h).astype(F32).astype(BF) for h in range(heads)], 0
    )
    scores = nt(spread, proj[:, width : 2 * width]) + jnp.concatenate([bias] * heads, 0)
    shifted = jnp.exp(scores - jnp.max(scores, -1, keepdims=True))
    probs = (shifted / jnp.sum(shifted, -1, keepdims=True)).astype(BF)
    mixed = nn(probs, proj[:, 2 * width :])
    attended = jnp.zeros((count, width), F32)
    for h in range(heads):
        attended = attended + jnp.where(lane_head == h, mixed[h * count : (h + 1) * count], 0.0)
    for copy in copies:
        copy.wait()
    first = x_cls + (nn(attended.astype(BF), w_out[...]) + b_out[...])
    normed = normalise(first)[0] * g1[...] + b1[...]
    inner = nn(normed.astype(BF), w_in[...]) + b_in[...]
    act = gelu_pair(inner)[0].astype(BF)
    second = normed + (nn(act, w_back[...]) + b_back[...])
    final = normalise(second)[0] * g2[...] + b2[...]
    cls[...] = final.astype(BF)


def attention_kernel(place, seg_row, seg_col, proj, attended, probs, bias, *work):
    length = proj.shape[0]
    width = proj.shape[1] // 3
    tower = place[0]
    lane = lax.broadcasted_iota(jnp.int32, (1, length), 1)
    sub = lax.broadcasted_iota(jnp.int32, (length, 1), 0)
    row_seg = jnp.where(tower == 0, lane // QLEN, seg_row[...])
    col_seg = jnp.where(tower == 0, sub // QLEN, seg_col[...])
    bias[...] = jnp.where(col_seg == row_seg, 0.0, -1e9)
    masks = [head_mask(0), head_mask(1)]
    scale = jnp.asarray(1.0 / math.sqrt(HEAD_DIM), BF)
    step = 2 * HEAD_DIM
    pairs = width // step
    work_a, work_b = work

    def columns(part, pair):
        return proj[:, pl.ds(pl.multiple_of(part * width + pair * step, step), step)]

    def scores(pair, ref):
        queries, keys = columns(0, pair) * scale, columns(1, pair)
        for half in range(2):
            ref[half] = nt(queries * masks[half], keys)

    def soften(pair, ref):
        for half in range(2):
            for r in range(0, length, TILE):
                value = ref[half, r : r + TILE, :] + bias[r : r + TILE, :]
                shifted = jnp.exp(value - jnp.max(value, -1, keepdims=True))
                total = jnp.sum(shifted, -1, keepdims=True)
                probs[2 * pair + half, r : r + TILE, :] = (shifted * (1.0 / total)).astype(BF)

    def mix(pair):
        values = columns(2, pair)
        mixed = nn(probs[2 * pair], values * masks[0]) + nn(probs[2 * pair + 1], values * masks[1])
        attended[:, pl.ds(pl.multiple_of(pair * step, step), step)] = mixed.astype(BF)

    def two_pairs(k, carry):
        pair = 2 * k
        scores(pair + 1, work_b)
        soften(pair, work_a)
        scores(jnp.minimum(pair + 2, pairs - 1), work_a)
        mix(pair)
        soften(pair + 1, work_b)
        mix(pair + 1)
        return carry

    scores(0, work_a)
    lax.fori_loop(0, pairs // 2, two_pairs, 0)


def first_kernel(x, attended, w_out, b_out, g1, b1, n1, r1, low, work):
    work[...] = nn(attended[...], w_out[...])
    def step(i, carry):
        rows = pl.ds(pl.multiple_of(i * TILE, TILE), TILE)
        first = x[rows, :].astype(F32) + (work[rows, :] + b_out[...])
        normed, inverse = normalise(first)
        n1[rows, :] = normed
        r1[rows, :] = inverse
        low[rows, :] = (normed * g1[...] + b1[...]).astype(BF)
        return carry

    lax.fori_loop(0, x.shape[0] // TILE, step, 0, unroll=4)


def inner_kernel(low, w_in, b_in, act, slope, work_a, work_b):
    length = low.shape[0]
    block = work_a.shape[1]
    blocks = w_in.shape[1] // block

    def columns(i):
        return pl.ds(pl.multiple_of(i * block, block), block)

    def gelu_block(i, work):
        bias = b_in[:, columns(i)]
        for r in range(0, length, TILE):
            value, grad = gelu_pair(work[r : r + TILE, :] + bias)
            act[r : r + TILE, columns(i)] = value.astype(BF)
            slope[r : r + TILE, columns(i)] = grad.astype(BF)

    work_a[...] = nn(low[...], w_in[:, :block])

    def step(k, carry):
        i = 2 * k
        work_b[...] = nn(low[...], w_in[:, columns(i + 1)])
        gelu_block(i, work_a)
        work_a[...] = nn(low[...], w_in[:, columns(jnp.minimum(i + 2, blocks - 1))])
        gelu_block(i + 1, work_b)
        return carry

    lax.fori_loop(0, blocks // 2, step, 0)


def second_kernel(act, w_back, b_back, n1, g1, b1, g2, b2, n2, r2, out, work):
    part = work.shape[0]

    def normalise_part(k, carry):
        at = pl.multiple_of(k * part, part)
        work[...] = nn(act[pl.ds(at, part), :], w_back[...])
        for r in range(0, part, TILE):
            rows = pl.ds(pl.multiple_of(at + r, TILE), TILE)
            branch = work[r : r + TILE, :] + b_back[...]
            second = (n1[rows, :] * g1[...] + b1[...]) + branch
            normed, inverse = normalise(second)
            n2[rows, :] = normed
            r2[rows, :] = inverse
            out[rows, :] = (normed * g2[...] + b2[...]).astype(BF)
        return carry

    lax.fori_loop(0, act.shape[0] // part, normalise_part, 0)


def packet_kernel(place, cls, other, labels, out):
    query = place[0] == 0
    count, width = cls.shape
    mine, came = cls[...].astype(F32), other[...].astype(F32)
    q_rows = jnp.where(query, mine, came)
    p_rows = jnp.where(query, came, mine)[:SEGS]
    value = labels[...]
    gap = jnp.zeros((1, 128 - count), F32)
    row = jnp.concatenate(
        [(value >> 8).astype(F32), gap, (value & 255).astype(F32), gap, jnp.zeros((1, width - 256), F32)], 1
    )
    rest = jnp.zeros((PACKET - count - SEGS - 1, width), F32)
    out[...] = jnp.concatenate([q_rows, p_rows, row, rest], 0).astype(BF)


def loss_kernel(place, near, far, grad, *, order, count):
    tower, me = place[0], place[1]
    packets = jnp.concatenate([near[...], far[...]], 0)
    total, width = packets.shape
    scale = 2.0 / math.sqrt(width)
    row = lax.broadcasted_iota(jnp.int32, (total, 1), 0)
    col = lax.broadcasted_iota(jnp.int32, (1, total), 1)
    col_slot, col_part = col // PACKET, col % PACKET
    mixed = jnp.zeros_like(col)
    for j, b in enumerate(order):
        mixed = mixed | (((col_slot >> j) & 1) << b)
    is_passage = jnp.logical_and(col_part >= count, col_part < count + SEGS)
    number = jnp.where(is_passage, (mixed ^ me) * SEGS + (col_part - count), -1)
    label_of = ((row // PACKET) * PACKET + (count + SEGS) == col).astype(F32).astype(BF)
    label_rows = nn(label_of, packets[:, :256])
    lane = lax.broadcasted_iota(jnp.int32, (1, 256), 1)
    part = row % PACKET
    weight = jnp.where(lane == part, 256.0, 0.0) + jnp.where(lane == part + 128, 1.0, 0.0)
    label = jnp.sum(label_rows * weight, 1, keepdims=True).astype(jnp.int32)
    logits = jnp.where(is_passage, nt(packets, packets) * scale, -1e30)
    soft = jnp.exp(logits - jnp.max(logits, -1, keepdims=True))
    soft = soft / jnp.sum(soft, -1, keepdims=True)
    grad_logits = soft - (number == label).astype(F32)
    grad_logits = grad_logits * (part < count).astype(F32)
    wide = packets.astype(F32)
    grad_q = jnp.dot(
        grad_logits[:count], wide, precision=lax.Precision.HIGHEST, preferred_element_type=F32
    )
    pick = lax.broadcasted_iota(jnp.int32, (count, 1), 0)
    pick = jnp.logical_and(pick + count == col, pick < SEGS).astype(F32)
    turned = lax.dot_general(
        pick, grad_logits, (((1,), (1,)), ((), ())),
        precision=lax.Precision.HIGHEST, preferred_element_type=F32,
    )
    grad_p = jnp.dot(turned, wide, precision=lax.Precision.HIGHEST, preferred_element_type=F32)
    grad[...] = jnp.where(tower == 0, grad_q, grad_p) * scale


def plain_loss(packets, tower, me, count):
    devices, _, width = packets.shape
    scale = 2.0 / math.sqrt(width)
    queries = packets[:, :count].reshape(devices * count, width)
    passages = packets[:, count : count + SEGS].reshape(devices * SEGS, width)
    row = packets[:, count + SEGS].astype(jnp.int32)
    label = (row[:, :count] * 256 + row[:, 128 : 128 + count]).reshape(devices * count, 1)
    soft = jax.nn.softmax(nt(queries, passages) * scale, -1)
    grad = soft - (label == jnp.arange(devices * SEGS, dtype=jnp.int32)).astype(F32)
    grad_q = lax.dynamic_slice_in_dim(grad, me * count, count, 0)
    grad_q = jnp.dot(grad_q, passages.astype(F32), precision=lax.Precision.HIGHEST)
    grad_p = lax.dynamic_slice_in_dim(grad, me * SEGS, SEGS, 1)
    grad_p = jnp.dot(grad_p.T, queries.astype(F32), precision=lax.Precision.HIGHEST)
    grad_p = jnp.pad(grad_p, ((0, count - SEGS), (0, 0)))
    return jnp.where(tower == 0, grad_q, grad_p) * scale


def split_three(value):
    high = value.astype(BF)
    rest = value - high.astype(F32)
    middle = rest.astype(BF)
    return jnp.concatenate([high, middle, (rest - middle.astype(F32)).astype(BF)], 0)


def norm_back_rows(rows, grad, normed, inverse, gain, out, low, totals):
    back = norm_back(grad, normed[rows, :], inverse[rows, :], gain[...])
    out[rows, :] = back
    back_low = back.astype(BF)
    low[rows, :] = back_low
    parts = (fold(grad * normed[rows, :]), fold(grad), fold(back_low.astype(F32)))
    return parts if totals is None else tuple(a + b for a, b in zip(totals, parts))


def second_back_kernel(place, seg, out_grad, cls_grad, n2, r2, g2, grad, low, sums, work):
    length, width = out_grad.shape
    count = cls_grad.shape[0]
    pick = chosen_rows(place[0], seg[...], count, length).astype(BF)
    work[...] = tn(jnp.concatenate([pick] * 3, 0), split_three(cls_grad[...]))
    totals = None
    for r in range(0, length, TILE):
        rows = slice(r, r + TILE)
        final = out_grad[rows, :].astype(F32) + work[rows, :]
        totals = norm_back_rows(rows, final, n2, r2, g2, grad, low, totals)
    for k, part in enumerate(totals):
        sums[k : k + 1, :] = jnp.sum(part, 0, keepdims=True)


def inner_back_kernel(low, w_back, slope, out, sums):
    block = 256

    def step(i, carry):
        cols = pl.ds(pl.multiple_of(i * block, block), block)
        value = (nt(low[...], w_back[cols, :]) * slope[:, cols].astype(F32)).astype(BF)
        out[:, cols] = value
        sums[:, cols] = jnp.sum(value.astype(F32), 0, keepdims=True)
        return carry

    lax.fori_loop(0, w_back.shape[0] // block, step, 0, unroll=4)


def first_back_kernel(inner, w_in, grad_second, n1, r1, g1, w_out, grad, low, att, sums, work_a, work_b):
    length, width = grad_second.shape
    part = length // 2
    works = (work_a, work_b)
    for k in range(2):
        works[k][...] = nt(inner[k * part : (k + 1) * part, :], w_in[...])
    totals = None
    for k in range(2):
        for r in range(0, part, TILE):
            rows = slice(k * part + r, k * part + r + TILE)
            value = grad_second[rows, :] + works[k][r : r + TILE, :]
            totals = norm_back_rows(rows, value, n1, r1, g1, grad, low, totals)
        rows = slice(k * part, (k + 1) * part)
        att[rows, :] = nt(low[rows, :], w_out[...]).astype(BF)
    for k, total in enumerate(totals):
        sums[k : k + 1, :] = jnp.sum(total, 0, keepdims=True)


def attention_back_kernel(proj, probs, att_grad, out, sums, dp_a, dp_b, ds_a, ds_b, *, first):
    length = proj.shape[0]
    width = proj.shape[1] // 3
    own = out.shape[1] // 3
    masks = [head_mask(0), head_mask(1)]
    scale = 1.0 / math.sqrt(HEAD_DIM)
    step = 2 * HEAD_DIM
    pairs = own // step

    def columns(part, pair):
        return proj[:, pl.ds(pl.multiple_of(part * width + (first + pair) * step, step), step)]

    def grad_columns(pair):
        return att_grad[:, pl.ds(pl.multiple_of((first + pair) * step, step), step)]

    def grad_probs(pair, dp):
        grads, values = grad_columns(pair), columns(2, pair)
        for half in range(2):
            dp[half] = nt(grads * masks[half], values)

    def grad_scores(pair, dp, ds):
        for half in range(2):
            for r in range(0, length, TILE):
                wide = probs[2 * (first + pair) + half, r : r + TILE, :].astype(F32)
                grad = dp[half, r : r + TILE, :]
                delta = jnp.sum(grad * wide, -1, keepdims=True)
                ds[half, r : r + TILE, :] = (wide * (grad - delta)).astype(BF)

    def results(pair, ds):
        queries_t, grads_t = columns(0, pair).T, grad_columns(pair).T
        keys = columns(1, pair)
        grad_q, grad_k_t, grad_v_t = None, [], []
        for half in range(2):
            scores = ds[half]
            lanes = slice(half * HEAD_DIM, (half + 1) * HEAD_DIM)
            grad_v_t.append(nn(grads_t[lanes], probs[2 * (first + pair) + half]))
            grad_k_t.append(nn(queries_t[lanes], scores))
            term = nn(scores, keys * masks[half])
            grad_q = term if grad_q is None else grad_q + term
        parts = (
            grad_q * scale,
            jnp.concatenate(grad_k_t, 0).T * scale,
            jnp.concatenate(grad_v_t, 0).T,
        )
        for k, part in enumerate(parts):
            cols = pl.ds(pl.multiple_of(k * own + pair * step, step), step)
            part_low = part.astype(BF)
            out[:, cols] = part_low
            sums[:, cols] = jnp.sum(part_low.astype(F32), 0, keepdims=True)

    def two_pairs(k, carry):
        pair = 2 * k
        grad_probs(pair + 1, dp_b)
        grad_scores(pair, dp_a, ds_a)
        grad_probs(jnp.minimum(pair + 2, pairs - 1), dp_a)
        results(pair, ds_a)
        grad_scores(pair + 1, dp_b, ds_b)
        results(pair + 1, ds_b)
        return carry

    grad_probs(0, dp_a)
    lax.fori_loop(0, pairs // 2, two_pairs, 0)


def input_back_kernel(left, right, w_qkv, grad_first, out, work):
    width = out.shape[1]
    for k in range(3):
        at = k * width
        for part in (left, right):
            own = part.shape[1] // 3
            work[:, at : at + own] = part[:, k * own : (k + 1) * own]
            at += own
    block = 256
    for i in range(width // block):
        cols = slice(i * block, (i + 1) * block)
        value = grad_first[:, cols] + nt(work[...], w_qkv[cols, :])
        out[:, cols] = value.astype(BF)


def slot_device(me, order, slot):
    mixed = 0
    for j, b in enumerate(order):
        mixed = mixed | (((slot >> (len(order) - 1 - j)) & 1) << b)
    return me ^ mixed


def spread_shares(place, work, outs, order):
    me = place[1]
    if len(outs) == 1:
        outs = (outs[0].at[0], outs[0].at[1])
        me = me & ~(1 << order[0])
    keep, *sends = outs
    half, share, _ = keep.shape
    for slot in range(2 * half):
        ref, at = (keep, slot) if slot < half else piece_of(sends, slot - half)
        device = slot_device(me, order, slot)
        ref[at] = work[pl.ds(pl.multiple_of(device * share, 16), share), :]


def piece_of(refs, slot):
    size = refs[0].shape[0]
    return refs[slot // size], slot % size


def weight_grad_kernel(place, *refs, order, pairs):
    *outs, work = refs[2 * pairs :]
    block = 768

    def run(i):
        return pl.ds(pl.multiple_of(i * block, block), block)

    at = 0
    for left, right in zip(refs[: 2 * pairs : 2], refs[1 : 2 * pairs : 2]):
        rows, cols = left.shape[1], right.shape[1]

        def by_rows(i, carry, left=left, right=right, at=at, cols=cols):
            work[run(i), at : at + cols] = tn(left[:, run(i)], right[...]).astype(BF)
            return carry

        def by_columns(i, carry, left=left, right=right, at=at):
            there = pl.ds(pl.multiple_of(at + i * block, 128), block)
            work[:, there] = tn(left[...], right[:, run(i)]).astype(BF)
            return carry

        if rows > block:
            lax.fori_loop(0, rows // block, by_rows, 0)
        else:
            lax.fori_loop(0, cols // block, by_columns, 0)
        at += cols
    spread_shares(place, work, outs, order)


def last_grad_kernel(
    place, x, grad_proj, sums_two, sums_one, sums_left, sums_right, sums_in, *refs, order
):
    *outs, work = refs
    width = x.shape[1]
    share = outs[0].shape[1]
    devices = 2 * outs[0].shape[0]
    wide = grad_proj.shape[1]
    work[:, :wide] = tn(x[...], grad_proj[...]).astype(BF)
    extra = slice(wide, wide + 128)
    thirds = [sums.shape[1] // 3 for sums in (sums_left, sums_right)]
    query, value = (
        jnp.concatenate(
            [sums[:, k * own : (k + 1) * own] for sums, own in zip((sums_left, sums_right), thirds)], 1
        )
        for k in (0, 2)
    )
    stacked = jnp.concatenate([query, value, sums_two[0:3], sums_one[0:3]], 0)
    work[:, extra] = jnp.zeros((width, 128), BF)
    in_share = sums_in.shape[1] // devices
    for d in range(devices):
        rows = [stacked[:, d * share : (d + 1) * share]]
        for k in range(in_share // share):
            at = d * in_share + k * share
            rows.append(sums_in[:, at : at + share])
        rows.append(jnp.zeros((16 - 8 - in_share // share, share), F32))
        block = jnp.concatenate(rows, 0)
        block = jnp.concatenate([block, jnp.zeros((16, 128 - share), F32)], 1)
        high = block.astype(BF)
        work[d * share : d * share + 16, extra] = high
        work[d * share + 16 : d * share + 32, extra] = (block - high.astype(F32)).astype(BF)
    spread_shares(place, work, outs, order)


def add_extra(left, right):
    total = (
        left[0:16].astype(F32) + left[16:32].astype(F32) + right[0:16].astype(F32) + right[16:32].astype(F32)
    )
    return total


def halve_kernel(*refs, cames, extra):
    kept, came, (keep, *sends) = refs[0], refs[1 : 1 + cames], refs[1 + cames :]
    half = keep.shape[0]
    cols = keep.shape[2] - extra
    for slot in range(2 * half):
        ref, at = (keep, slot) if slot < half else piece_of(sends, slot - half)
        other, there = piece_of(came, slot)
        ref[at, :, :cols] = (kept[slot, :, :cols].astype(F32) + other[there, :, :cols].astype(F32)).astype(BF)
        if extra:
            total = add_extra(kept[slot, :, cols:], other[there, :, cols:])
            high = total.astype(BF)
            ref[at, 0:16, cols:] = high
            ref[at, 16:32, cols:] = (total - high.astype(F32)).astype(BF)
            ref[at, 32:, cols:] = jnp.zeros((keep.shape[1] - 32, extra), BF)


def halve_cores_kernel(both, *outs, extra):
    halve_kernel(both.at[0], both.at[1], *outs, cames=1, extra=extra)


def finish_kernel(kept, came, out):
    out[...] = kept[0].astype(F32) + came[0].astype(F32)


def finish_last_kernel(
    kept, came, kept_last, came_last, w_qkv, w_out, bq, bv, gain2, bias2, b_back, gain1, bias1, b_out, b_in
):
    width = w_out.shape[1]
    share = bq.shape[1]
    left, right = (kept.shape[2] - width) // 3, (kept_last.shape[2] - 128) // 3
    for k in range(3):
        at = k * width
        cols = slice(k * left, (k + 1) * left)
        w_qkv[:, at : at + left] = kept[0, :, cols].astype(F32) + came[0, :, cols].astype(F32)
        cols = slice(k * right, (k + 1) * right)
        w_qkv[:, at + left : at + width] = kept_last[0, :, cols].astype(F32) + came_last[0, :, cols].astype(F32)
    w_out[...] = kept[0, :, 3 * left :].astype(F32) + came[0, :, 3 * left :].astype(F32)
    vectors = add_extra(kept_last[0, :, 3 * right :], came_last[0, :, 3 * right :])
    for k, ref in enumerate((bq, bv, gain2, bias2, b_back, gain1, bias1, b_out)):
        ref[...] = vectors[k : k + 1, :share]
    pieces = b_in.shape[1] // share
    b_in[...] = jnp.concatenate([vectors[8 + k : 9 + k, :share] for k in range(pieces)], 1)


def plain_grad_kernel(left, right, out):
    out[...] = tn(left[...], right[...])


def swapped(value, axis, mask):
    count = lax.axis_size(axis)
    return lax.ppermute(value, axis, [(i, i ^ mask) for i in range(count)])


class Sequence:
    def __init__(self):
        self.last = None

    def now(self, value):
        return value if self.last is None else after(value, self.last)

    def ran(self, results):
        self.last = results[0]
        return results

    def chunk(self, outs, extra=0, pieces=1):
        chunk = {"extra": extra}
        if len(outs) > 1:
            chunk["keep"], *chunk["sends"] = self.ran(outs)
        else:
            pairs = [[i, i + 1] for i in range(0, lax.axis_size("dp"), 2)]
            both = lax.all_to_all(outs[0], "dp", 0, 0, tiled=True, axis_index_groups=pairs)
            self.last = both
            self.parted(chunk, functools.partial(halve_cores_kernel, extra=extra), [both], both.shape[1:], pieces)
        return chunk

    def parted(self, chunk, body, args, shape, pieces):
        half = sds((shape[0] // 2,) + shape[1:], BF)
        piece = sds((shape[0] // 2 // pieces,) + shape[1:], BF)
        chunk["keep"], *chunk["sends"] = self.ran(
            kernel_call(body, [half] + [piece] * pieces, args, mib=4, name="halve")
        )

    def go(self, chunk, bit, behind=None):
        sends = [self.now(send) for send in chunk["sends"]]
        if behind is not None:
            sends = [after(send, *behind["came"]) for send in sends]
        chunk["came"] = [swapped(send, "dp", 1 << bit) for send in sends]

    def take(self, chunk, pieces=1):
        keep, came = chunk["keep"], [self.now(value) for value in chunk["came"]]
        body = functools.partial(halve_kernel, cames=len(came), extra=chunk["extra"])
        self.parted(chunk, body, [keep] + came, keep.shape, pieces)

    def finish(self, chunk):
        args = [chunk["keep"], self.now(chunk["came"][0])]
        return self.ran([kernel_call(finish_kernel, sds(args[0].shape[1:], F32), args, mib=4, name="finish")])[0]


def after(value, *earlier):
    return lax.optimization_barrier((value,) + earlier)[0]


def shards(
    hidden_in,
    seg_ids,
    labels,
    out_grad,
    w_qkv,
    b_query,
    b_value,
    w_out,
    b_out,
    ln1_gain,
    ln1_bias,
    w_in,
    b_in,
    w_back,
    b_back,
    ln2_gain,
    ln2_bias,
):
    x, cotangent = hidden_in[0], out_grad[0]
    w_qkv, w_out, w_in, w_back = w_qkv[0], w_out[0], w_in[0], w_back[0]
    length, width = x.shape
    hidden = w_in.shape[1]
    heads = width // HEAD_DIM
    count = length // QLEN
    devices = lax.axis_size("dp")
    bits = devices.bit_length() - 1
    tower, me = lax.axis_index("tower"), lax.axis_index("dp")
    place = jnp.stack([tower, me]).astype(jnp.int32)
    seg_col = seg_ids.reshape(length, 1)
    fast = devices == 16

    proj = kernel_call(
        proj_kernel, sds((length, 3 * width), BF),
        [pltpu.with_memory_space_constraint(member, pltpu.HBM) for member in (x, w_qkv, b_query, b_value)], hbm=4,
        scratch=[pltpu.VMEM((length, width), BF)] + [pltpu.VMEM((width, width), BF)] * 3
        + [pltpu.VMEM((1, width), F32)] * 2 + [pltpu.SemaphoreType.DMA((6,))],
        mib=8, flops=2 * length * 3 * width * width, name="proj",
    )
    cls = kernel_call(
        cls_kernel, sds((count, width), BF),
        [place, seg_ids, x, proj, w_out, w_in, w_back] + [
            pltpu.with_memory_space_constraint(member, pltpu.HBM)
            for member in (b_out, ln1_gain, ln1_bias, b_in, b_back, ln2_gain, ln2_bias)
        ],
        hbm=7,
        scratch=[pltpu.VMEM((1, width), F32)] * 3 + [pltpu.VMEM((1, hidden), F32)]
        + [pltpu.VMEM((1, width), F32)] * 3 + [pltpu.SemaphoreType.DMA((7,))],
        smem=1, mib=3, flops=2 * 256 * width * hidden * 2, name="cls",
    )
    other = swapped(cls, "tower", 1)
    attended, probs = kernel_call(
        attention_kernel, [sds((length, width), BF), sds((heads, length, length), BF)],
        [place, seg_ids, seg_col, after(proj, cls)], smem=1,
        scratch=[pltpu.VMEM((length, length), F32)] + [pltpu.VMEM((2, length, length), F32)] * 2,
        mib=9, flops=4 * heads * length * length * 256, name="attention",
    )
    held = kernel_call(
        packet_kernel, sds((PACKET, width), BF), [place, cls, after(other, attended), labels[None]],
        smem=1, mib=1, name="packet",
    )
    order = [3, 2, 1, 0] if fast else list(range(bits))
    if fast:
        came = swapped(held, "dp", 1 << order[0])
    work, half_work = pltpu.VMEM((length, width), F32), pltpu.VMEM((length // 2, width), F32)
    n1, r1, first_low = kernel_call(
        first_kernel,
        [sds((length, width), F32), sds((length, 1), F32), sds((length, width), BF)],
        [x, after(attended, held), w_out, b_out, ln1_gain, ln1_bias], scratch=[work],
        mib=4, flops=2 * length * width * width, name="first",
    )
    if fast:
        held = jnp.concatenate([held, after(came, first_low)], 0)
        came = swapped(held, "dp", 1 << order[1])
    act, slope = kernel_call(
        inner_kernel, [sds((length, hidden), BF), sds((length, hidden), BF)],
        [after(first_low, held), w_in, b_in], scratch=[pltpu.VMEM((length, 256), F32)] * 2,
        mib=4, flops=8 * length * width * hidden, name="inner",
    )
    if fast:
        held = jnp.concatenate([held, after(came, act)], 0)
        came = swapped(held, "dp", 1 << order[2])
    n2, r2, out_hidden = kernel_call(
        second_kernel,
        [sds((length, width), F32), sds((length, 1), F32), sds((length, width), BF)],
        [after(act, held), w_back, b_back, n1, ln1_gain, ln1_bias, ln2_gain, ln2_bias], scratch=[half_work],
        mib=5, flops=2 * length * width * hidden, name="second",
    )
    if fast:
        near = jnp.concatenate([held, after(came, out_hidden)], 0)
        far = swapped(near, "dp", 1 << order[3])
        cls_grad = kernel_call(
            functools.partial(loss_kernel, order=order, count=count), sds((count, width), F32),
            [place, near, far], smem=1,
            mib=5, flops=8 * devices * count * devices * SEGS * width, name="loss",
        )
    else:
        packets = lax.all_gather(held, "dp", axis=0)
        cls_grad = plain_loss(packets, tower, me, count)

    grad_second, second_low, sums_two = kernel_call(
        second_back_kernel,
        [sds((length, width), F32), sds((length, width), BF), sds((8, width), F32)],
        [place, seg_ids, cotangent, cls_grad, n2, r2, ln2_gain], smem=1, scratch=[work],
        mib=4, flops=2 * length * width * 256, name="second_back",
    )

    def plain_grad(left, right, name):
        rows, cols = left.shape[1], right.shape[1]
        whole = kernel_call(
            plain_grad_kernel, sds((rows, cols), F32), [left, right], mib=24,
            flops=2 * length * rows * cols, name=name,
        )
        return lax.psum_scatter(whole, "dp", scatter_dimension=0, tiled=True)

    inner_call = dict(mib=3, flops=2 * length * width * hidden, name="inner_back")
    inner_shape = [sds((length, hidden), BF), sds((1, hidden), F32)]
    first_call = dict(
        scratch=[half_work] * 2, mib=5, flops=2 * length * width * (hidden + width), name="first_back"
    )
    first_shape = [
        sds((length, width), F32), sds((length, width), BF), sds((length, width), BF), sds((8, width), F32)
    ]
    def attention_back(gradient, first, pairs):
        step = (length, length)
        return kernel_call(
            functools.partial(attention_back_kernel, first=first),
            [sds((length, 6 * HEAD_DIM * pairs), BF), sds((1, 6 * HEAD_DIM * pairs), F32)],
            [proj, probs, gradient],
            scratch=[pltpu.VMEM((2,) + step, F32)] * 2 + [pltpu.VMEM((2,) + step, BF)] * 2,
            mib=9, flops=16 * pairs * length * length * 256, name=f"attention_back_{first}",
        )

    head_pairs = heads // 2
    split = 2 * head_pairs // 3

    def input_back(left, right):
        return kernel_call(
            input_back_kernel, sds((length, width), BF), [left, right, w_qkv, grad_first],
            scratch=[pltpu.VMEM((length, 3 * width), BF)],
            mib=5, flops=6 * length * width * width, name="input_back",
        )

    if fast:
        share = width // devices
        line = Sequence()

        CORE, X, Z1, Z2 = range(4)

        def grads(*pairs, name, order=(CORE, X, Z1, Z2), pieces=1, at_once=False):
            rows = pairs[0][0].shape[1]
            shape = (devices // 2, rows // devices, sum(right.shape[1] for _, right in pairs))
            args = [member for left, right in pairs for member in (left, line.now(right))]
            outs = kernel_call(
                functools.partial(weight_grad_kernel, order=order, pairs=len(pairs)),
                [sds((2,) + shape, BF)] if at_once
                else [sds(shape, BF)] + [sds((shape[0] // pieces,) + shape[1:], BF)] * pieces,
                [place] + args, smem=1, scratch=[pltpu.VMEM((rows, shape[2]), BF)],
                mib=8, flops=2 * length * rows * shape[2], name=name,
            )
            return line.chunk(outs, pieces=pieces)

        a = grads((act, second_low), name="grad_w_back", order=(CORE, Z1, Z2, X))
        line.go(a, CORE)
        inner_low, sums_in = line.ran(
            kernel_call(inner_back_kernel, inner_shape, [line.now(second_low), w_back, slope], **inner_call)
        )
        line.take(a)
        line.go(a, Z1)
        b = grads((first_low, inner_low), name="grad_w_in", pieces=1)
        line.go(b, CORE)
        grad_first, branch_low, att_grad, sums_one = line.ran(
            kernel_call(
                first_back_kernel, first_shape,
                [line.now(inner_low), w_in, grad_second, n1, r1, ln1_gain, w_out], **first_call
            )
        )
        line.take(b)
        line.go(b, X)
        grad_left, sums_left = line.ran(attention_back(line.now(att_grad), 0, split))
        c = grads((x, grad_left), (attended, branch_low), name="grad_w_qkv_1", pieces=1)
        line.go(c, CORE)
        grad_right, sums_right = line.ran(attention_back(line.now(att_grad), split, head_pairs - split))
        line.take(c, pieces=2)
        line.take(a)
        line.go(a, Z2)
        cols = 6 * HEAD_DIM * (head_pairs - split) + 128
        d = line.chunk(
            kernel_call(
                functools.partial(last_grad_kernel, order=(CORE, X, Z1, Z2)),
                [sds((devices // 2, share, cols), BF)] + [sds((devices // 2 // 1, share, cols), BF)] * 1,
                [place, x, line.now(grad_right), sums_two, sums_one, sums_left, sums_right, sums_in],
                smem=1, scratch=[pltpu.VMEM((width, cols), BF)], mib=5,
                flops=2 * length * width * cols, name="grad_w_qkv_2",
            ),
            extra=128,
        )
        line.go(d, CORE)
        grad_hidden = line.ran([input_back(grad_left, line.now(grad_right))])[0]
        line.take(d)
        line.go(c, X, behind=b)
        line.take(b, pieces=2)
        line.go(b, Z1)
        line.take(a)
        line.go(d, X, behind=c)
        line.take(c, pieces=2)
        line.go(c, Z1)
        line.take(b)
        line.go(b, Z2)
        line.go(a, X, behind=d)
        line.take(d)
        line.go(d, Z1)
        line.take(c)
        line.go(c, Z2)
        share_w_in = line.finish(b)
        line.take(d)
        line.go(d, Z2)
        share_w_back = line.finish(a)
        (
            share_w_qkv, share_w_out, share_bq, share_bv, share_gain2, share_bias2, share_b_back,
            share_gain1, share_bias1, share_b_out, share_b_in,
        ) = kernel_call(
            finish_last_kernel,
            [sds((share, 3 * width), F32), sds((share, width), F32)] + [sds((1, share), F32)] * 8
            + [sds((1, hidden // devices), F32)],
            [c["keep"], line.now(c["came"][0]), d["keep"], d["came"][0]], mib=4, name="finish_last",
        )
    else:
        share_w_back = plain_grad(act, second_low, "grad_w_back")
        inner_low, sums_in = kernel_call(
            inner_back_kernel, inner_shape, [second_low, w_back, slope], **inner_call
        )
        share_w_in = plain_grad(first_low, inner_low, "grad_w_in")
        grad_first, branch_low, att_grad, sums_one = kernel_call(
            first_back_kernel, first_shape, [inner_low, w_in, grad_second, n1, r1, ln1_gain, w_out],
            **first_call
        )
        grad_left, sums_left = attention_back(att_grad, 0, split)
        grad_right, sums_right = attention_back(att_grad, split, head_pairs - split)
        grad_hidden = input_back(grad_left, grad_right)

        def joined(left, right):
            pieces = [jnp.split(half, 3, 1) for half in (left, right)]
            return jnp.concatenate([piece for both in zip(*pieces) for piece in both], 1)

        grad_proj, sums_qkv = joined(grad_left, grad_right), joined(sums_left, sums_right)
        share_w_qkv = plain_grad(x, grad_proj, "grad_w_qkv")
        share_w_out = plain_grad(attended, branch_low, "grad_w_out")

        def scattered(vector):
            return lax.psum_scatter(vector, "dp", scatter_dimension=1, tiled=True)

        share_bq, share_bv = scattered(sums_qkv[:, :width]), scattered(sums_qkv[:, 2 * width :])
        share_gain2, share_bias2, share_b_back = (scattered(sums_two[k : k + 1]) for k in range(3))
        share_gain1, share_bias1, share_b_out = (scattered(sums_one[k : k + 1]) for k in range(3))
        share_b_in = scattered(sums_in)
    return (
        out_hidden[None],
        grad_hidden[None],
        share_w_qkv[None],
        share_bq,
        share_bv,
        share_w_out[None],
        share_b_out,
        share_gain1,
        share_bias1,
        share_w_in[None],
        share_b_in,
        share_w_back[None],
        share_b_back,
        share_gain2,
        share_bias2,
    )


def solution(mesh):
    matrix, vector = P("tower", None, None), P("tower", None)
    rows, spread = P("tower", "dp", None), P("tower", "dp")
    return jax.shard_map(
        shards,
        mesh=mesh,
        in_specs=(
            rows, P("dp", None), P("dp"), rows, matrix, vector, vector, matrix, vector, vector, vector,
            matrix, vector, matrix, vector, vector, vector,
        ),
        out_specs=(
            rows, rows, rows, spread, spread, rows, spread, spread, spread, rows, spread, rows, spread,
            spread, spread,
        ),
        check_vma=False,
    )
```

```python
import functools
import math

import jax
import jax.numpy as jnp
from jax import lax
from jax.experimental import pallas as pl
from jax.experimental.pallas import tpu as pltpu
from jax.sharding import PartitionSpec as P

HEAD_DIM = 64
QLEN = 32
SEGS = 4
PACKET = 24
EPS = 1e-05
BF = jnp.bfloat16
F32 = jnp.float32
TILE = 32

COSTS = {"proj": 3 * 10**9, "cls": 3 * 10**9, "attention": 8 * 10**9, "first": 2 * 10**9, "inner": 6 * 10**9, "second": 4 * 10**9, "first_back": 3 * 10**10, "attention_back_4": 3 * 10**10, "input_back": 3 * 10**10}

VM = pl.BlockSpec(memory_space=pltpu.VMEM)
SM = pl.BlockSpec(memory_space=pltpu.SMEM)
HB = pl.BlockSpec(memory_space=pltpu.HBM)


def nn(a, b):
    return lax.dot_general(a, b, (((1,), (0,)), ((), ())), preferred_element_type=F32)


def nt(a, b):
    return lax.dot_general(a, b, (((1,), (1,)), ((), ())), preferred_element_type=F32)


def tn(a, b):
    return lax.dot_general(a, b, (((0,), (0,)), ((), ())), preferred_element_type=F32)


def kernel_call(body, outs, args, scratch=(), smem=0, hbm=0, mib=32, flops=0, name=None):
    single = not isinstance(outs, (list, tuple))
    shapes = [outs] if single else list(outs)
    result = pl.pallas_call(
        body,
        out_shape=shapes,
        in_specs=[SM] * smem + [VM] * (len(args) - smem - hbm) + [HB] * hbm,
        out_specs=[VM] * len(shapes),
        scratch_shapes=list(scratch),
        compiler_params=pltpu.CompilerParams(vmem_limit_bytes=mib << 20),
        cost_estimate=pl.CostEstimate(flops=COSTS.get(name, 0), bytes_accessed=0, transcendentals=0),
        name=name,
    )(*args)
    return result[0] if single else result


def sds(shape, dtype):
    return jax.ShapeDtypeStruct(shape, dtype)


def fold(value):
    rows, cols = value.shape
    return jnp.sum(value.reshape(rows // 8, 8, cols), 0)


def head_mask(half):
    lane = lax.broadcasted_iota(jnp.int32, (1, 2 * HEAD_DIM), 1)
    return (lane // HEAD_DIM == half).astype(F32).astype(BF)


def normalise(value):
    centred = value - jnp.mean(value, -1, keepdims=True)
    inverse = lax.rsqrt(jnp.mean(centred * centred, -1, keepdims=True) + EPS)
    return centred * inverse, inverse


def norm_back(grad, normed, inverse, gain):
    scaled = grad * gain
    return inverse * (
        scaled
        - jnp.mean(scaled, -1, keepdims=True)
        - normed * jnp.mean(scaled * normed, -1, keepdims=True)
    )


def gelu_pair(value):
    cdf = 0.5 * lax.erf(value * (1.0 / math.sqrt(2.0))) + 0.5
    density = jnp.exp(value * value * -0.5) * (1.0 / math.sqrt(2.0 * math.pi))
    return value * cdf, cdf + value * density


def proj_kernel(x_hbm, w_hbm, bq_hbm, bv_hbm, out, x, w0, w1, w2, bq, bv, sems):
    width = x.shape[1]
    parts = (w0, w1, w2)
    copies = [
        pltpu.make_async_copy(w_hbm.at[:, pl.ds(k * width, width)], parts[k], sems.at[k]) for k in range(3)
    ]
    x_copy = pltpu.make_async_copy(x_hbm, x, sems.at[3])
    bq_copy = pltpu.make_async_copy(bq_hbm, bq, sems.at[4])
    bv_copy = pltpu.make_async_copy(bv_hbm, bv, sems.at[5])
    for copy in (x_copy, copies[1], copies[0], bq_copy, copies[2], bv_copy):
        copy.start()
    x_copy.wait()
    for k in (1, 0, 2):
        copies[k].wait()
        value = nn(x[...], parts[k][...])
        if k == 0:
            bq_copy.wait()
            value = value + bq[...]
        if k == 2:
            bv_copy.wait()
            value = value + bv[...]
        out[:, k * width : (k + 1) * width] = value.astype(BF)


def chosen_rows(tower, seg, count, length):
    row = lax.broadcasted_iota(jnp.int32, (count, 1), 0)
    place = lax.broadcasted_iota(jnp.int32, (count, length), 1)
    start = jnp.sum((seg < row).astype(F32), 1, keepdims=True).astype(jnp.int32)
    wanted = jnp.where(tower == 0, row * QLEN, jnp.where(row < SEGS, start, -1))
    return (place == wanted).astype(F32)


def cls_kernel(place, seg, x, proj, w_out, w_in, w_back, *refs):
    vectors, (cls, *held, sems) = refs[:7], refs[7:]
    copies = [pltpu.make_async_copy(a, b, sems.at[k]) for k, (a, b) in enumerate(zip(vectors, held))]
    for copy in copies:
        copy.start()
    b_out, g1, b1, b_in, b_back, g2, b2 = held
    length, width = x.shape
    count = cls.shape[0]
    heads = width // HEAD_DIM
    tower = place[0]
    pick = chosen_rows(tower, seg[...], count, length)
    pick_low = pick.astype(BF)
    x_cls = nn(pick_low, x[...])
    q_cls = (nn(pick_low, proj[:, :width]) * (1.0 / math.sqrt(HEAD_DIM))).astype(BF)
    place_row = lax.broadcasted_iota(jnp.int32, (1, length), 1)
    own_seg = jnp.where(tower == 0, place_row // QLEN, seg[...])
    row = lax.broadcasted_iota(jnp.int32, (count, 1), 0)
    bias = jnp.where(own_seg == row, 0.0, -1e9)
    lane_head = lax.broadcasted_iota(jnp.int32, (1, width), 1) // HEAD_DIM
    spread = jnp.concatenate(
        [q_cls * (lane_head == h).astype(F32).astype(BF) for h in range(heads)], 0
    )
    scores = nt(spread, proj[:, width : 2 * width]) + jnp.concatenate([bias] * heads, 0)
    shifted = jnp.exp(scores - jnp.max(scores, -1, keepdims=True))
    probs = (shifted / jnp.sum(shifted, -1, keepdims=True)).astype(BF)
    mixed = nn(probs, proj[:, 2 * width :])
    attended = jnp.zeros((count, width), F32)
    for h in range(heads):
        attended = attended + jnp.where(lane_head == h, mixed[h * count : (h + 1) * count], 0.0)
    for copy in copies:
        copy.wait()
    first = x_cls + (nn(attended.astype(BF), w_out[...]) + b_out[...])
    normed = normalise(first)[0] * g1[...] + b1[...]
    inner = nn(normed.astype(BF), w_in[...]) + b_in[...]
    act = gelu_pair(inner)[0].astype(BF)
    second = normed + (nn(act, w_back[...]) + b_back[...])
    final = normalise(second)[0] * g2[...] + b2[...]
    cls[...] = final.astype(BF)


def attention_kernel(place, seg_row, seg_col, proj, attended, probs, bias, *work):
    length = proj.shape[0]
    width = proj.shape[1] // 3
    tower = place[0]
    lane = lax.broadcasted_iota(jnp.int32, (1, length), 1)
    sub = lax.broadcasted_iota(jnp.int32, (length, 1), 0)
    row_seg = jnp.where(tower == 0, lane // QLEN, seg_row[...])
    col_seg = jnp.where(tower == 0, sub // QLEN, seg_col[...])
    bias[...] = jnp.where(col_seg == row_seg, 0.0, -1e9)
    masks = [head_mask(0), head_mask(1)]
    scale = jnp.asarray(1.0 / math.sqrt(HEAD_DIM), BF)
    step = 2 * HEAD_DIM
    pairs = width // step
    work_a, work_b = work

    def columns(part, pair):
        return proj[:, pl.ds(pl.multiple_of(part * width + pair * step, step), step)]

    def scores(pair, ref):
        queries, keys = columns(0, pair) * scale, columns(1, pair)
        for half in range(2):
            ref[half] = nt(queries * masks[half], keys)

    def soften(pair, ref):
        for half in range(2):
            for r in range(0, length, TILE):
                value = ref[half, r : r + TILE, :] + bias[r : r + TILE, :]
                shifted = jnp.exp(value - jnp.max(value, -1, keepdims=True))
                total = jnp.sum(shifted, -1, keepdims=True)
                probs[2 * pair + half, r : r + TILE, :] = (shifted * (1.0 / total)).astype(BF)

    def mix(pair):
        values = columns(2, pair)
        mixed = nn(probs[2 * pair], values * masks[0]) + nn(probs[2 * pair + 1], values * masks[1])
        attended[:, pl.ds(pl.multiple_of(pair * step, step), step)] = mixed.astype(BF)

    def two_pairs(k, carry):
        pair = 2 * k
        scores(pair + 1, work_b)
        soften(pair, work_a)
        scores(jnp.minimum(pair + 2, pairs - 1), work_a)
        mix(pair)
        soften(pair + 1, work_b)
        mix(pair + 1)
        return carry

    scores(0, work_a)
    lax.fori_loop(0, pairs // 2, two_pairs, 0)


def first_kernel(x, attended, w_out, b_out, g1, b1, n1, r1, low, work):
    work[...] = nn(attended[...], w_out[...])
    def step(i, carry):
        rows = pl.ds(pl.multiple_of(i * TILE, TILE), TILE)
        first = x[rows, :].astype(F32) + (work[rows, :] + b_out[...])
        normed, inverse = normalise(first)
        n1[rows, :] = normed
        r1[rows, :] = inverse
        low[rows, :] = (normed * g1[...] + b1[...]).astype(BF)
        return carry

    lax.fori_loop(0, x.shape[0] // TILE, step, 0, unroll=4)


def inner_kernel(low, w_in, b_in, act, slope, work_a, work_b):
    length = low.shape[0]
    block = work_a.shape[1]
    blocks = w_in.shape[1] // block

    def columns(i):
        return pl.ds(pl.multiple_of(i * block, block), block)

    def gelu_block(i, work):
        bias = b_in[:, columns(i)]
        for r in range(0, length, TILE):
            value, grad = gelu_pair(work[r : r + TILE, :] + bias)
            act[r : r + TILE, columns(i)] = value.astype(BF)
            slope[r : r + TILE, columns(i)] = grad.astype(BF)

    work_a[...] = nn(low[...], w_in[:, :block])

    def step(k, carry):
        i = 2 * k
        work_b[...] = nn(low[...], w_in[:, columns(i + 1)])
        gelu_block(i, work_a)
        work_a[...] = nn(low[...], w_in[:, columns(jnp.minimum(i + 2, blocks - 1))])
        gelu_block(i + 1, work_b)
        return carry

    lax.fori_loop(0, blocks // 2, step, 0)


def second_kernel(act, w_back, b_back, n1, g1, b1, g2, b2, n2, r2, out, work):
    part = work.shape[0]

    def normalise_part(k, carry):
        at = pl.multiple_of(k * part, part)
        work[...] = nn(act[pl.ds(at, part), :], w_back[...])
        for r in range(0, part, TILE):
            rows = pl.ds(pl.multiple_of(at + r, TILE), TILE)
            branch = work[r : r + TILE, :] + b_back[...]
            second = (n1[rows, :] * g1[...] + b1[...]) + branch
            normed, inverse = normalise(second)
            n2[rows, :] = normed
            r2[rows, :] = inverse
            out[rows, :] = (normed * g2[...] + b2[...]).astype(BF)
        return carry

    lax.fori_loop(0, act.shape[0] // part, normalise_part, 0)


def packet_kernel(place, cls, other, labels, out):
    query = place[0] == 0
    count, width = cls.shape
    mine, came = cls[...].astype(F32), other[...].astype(F32)
    q_rows = jnp.where(query, mine, came)
    p_rows = jnp.where(query, came, mine)[:SEGS]
    value = labels[...]
    gap = jnp.zeros((1, 128 - count), F32)
    row = jnp.concatenate(
        [(value >> 8).astype(F32), gap, (value & 255).astype(F32), gap, jnp.zeros((1, width - 256), F32)], 1
    )
    rest = jnp.zeros((PACKET - count - SEGS - 1, width), F32)
    out[...] = jnp.concatenate([q_rows, p_rows, row, rest], 0).astype(BF)


def times_low(value, low):
    rows = value.shape[0]
    parts = nn(split_three(value), low)
    return parts[:rows] + parts[rows : 2 * rows] + parts[2 * rows :]


def loss_kernel(place, near, far, grad, *, order, count):
    tower, me = place[0], place[1]
    packets = jnp.concatenate([near[...], far[...]], 0)
    total, width = packets.shape
    scale = 2.0 / math.sqrt(width)
    row = lax.broadcasted_iota(jnp.int32, (total, 1), 0)
    col = lax.broadcasted_iota(jnp.int32, (1, total), 1)
    col_slot, col_part = col // PACKET, col % PACKET
    mixed = jnp.zeros_like(col)
    for j, b in enumerate(order):
        mixed = mixed | (((col_slot >> j) & 1) << b)
    is_passage = jnp.logical_and(col_part >= count, col_part < count + SEGS)
    number = jnp.where(is_passage, (mixed ^ me) * SEGS + (col_part - count), -1)
    label_of = ((row // PACKET) * PACKET + (count + SEGS) == col).astype(F32).astype(BF)
    label_rows = nn(label_of, packets[:, :256])
    lane = lax.broadcasted_iota(jnp.int32, (1, 256), 1)
    part = row % PACKET
    weight = jnp.where(lane == part, 256.0, 0.0) + jnp.where(lane == part + 128, 1.0, 0.0)
    label = jnp.sum(label_rows * weight, 1, keepdims=True).astype(jnp.int32)
    logits = jnp.where(is_passage, nt(packets, packets) * scale, -1e30)
    soft = jnp.exp(logits - jnp.max(logits, -1, keepdims=True))
    soft = soft / jnp.sum(soft, -1, keepdims=True)
    grad_logits = soft - (number == label).astype(F32)
    grad_logits = grad_logits * (part < count).astype(F32)
    grad_q = times_low(grad_logits[:count], packets)
    pick = lax.broadcasted_iota(jnp.int32, (count, 1), 0)
    pick = jnp.logical_and(pick + count == col, pick < SEGS).astype(F32).astype(BF)
    turned = nt(pick, split_three(grad_logits))
    turned = turned[:, :total] + turned[:, total : 2 * total] + turned[:, 2 * total :]
    grad_p = times_low(turned, packets)
    grad[...] = jnp.where(tower == 0, grad_q, grad_p) * scale


def plain_loss(packets, tower, me, count):
    devices, _, width = packets.shape
    scale = 2.0 / math.sqrt(width)
    queries = packets[:, :count].reshape(devices * count, width)
    passages = packets[:, count : count + SEGS].reshape(devices * SEGS, width)
    row = packets[:, count + SEGS].astype(jnp.int32)
    label = (row[:, :count] * 256 + row[:, 128 : 128 + count]).reshape(devices * count, 1)
    soft = jax.nn.softmax(nt(queries, passages) * scale, -1)
    grad = soft - (label == jnp.arange(devices * SEGS, dtype=jnp.int32)).astype(F32)
    grad_q = lax.dynamic_slice_in_dim(grad, me * count, count, 0)
    grad_q = jnp.dot(grad_q, passages.astype(F32), precision=lax.Precision.HIGHEST)
    grad_p = lax.dynamic_slice_in_dim(grad, me * SEGS, SEGS, 1)
    grad_p = jnp.dot(grad_p.T, queries.astype(F32), precision=lax.Precision.HIGHEST)
    grad_p = jnp.pad(grad_p, ((0, count - SEGS), (0, 0)))
    return jnp.where(tower == 0, grad_q, grad_p) * scale


def split_three(value):
    high = value.astype(BF)
    rest = value - high.astype(F32)
    middle = rest.astype(BF)
    return jnp.concatenate([high, middle, (rest - middle.astype(F32)).astype(BF)], 0)


def norm_back_rows(rows, grad, normed, inverse, gain, out, low, totals):
    back = norm_back(grad, normed[rows, :], inverse[rows, :], gain[...])
    out[rows, :] = back
    back_low = back.astype(BF)
    low[rows, :] = back_low
    parts = (fold(grad * normed[rows, :]), fold(grad), fold(back_low.astype(F32)))
    return parts if totals is None else tuple(a + b for a, b in zip(totals, parts))


def second_back_kernel(place, seg, out_grad, cls_grad, n2, r2, g2, grad, low, sums, work):
    length, width = out_grad.shape
    count = cls_grad.shape[0]
    pick = chosen_rows(place[0], seg[...], count, length).astype(BF)
    work[...] = tn(jnp.concatenate([pick] * 3, 0), split_three(cls_grad[...]))
    totals = None
    for r in range(0, length, TILE):
        rows = slice(r, r + TILE)
        final = out_grad[rows, :].astype(F32) + work[rows, :]
        totals = norm_back_rows(rows, final, n2, r2, g2, grad, low, totals)
    for k, part in enumerate(totals):
        sums[k : k + 1, :] = jnp.sum(part, 0, keepdims=True)


def inner_back_kernel(low, w_back, slope, out, sums):
    block = 256

    def step(i, carry):
        cols = pl.ds(pl.multiple_of(i * block, block), block)
        value = (nt(low[...], w_back[cols, :]) * slope[:, cols].astype(F32)).astype(BF)
        out[:, cols] = value
        sums[:, cols] = jnp.sum(value.astype(F32), 0, keepdims=True)
        return carry

    lax.fori_loop(0, w_back.shape[0] // block, step, 0, unroll=4)


def first_back_kernel(inner, w_in, grad_second, n1, r1, g1, w_out, grad, low, att, sums, work_a, work_b):
    length, width = grad_second.shape
    part = length // 2
    works = (work_a, work_b)
    for k in range(2):
        works[k][...] = nt(inner[k * part : (k + 1) * part, :], w_in[...])
    totals = None
    for k in range(2):
        for r in range(0, part, TILE):
            rows = slice(k * part + r, k * part + r + TILE)
            value = grad_second[rows, :] + works[k][r : r + TILE, :]
            totals = norm_back_rows(rows, value, n1, r1, g1, grad, low, totals)
        rows = slice(k * part, (k + 1) * part)
        att[rows, :] = nt(low[rows, :], w_out[...]).astype(BF)
    for k, total in enumerate(totals):
        sums[k : k + 1, :] = jnp.sum(total, 0, keepdims=True)


def attention_back_kernel(proj, probs, att_grad, out, sums, dp_a, dp_b, ds_a, ds_b, *, first):
    length = proj.shape[0]
    width = proj.shape[1] // 3
    own = out.shape[1] // 3
    masks = [head_mask(0), head_mask(1)]
    scale = 1.0 / math.sqrt(HEAD_DIM)
    step = 2 * HEAD_DIM
    pairs = own // step

    def columns(part, pair):
        return proj[:, pl.ds(pl.multiple_of(part * width + (first + pair) * step, step), step)]

    def grad_columns(pair):
        return att_grad[:, pl.ds(pl.multiple_of((first + pair) * step, step), step)]

    def grad_probs(pair, dp):
        grads, values = grad_columns(pair), columns(2, pair)
        for half in range(2):
            dp[half] = nt(grads * masks[half], values)

    def grad_scores(pair, dp, ds):
        for half in range(2):
            for r in range(0, length, TILE):
                wide = probs[2 * (first + pair) + half, r : r + TILE, :].astype(F32)
                grad = dp[half, r : r + TILE, :]
                delta = jnp.sum(grad * wide, -1, keepdims=True)
                ds[half, r : r + TILE, :] = (wide * (grad - delta)).astype(BF)

    def results(pair, ds):
        queries_t, grads_t = columns(0, pair).T, grad_columns(pair).T
        keys = columns(1, pair)
        grad_q, grad_k_t, grad_v_t = None, [], []
        for half in range(2):
            scores = ds[half]
            lanes = slice(half * HEAD_DIM, (half + 1) * HEAD_DIM)
            grad_v_t.append(nn(grads_t[lanes], probs[2 * (first + pair) + half]))
            grad_k_t.append(nn(queries_t[lanes], scores))
            term = nn(scores, keys * masks[half])
            grad_q = term if grad_q is None else grad_q + term
        parts = (
            grad_q * scale,
            jnp.concatenate(grad_k_t, 0).T * scale,
            jnp.concatenate(grad_v_t, 0).T,
        )
        for k, part in enumerate(parts):
            cols = pl.ds(pl.multiple_of(k * own + pair * step, step), step)
            part_low = part.astype(BF)
            out[:, cols] = part_low
            sums[:, cols] = jnp.sum(part_low.astype(F32), 0, keepdims=True)

    def two_pairs(k, carry):
        pair = 2 * k
        grad_probs(pair + 1, dp_b)
        grad_scores(pair, dp_a, ds_a)
        grad_probs(jnp.minimum(pair + 2, pairs - 1), dp_a)
        results(pair, ds_a)
        grad_scores(pair + 1, dp_b, ds_b)
        results(pair + 1, ds_b)
        return carry

    grad_probs(0, dp_a)
    lax.fori_loop(0, pairs // 2, two_pairs, 0)


def input_back_kernel(left, right, w_qkv, grad_first, out, work):
    width = out.shape[1]
    for k in range(3):
        at = k * width
        for part in (left, right):
            own = part.shape[1] // 3
            work[:, at : at + own] = part[:, k * own : (k + 1) * own]
            at += own
    block = 256
    for i in range(width // block):
        cols = slice(i * block, (i + 1) * block)
        value = grad_first[:, cols] + nt(work[...], w_qkv[cols, :])
        out[:, cols] = value.astype(BF)


def slot_device(me, order, slot):
    mixed = 0
    for j, b in enumerate(order):
        mixed = mixed | (((slot >> (len(order) - 1 - j)) & 1) << b)
    return me ^ mixed


def spread_shares(place, work, outs, order):
    me = place[1]
    if len(outs) == 1:
        outs = (outs[0].at[0], outs[0].at[1])
        me = me & ~(1 << order[0])
    keep, *sends = outs
    half, share, _ = keep.shape
    for slot in range(2 * half):
        ref, at = (keep, slot) if slot < half else piece_of(sends, slot - half)
        device = slot_device(me, order, slot)
        ref[at] = work[pl.ds(pl.multiple_of(device * share, 16), share), :]


def piece_of(refs, slot):
    size = refs[0].shape[0]
    return refs[slot // size], slot % size


def weight_grad_kernel(place, *refs, order, pairs):
    *outs, work = refs[2 * pairs :]
    block = 768

    def run(i):
        return pl.ds(pl.multiple_of(i * block, block), block)

    at = 0
    for left, right in zip(refs[: 2 * pairs : 2], refs[1 : 2 * pairs : 2]):
        rows, cols = left.shape[1], right.shape[1]

        def by_rows(i, carry, left=left, right=right, at=at, cols=cols):
            work[run(i), at : at + cols] = tn(left[:, run(i)], right[...]).astype(BF)
            return carry

        def by_columns(i, carry, left=left, right=right, at=at):
            there = pl.ds(pl.multiple_of(at + i * block, 128), block)
            work[:, there] = tn(left[...], right[:, run(i)]).astype(BF)
            return carry

        if rows > block:
            lax.fori_loop(0, rows // block, by_rows, 0)
        else:
            lax.fori_loop(0, cols // block, by_columns, 0)
        at += cols
    spread_shares(place, work, outs, order)


def last_grad_kernel(
    place, x, grad_proj, sums_two, sums_one, sums_left, sums_right, sums_in, *refs, order
):
    *outs, work = refs
    width = x.shape[1]
    share = outs[0].shape[1]
    devices = 2 * outs[0].shape[0]
    wide = grad_proj.shape[1]
    work[:, :wide] = tn(x[...], grad_proj[...]).astype(BF)
    extra = slice(wide, wide + 128)
    thirds = [sums.shape[1] // 3 for sums in (sums_left, sums_right)]
    query, value = (
        jnp.concatenate(
            [sums[:, k * own : (k + 1) * own] for sums, own in zip((sums_left, sums_right), thirds)], 1
        )
        for k in (0, 2)
    )
    stacked = jnp.concatenate([query, value, sums_two[0:3], sums_one[0:3]], 0)
    work[:, extra] = jnp.zeros((width, 128), BF)
    in_share = sums_in.shape[1] // devices
    for d in range(devices):
        rows = [stacked[:, d * share : (d + 1) * share]]
        for k in range(in_share // share):
            at = d * in_share + k * share
            rows.append(sums_in[:, at : at + share])
        rows.append(jnp.zeros((16 - 8 - in_share // share, share), F32))
        block = jnp.concatenate(rows, 0)
        block = jnp.concatenate([block, jnp.zeros((16, 128 - share), F32)], 1)
        high = block.astype(BF)
        work[d * share : d * share + 16, extra] = high
        work[d * share + 16 : d * share + 32, extra] = (block - high.astype(F32)).astype(BF)
    spread_shares(place, work, outs, order)


def add_extra(left, right):
    total = (
        left[0:16].astype(F32) + left[16:32].astype(F32) + right[0:16].astype(F32) + right[16:32].astype(F32)
    )
    return total


def halve_kernel(*refs, cames, extra):
    kept, came, (keep, *sends) = refs[0], refs[1 : 1 + cames], refs[1 + cames :]
    half = keep.shape[0]
    cols = keep.shape[2] - extra
    for slot in range(2 * half):
        ref, at = (keep, slot) if slot < half else piece_of(sends, slot - half)
        other, there = piece_of(came, slot)
        ref[at, :, :cols] = (kept[slot, :, :cols].astype(F32) + other[there, :, :cols].astype(F32)).astype(BF)
        if extra:
            total = add_extra(kept[slot, :, cols:], other[there, :, cols:])
            high = total.astype(BF)
            ref[at, 0:16, cols:] = high
            ref[at, 16:32, cols:] = (total - high.astype(F32)).astype(BF)
            ref[at, 32:, cols:] = jnp.zeros((keep.shape[1] - 32, extra), BF)


def halve_cores_kernel(both, *outs, extra):
    halve_kernel(both.at[0], both.at[1], *outs, cames=1, extra=extra)


def finish_kernel(kept, came, out):
    out[...] = kept[0].astype(F32) + came[0].astype(F32)


def finish_last_kernel(
    kept, came, kept_last, came_last, w_qkv, w_out, bq, bv, gain2, bias2, b_back, gain1, bias1, b_out, b_in
):
    width = w_out.shape[1]
    share = bq.shape[1]
    left, right = (kept.shape[2] - width) // 3, (kept_last.shape[2] - 128) // 3
    for k in range(3):
        at = k * width
        cols = slice(k * left, (k + 1) * left)
        w_qkv[:, at : at + left] = kept[0, :, cols].astype(F32) + came[0, :, cols].astype(F32)
        cols = slice(k * right, (k + 1) * right)
        w_qkv[:, at + left : at + width] = kept_last[0, :, cols].astype(F32) + came_last[0, :, cols].astype(F32)
    w_out[...] = kept[0, :, 3 * left :].astype(F32) + came[0, :, 3 * left :].astype(F32)
    vectors = add_extra(kept_last[0, :, 3 * right :], came_last[0, :, 3 * right :])
    for k, ref in enumerate((bq, bv, gain2, bias2, b_back, gain1, bias1, b_out)):
        ref[...] = vectors[k : k + 1, :share]
    pieces = b_in.shape[1] // share
    b_in[...] = jnp.concatenate([vectors[8 + k : 9 + k, :share] for k in range(pieces)], 1)


def plain_grad_kernel(left, right, out):
    out[...] = tn(left[...], right[...])


def swapped(value, axis, mask):
    count = lax.axis_size(axis)
    return lax.ppermute(value, axis, [(i, i ^ mask) for i in range(count)])


class Sequence:
    def __init__(self):
        self.last = None

    def now(self, value):
        return value if self.last is None else after(value, self.last)

    def ran(self, results):
        self.last = results[0]
        return results

    def chunk(self, outs, extra=0, pieces=1):
        chunk = {"extra": extra}
        if len(outs) > 1:
            chunk["keep"], *chunk["sends"] = self.ran(outs)
        else:
            pairs = [[i, i + 1] for i in range(0, lax.axis_size("dp"), 2)]
            both = lax.all_to_all(outs[0], "dp", 0, 0, tiled=True, axis_index_groups=pairs)
            self.last = both
            self.parted(chunk, functools.partial(halve_cores_kernel, extra=extra), [both], both.shape[1:], pieces)
        return chunk

    def parted(self, chunk, body, args, shape, pieces):
        half = sds((shape[0] // 2,) + shape[1:], BF)
        piece = sds((shape[0] // 2 // pieces,) + shape[1:], BF)
        chunk["keep"], *chunk["sends"] = self.ran(
            kernel_call(body, [half] + [piece] * pieces, args, mib=4, name="halve")
        )

    def go(self, chunk, bit, behind=None):
        sends = [self.now(send) for send in chunk["sends"]]
        if behind is not None:
            sends = [after(send, *behind["came"]) for send in sends]
        chunk["came"] = [swapped(send, "dp", 1 << bit) for send in sends]

    def take(self, chunk, pieces=1):
        keep, came = chunk["keep"], [self.now(value) for value in chunk["came"]]
        body = functools.partial(halve_kernel, cames=len(came), extra=chunk["extra"])
        self.parted(chunk, body, [keep] + came, keep.shape, pieces)

    def finish(self, chunk):
        args = [chunk["keep"], self.now(chunk["came"][0])]
        return self.ran([kernel_call(finish_kernel, sds(args[0].shape[1:], F32), args, mib=4, name="finish")])[0]


def after(value, *earlier):
    return lax.optimization_barrier((value,) + earlier)[0]


def shards(
    hidden_in,
    seg_ids,
    labels,
    out_grad,
    w_qkv,
    b_query,
    b_value,
    w_out,
    b_out,
    ln1_gain,
    ln1_bias,
    w_in,
    b_in,
    w_back,
    b_back,
    ln2_gain,
    ln2_bias,
):
    x, cotangent = hidden_in[0], out_grad[0]
    w_qkv, w_out, w_in, w_back = w_qkv[0], w_out[0], w_in[0], w_back[0]
    length, width = x.shape
    hidden = w_in.shape[1]
    heads = width // HEAD_DIM
    count = length // QLEN
    devices = lax.axis_size("dp")
    bits = devices.bit_length() - 1
    tower, me = lax.axis_index("tower"), lax.axis_index("dp")
    place = jnp.stack([tower, me]).astype(jnp.int32)
    seg_col = seg_ids.reshape(length, 1)
    fast = devices == 16

    proj = kernel_call(
        proj_kernel, sds((length, 3 * width), BF),
        [pltpu.with_memory_space_constraint(member, pltpu.HBM) for member in (x, w_qkv, b_query, b_value)], hbm=4,
        scratch=[pltpu.VMEM((length, width), BF)] + [pltpu.VMEM((width, width), BF)] * 3
        + [pltpu.VMEM((1, width), F32)] * 2 + [pltpu.SemaphoreType.DMA((6,))],
        mib=8, flops=2 * length * 3 * width * width, name="proj",
    )
    cls = kernel_call(
        cls_kernel, sds((count, width), BF),
        [place, seg_ids, x, proj, w_out, w_in, w_back] + [
            pltpu.with_memory_space_constraint(member, pltpu.HBM)
            for member in (b_out, ln1_gain, ln1_bias, b_in, b_back, ln2_gain, ln2_bias)
        ],
        hbm=7,
        scratch=[pltpu.VMEM((1, width), F32)] * 3 + [pltpu.VMEM((1, hidden), F32)]
        + [pltpu.VMEM((1, width), F32)] * 3 + [pltpu.SemaphoreType.DMA((7,))],
        smem=1, mib=3, flops=2 * 256 * width * hidden * 2, name="cls",
    )
    other = swapped(cls, "tower", 1)
    attended, probs = kernel_call(
        attention_kernel, [sds((length, width), BF), sds((heads, length, length), BF)],
        [place, seg_ids, seg_col, after(proj, cls)], smem=1,
        scratch=[pltpu.VMEM((length, length), F32)] + [pltpu.VMEM((2, length, length), F32)] * 2,
        mib=9, flops=4 * heads * length * length * 256, name="attention",
    )
    held = kernel_call(
        packet_kernel, sds((PACKET, width), BF), [place, cls, after(other, attended), labels[None]],
        smem=1, mib=1, name="packet",
    )
    order = [3, 2, 1, 0] if fast else list(range(bits))
    if fast:
        came = swapped(held, "dp", 1 << order[0])
    work, half_work = pltpu.VMEM((length, width), F32), pltpu.VMEM((length // 2, width), F32)
    n1, r1, first_low = kernel_call(
        first_kernel,
        [sds((length, width), F32), sds((length, 1), F32), sds((length, width), BF)],
        [x, after(attended, held), w_out, b_out, ln1_gain, ln1_bias], scratch=[work],
        mib=4, flops=2 * length * width * width, name="first",
    )
    if fast:
        held = jnp.concatenate([held, after(came, first_low)], 0)
        came = swapped(held, "dp", 1 << order[1])
    act, slope = kernel_call(
        inner_kernel, [sds((length, hidden), BF), sds((length, hidden), BF)],
        [after(first_low, held), w_in, b_in], scratch=[pltpu.VMEM((length, 256), F32)] * 2,
        mib=4, flops=8 * length * width * hidden, name="inner",
    )
    if fast:
        held = jnp.concatenate([held, after(came, act)], 0)
        came = swapped(held, "dp", 1 << order[2])
    n2, r2, out_hidden = kernel_call(
        second_kernel,
        [sds((length, width), F32), sds((length, 1), F32), sds((length, width), BF)],
        [after(act, held), w_back, b_back, n1, ln1_gain, ln1_bias, ln2_gain, ln2_bias], scratch=[half_work],
        mib=5, flops=2 * length * width * hidden, name="second",
    )
    if fast:
        near = jnp.concatenate([held, after(came, out_hidden)], 0)
        far = swapped(near, "dp", 1 << order[3])
        cls_grad = kernel_call(
            functools.partial(loss_kernel, order=order, count=count), sds((count, width), F32),
            [place, near, far], smem=1,
            mib=5, flops=8 * devices * count * devices * SEGS * width, name="loss",
        )
    else:
        packets = lax.all_gather(held, "dp", axis=0)
        cls_grad = plain_loss(packets, tower, me, count)

    grad_second, second_low, sums_two = kernel_call(
        second_back_kernel,
        [sds((length, width), F32), sds((length, width), BF), sds((8, width), F32)],
        [place, seg_ids, cotangent, cls_grad, n2, r2, ln2_gain], smem=1, scratch=[work],
        mib=4, flops=2 * length * width * 256, name="second_back",
    )

    def plain_grad(left, right, name):
        rows, cols = left.shape[1], right.shape[1]
        whole = kernel_call(
            plain_grad_kernel, sds((rows, cols), F32), [left, right], mib=24,
            flops=2 * length * rows * cols, name=name,
        )
        return lax.psum_scatter(whole, "dp", scatter_dimension=0, tiled=True)

    inner_call = dict(mib=3, flops=2 * length * width * hidden, name="inner_back")
    inner_shape = [sds((length, hidden), BF), sds((1, hidden), F32)]
    first_call = dict(
        scratch=[half_work] * 2, mib=5, flops=2 * length * width * (hidden + width), name="first_back"
    )
    first_shape = [
        sds((length, width), F32), sds((length, width), BF), sds((length, width), BF), sds((8, width), F32)
    ]
    def attention_back(gradient, first, pairs):
        step = (length, length)
        return kernel_call(
            functools.partial(attention_back_kernel, first=first),
            [sds((length, 6 * HEAD_DIM * pairs), BF), sds((1, 6 * HEAD_DIM * pairs), F32)],
            [proj, probs, gradient],
            scratch=[pltpu.VMEM((2,) + step, F32)] * 2 + [pltpu.VMEM((2,) + step, BF)] * 2,
            mib=9, flops=16 * pairs * length * length * 256, name=f"attention_back_{first}",
        )

    head_pairs = heads // 2
    split = 2 * head_pairs // 3

    def input_back(left, right):
        return kernel_call(
            input_back_kernel, sds((length, width), BF), [left, right, w_qkv, grad_first],
            scratch=[pltpu.VMEM((length, 3 * width), BF)],
            mib=5, flops=6 * length * width * width, name="input_back",
        )

    if fast:
        share = width // devices
        line = Sequence()

        CORE, X, Z1, Z2 = range(4)

        def grads(*pairs, name, order=(CORE, X, Z1, Z2), pieces=1, at_once=False):
            rows = pairs[0][0].shape[1]
            shape = (devices // 2, rows // devices, sum(right.shape[1] for _, right in pairs))
            args = [member for left, right in pairs for member in (left, line.now(right))]
            outs = kernel_call(
                functools.partial(weight_grad_kernel, order=order, pairs=len(pairs)),
                [sds((2,) + shape, BF)] if at_once
                else [sds(shape, BF)] + [sds((shape[0] // pieces,) + shape[1:], BF)] * pieces,
                [place] + args, smem=1, scratch=[pltpu.VMEM((rows, shape[2]), BF)],
                mib=8, flops=2 * length * rows * shape[2], name=name,
            )
            return line.chunk(outs, pieces=pieces)

        a = grads((act, second_low), name="grad_w_back", order=(CORE, Z1, Z2, X))
        line.go(a, CORE)
        inner_low, sums_in = line.ran(
            kernel_call(inner_back_kernel, inner_shape, [line.now(second_low), w_back, slope], **inner_call)
        )
        line.take(a)
        line.go(a, Z1)
        b = grads((first_low, inner_low), name="grad_w_in", pieces=1)
        line.go(b, CORE)
        grad_first, branch_low, att_grad, sums_one = line.ran(
            kernel_call(
                first_back_kernel, first_shape,
                [line.now(inner_low), w_in, grad_second, n1, r1, ln1_gain, w_out], **first_call
            )
        )
        line.take(b)
        line.go(b, X)
        grad_left, sums_left = line.ran(attention_back(line.now(att_grad), 0, split))
        c = grads((x, grad_left), (attended, branch_low), name="grad_w_qkv_1", pieces=1)
        line.go(c, CORE)
        grad_right, sums_right = line.ran(attention_back(line.now(att_grad), split, head_pairs - split))
        line.take(c, pieces=2)
        line.take(a)
        line.go(a, Z2)
        cols = 6 * HEAD_DIM * (head_pairs - split) + 128
        d = line.chunk(
            kernel_call(
                functools.partial(last_grad_kernel, order=(CORE, X, Z1, Z2)),
                [sds((devices // 2, share, cols), BF)] + [sds((devices // 2 // 1, share, cols), BF)] * 1,
                [place, x, line.now(grad_right), sums_two, sums_one, sums_left, sums_right, sums_in],
                smem=1, scratch=[pltpu.VMEM((width, cols), BF)], mib=5,
                flops=2 * length * width * cols, name="grad_w_qkv_2",
            ),
            extra=128,
        )
        line.go(d, CORE)
        grad_hidden = line.ran([input_back(grad_left, line.now(grad_right))])[0]
        line.take(d)
        line.go(c, X, behind=b)
        line.take(b, pieces=2)
        line.go(b, Z1)
        line.take(a)
        line.go(d, X, behind=c)
        line.take(c, pieces=2)
        line.go(c, Z1)
        line.take(b)
        line.go(b, Z2)
        line.go(a, X, behind=d)
        line.take(d)
        line.go(d, Z1)
        line.take(c)
        line.go(c, Z2)
        share_w_in = line.finish(b)
        line.take(d)
        line.go(d, Z2)
        share_w_back = line.finish(a)
        (
            share_w_qkv, share_w_out, share_bq, share_bv, share_gain2, share_bias2, share_b_back,
            share_gain1, share_bias1, share_b_out, share_b_in,
        ) = kernel_call(
            finish_last_kernel,
            [sds((share, 3 * width), F32), sds((share, width), F32)] + [sds((1, share), F32)] * 8
            + [sds((1, hidden // devices), F32)],
            [c["keep"], line.now(c["came"][0]), d["keep"], d["came"][0]], mib=4, name="finish_last",
        )
    else:
        share_w_back = plain_grad(act, second_low, "grad_w_back")
        inner_low, sums_in = kernel_call(
            inner_back_kernel, inner_shape, [second_low, w_back, slope], **inner_call
        )
        share_w_in = plain_grad(first_low, inner_low, "grad_w_in")
        grad_first, branch_low, att_grad, sums_one = kernel_call(
            first_back_kernel, first_shape, [inner_low, w_in, grad_second, n1, r1, ln1_gain, w_out],
            **first_call
        )
        grad_left, sums_left = attention_back(att_grad, 0, split)
        grad_right, sums_right = attention_back(att_grad, split, head_pairs - split)
        grad_hidden = input_back(grad_left, grad_right)

        def joined(left, right):
            pieces = [jnp.split(half, 3, 1) for half in (left, right)]
            return jnp.concatenate([piece for both in zip(*pieces) for piece in both], 1)

        grad_proj, sums_qkv = joined(grad_left, grad_right), joined(sums_left, sums_right)
        share_w_qkv = plain_grad(x, grad_proj, "grad_w_qkv")
        share_w_out = plain_grad(attended, branch_low, "grad_w_out")

        def scattered(vector):
            return lax.psum_scatter(vector, "dp", scatter_dimension=1, tiled=True)

        share_bq, share_bv = scattered(sums_qkv[:, :width]), scattered(sums_qkv[:, 2 * width :])
        share_gain2, share_bias2, share_b_back = (scattered(sums_two[k : k + 1]) for k in range(3))
        share_gain1, share_bias1, share_b_out = (scattered(sums_one[k : k + 1]) for k in range(3))
        share_b_in = scattered(sums_in)
    return (
        out_hidden[None],
        grad_hidden[None],
        share_w_qkv[None],
        share_bq,
        share_bv,
        share_w_out[None],
        share_b_out,
        share_gain1,
        share_bias1,
        share_w_in[None],
        share_b_in,
        share_w_back[None],
        share_b_back,
        share_gain2,
        share_bias2,
    )


def solution(mesh):
    matrix, vector = P("tower", None, None), P("tower", None)
    rows, spread = P("tower", "dp", None), P("tower", "dp")
    return jax.shard_map(
        shards,
        mesh=mesh,
        in_specs=(
            rows, P("dp", None), P("dp"), rows, matrix, vector, vector, matrix, vector, vector, vector,
            matrix, vector, matrix, vector, vector, vector,
        ),
        out_specs=(
            rows, rows, rows, spread, spread, rows, spread, spread, spread, rows, spread, rows, spread,
            spread, spread,
        ),
        check_vma=False,
    )
```
